32 devices in a mesh: grp: 2 (over y), tm: 4 (over x, core), chan: 4 (over z).
Axes of the slice: x: 2, y: 2, z: 4, core: 2. Of those that a mesh axis runs over, the one named last changes fastest.
Arguments:
- records: bfloat16 [512, 3, 1024], P(('grp', 'tm', 'chan')), parts along dimension 0, may hold values from -6 to 6
- templates: bfloat16 [256, 3, 200, 256], P(('tm', 'chan')), may hold values from -6 to 6
- moveouts: int32 [256, 3], P(('tm', 'chan')), may hold values from 0 to 999
- uptime: int32 [512, 2], P(('grp', 'tm', 'chan')), parts along dimension 0, may hold values from 0 to 512
Outputs:
- cccsum: float32 [256, 2048], P(None, ('grp', 'tm', 'chan')), parts along dimension 1
The draws below stay inside these ranges and needn't reach their ends.
There are 2 independent parts, one for each index of `grp`. The reference program is written for one: setup_inputs(seed, part) draws one part's arguments, and reference() takes and returns one part's arrays. A program takes and returns all parts, laid end to end along the dimension named above; an argument that names none is the same for every part. Nothing has to cross between parts.
All inputs are finite; a program needn't handle non-finite values.
Results may differ from the reference program's by a relative error of at most 0.0041.
Values may be sent and summed in bfloat16 or wider, within the bound.
No kernel may reach another device: no remote copies, remote signals or barrier semaphores. Data moves between devices by JAX's collectives and lax.ppermute only.
A program may use at most 64 MiB of HBM per device.

```python
import jax
import jax.numpy as jnp
from jax import lax

STATIONS = 256
COMP = 3
TLEN = 200
TEMPLATES = 256
MAXMO = 1000
BLK = 512
NS = 1024
NBLK = 2


def draw_moveouts(key, part):
    first_key, second_key = jax.random.split(key)
    values = jax.random.randint(first_key, (STATIONS * COMP,), 0, MAXMO, dtype=jnp.int32)
    chosen = jax.random.permutation(second_key, STATIONS * COMP)
    values = values.at[chosen[0]].set(MAXMO - 1)
    values = values.at[chosen[1]].set(0)
    return values.reshape(STATIONS, COMP).astype(jnp.int32)


def draw_uptime(key, part):
    first_key, second_key = jax.random.split(jax.random.fold_in(key, 7))
    counts = jax.random.randint(first_key, (STATIONS * NBLK,), 0, 2 * BLK, dtype=jnp.int32)
    counts = jnp.minimum(counts, BLK)
    chosen = jax.random.permutation(second_key, STATIONS * NBLK)
    counts = counts.at[chosen[0]].set(0)
    counts = counts.at[chosen[1]].set(BLK)
    return counts.reshape(STATIONS, NBLK).astype(jnp.int32)


def block_levels(stream_key, extent, pieces, least, top_value):
    def one(dim, parts):
        draws = jax.random.uniform(jax.random.fold_in(jax.random.fold_in(stream_key, 6), dim), (parts,), jnp.float32, least / len(pieces), top_value / len(pieces))
        return jnp.repeat(jnp.exp(draws), extent[dim] // parts).reshape((-1,) + (1,) * (len(extent) - dim - 1))

    level = one(*pieces[0])
    for cut in pieces[1:]:
        level = level * one(*cut)
    return level


def gaussian(key, shape, scale, bound, pieces=(), kind=jnp.bfloat16):
    entries = scale * jax.random.normal(key, shape, jnp.float32)
    if pieces:
        entries = entries * block_levels(key, shape, pieces, -0.22, 0.18)
    return jnp.clip(entries, -bound, bound).astype(kind)


def setup_inputs(seed: int = 0, part: int = 0) -> dict:
    keys = jax.random.split(jax.random.key(seed), 5)
    part_splits = jax.random.split(jax.random.fold_in(keys[4], part), 5)
    records = gaussian(part_splits[0], (STATIONS, COMP, NS), 1.0, 6.0, ((0, 16),))
    templates = gaussian(keys[1], (STATIONS, COMP, TLEN, TEMPLATES), 1.0, 6.0, ((0, 16),))
    moveouts = draw_moveouts(jax.random.fold_in(keys[4], 71), part)
    uptime = draw_uptime(jax.random.fold_in(jax.random.fold_in(keys[4], part), 71), part)
    return dict(records=records, templates=templates, moveouts=moveouts, uptime=uptime)


def prepare_records(records, moveouts, uptime):
    stations, components, length = records.shape
    block_count = uptime.shape[1]
    offsets = lax.broadcasted_iota(jnp.int32, (block_count, length // block_count), 1)
    live_mask = (offsets[None, :, :] < uptime[:, :, None]).reshape(stations, 1, length)
    masked = jnp.where(live_mask, records, jnp.zeros((), records.dtype))
    padded = jnp.concatenate([masked, jnp.zeros((stations, components, MAXMO), records.dtype)], axis=2)
    flat_rows = padded.reshape(stations * components, length + MAXMO)
    starts = moveouts.reshape(stations * components).astype(jnp.int32)

    def slice_row(record_row, start_at):
        return lax.dynamic_slice_in_dim(record_row, start_at, length)
    shifted = jax.vmap(slice_row)(flat_rows, starts)
    return shifted.reshape(stations, components, length)

def normalize_templates(templates):
    values = templates.astype(jnp.float32)
    squares = lax.optimization_barrier(jnp.sum(values * values, axis=2, keepdims=True))
    return (values * lax.rsqrt(squares + 1e-06)).astype(jnp.bfloat16)

def correlate_station(station_rows, unit_rows):
    channels, length = station_rows.shape
    window_len = unit_rows.shape[1]
    out_len = length - window_len + 1
    tiled_rows = jnp.tile(station_rows, (1, window_len + 1))[:, :window_len * (length + 1)]
    windows = tiled_rows.reshape(channels, window_len, length + 1)[:, :, :out_len]
    energy = lax.optimization_barrier(jnp.sum(jnp.square(windows.astype(jnp.float32)), axis=1))
    factor = lax.rsqrt(jnp.maximum(energy, 1.0))
    scaled = (windows.astype(jnp.float32) * factor[:, None, :]).astype(jnp.bfloat16)
    unit_flat = unit_rows.reshape(channels * window_len, unit_rows.shape[2])
    return jnp.dot(unit_flat.T, scaled.reshape(channels * window_len, out_len), preferred_element_type=jnp.float32)

def reference(records, templates, moveouts, uptime):
    shifted = prepare_records(records, moveouts, uptime)
    unit_bank = normalize_templates(templates)
    padded = jnp.concatenate([shifted, jnp.zeros((STATIONS, COMP, TLEN - 1), shifted.dtype)], axis=2)

    def station_step(running, station_data):
        station_rows, unit_rows = station_data
        return (running + correlate_station(station_rows, unit_rows), None)
    initial = jnp.zeros((TEMPLATES, NS), jnp.float32)
    result, ignored = lax.scan(station_step, initial, (padded, unit_bank))
    return result
```

```python
import functools

import jax
import jax.numpy as jnp
from jax import lax
from jax.experimental import pallas as pl
from jax.experimental.pallas import tpu as pltpu
from jax.sharding import PartitionSpec as P

MAXMO = 1000
LANES = 128
GROUP = 16


def up(value, unit):
    return -(-value // unit) * unit


def window_sum(values, window):
    width = values.shape[1]

    def ahead(array, by):
        return array if by == 0 else pltpu.roll(array, width - by, 1)

    total, offset, size, run = None, 0, 1, values
    while size <= window:
        if window & size:
            piece = ahead(run, offset)
            total = piece if total is None else total + piece
            offset += size
        size *= 2
        if size <= window:
            run = run + ahead(run, size // 2)
    return total


def correlate_kernel(
    core_ref, moveouts_ref, uptime_ref, records_ref, templates_ref,
    send_ref, keep_ref,
    masked, shifted, factor, columns, hankel, bank, total,
    *, stations, components, length, window, block_count,
):
    station = pl.program_id(0)
    channels = stations * components
    rows = masked.shape[0]
    tiles = length // LANES
    depth_tiles = up(window, LANES) // LANES
    block_len = length // block_count
    span = shifted.shape[1]

    @pl.when(station == 0)
    def prologue():
        masked[...] = jnp.zeros(masked.shape, jnp.float32)
        offsets = lax.broadcasted_iota(jnp.int32, (components, block_len), 1)
        for s in range(stations):
            for b in range(block_count):
                part = slice(b * block_len, (b + 1) * block_len)
                values = records_ref[s, :, part].astype(jnp.float32)
                live = offsets < uptime_ref[s * block_count + b]
                masked[s * components:(s + 1) * components, part] = jnp.where(live, values, 0.0)
        shifted[...] = jnp.zeros(shifted.shape, jnp.float32)

        def shift_one(c, carry):
            moveout = moveouts_ref[c]
            base = pl.multiple_of(moveout // LANES * LANES, LANES)
            row = masked[pl.ds(c, 1), pl.ds(base, span)]
            shifted[pl.ds(c, 1), :] = pltpu.roll(row, span - (moveout - base), 1)
            return carry

        lax.fori_loop(0, channels, shift_one, 0)
        factor[...] = jnp.zeros(factor.shape, jnp.float32)
        for g in range(0, rows, 8):
            values = shifted[g:g + 8, :]
            energy = window_sum(values * values, window)[:, :length]
            factor[g:g + 8, :] = lax.rsqrt(jnp.maximum(energy, 1.0))
        source = lax.broadcasted_iota(jnp.int32, (LANES, LANES), 1)
        target = lax.broadcasted_iota(jnp.int32, (LANES, LANES), 0)
        mirrored = target // GROUP * GROUP + (GROUP - 1 - target % GROUP)
        swap = jnp.where(source == mirrored, 1.0, 0.0).astype(jnp.float32)
        for i in range(tiles):
            columns[i * LANES:(i + 1) * LANES, :] = lax.dot_general(
                swap, factor[:, i * LANES:(i + 1) * LANES],
                (((1,), (1,)), ((), ())),
                precision=lax.Precision.HIGHEST,
                preferred_element_type=jnp.float32,
            )
        bank[...] = jnp.zeros(bank.shape, bank.dtype)
        total[...] = jnp.zeros(total.shape, total.dtype)

    for j in range(components):
        values = templates_ref[0, j].astype(jnp.float32)
        squares = jnp.sum(values * values, axis=0, keepdims=True)
        unit = (values * lax.rsqrt(squares + 1e-06)).astype(jnp.bfloat16)
        bank[j * depth_tiles * LANES:j * depth_tiles * LANES + window, :] = unit

    for j in range(components):
        c = station * components + j
        half = jnp.broadcast_to(shifted[pl.ds(c, 1), :], (8, span))
        strip = jnp.concatenate(
            [pltpu.roll(half, span - GROUP + 1 + b, 1, stride=1, stride_axis=0) for b in (0, 8)],
            axis=0,
        ).astype(jnp.bfloat16)
        for a in range(LANES // GROUP):
            rolled = strip if a == 0 else pltpu.roll(strip, span - a * GROUP, 1)
            for i in range(tiles + depth_tiles - 1):
                hankel[j, i, a * GROUP:(a + 1) * GROUP, :] = rolled[:, i * LANES:(i + 1) * LANES]

    def one_tile(i, carry):
        at = pl.multiple_of(i * LANES, LANES)
        column = columns[pl.ds(at, LANES), :]
        parts = []
        for j in range(components):
            lane = jnp.full((LANES, LANES), station * components + j, jnp.int32)
            scale = jnp.take_along_axis(column, lane, axis=1).astype(jnp.bfloat16)
            for d in range(depth_tiles):
                parts.append(hankel[j, i + d] * scale)
        total[pl.ds(at, LANES), :] += jnp.dot(
            jnp.concatenate(parts, axis=1), bank[...], preferred_element_type=jnp.float32
        )
        return carry

    lax.fori_loop(0, tiles, one_tile, 0, unroll=tiles <= 8)

    @pl.when(station == stations - 1)
    def finish():
        core = core_ref[0]
        hops, region = keep_ref.shape[0], keep_ref.shape[1]
        for x in range(hops):
            own = pl.multiple_of((2 * x + core) * region, region)
            other = pl.multiple_of((2 * x + 1 - core) * region, region)
            keep_ref[x] = total[pl.ds(own, region), :]
            send_ref[x] = total[pl.ds(other, region), :].astype(send_ref.dtype)


def correlate(core, records, templates, moveouts, uptime, hops):
    stations, components, length = records.shape
    window, bank_size = templates.shape[2:]
    block_count = uptime.shape[1]
    depth = up(window, LANES)
    rows = up(stations * components, 8)
    reach = length + depth + LANES + up(MAXMO, LANES)
    region = length // (2 * hops)
    body = functools.partial(
        correlate_kernel, stations=stations, components=components, length=length,
        window=window, block_count=block_count,
    )
    whole = lambda s, *_: (0, 0, 0)
    return pl.pallas_call(
        body,
        grid_spec=pltpu.PrefetchScalarGridSpec(
            num_scalar_prefetch=3,
            grid=(stations,),
            in_specs=[
                pl.BlockSpec(records.shape, whole),
                pl.BlockSpec((1,) + templates.shape[1:], lambda s, *_: (s, 0, 0, 0)),
            ],
            out_specs=[
                pl.BlockSpec((hops, region, bank_size), whole),
                pl.BlockSpec((hops, region, bank_size), whole),
            ],
            scratch_shapes=[
                pltpu.VMEM((rows, reach), jnp.float32),
                pltpu.VMEM((rows, length + depth + LANES), jnp.float32),
                pltpu.VMEM((up(rows, LANES), length), jnp.float32),
                pltpu.VMEM((length, up(rows, LANES)), jnp.float32),
                pltpu.VMEM((components, (length + depth) // LANES - 1, LANES, LANES), jnp.bfloat16),
                pltpu.VMEM((components * depth, bank_size), jnp.bfloat16),
                pltpu.VMEM((length, bank_size), jnp.float32),
            ],
        ),
        out_shape=[
            jax.ShapeDtypeStruct((hops, region, bank_size), jnp.bfloat16),
            jax.ShapeDtypeStruct((hops, region, bank_size), jnp.float32),
        ],
        compiler_params=pltpu.CompilerParams(vmem_limit_bytes=48 * 2**20),
        name="correlate",
    )(core, moveouts.reshape(-1), uptime.reshape(-1), records, templates)


def body(records, templates, moveouts, uptime):
    tm, chan = lax.axis_size("tm"), lax.axis_size("chan")
    hops = tm // 2
    t, z = lax.axis_index("tm"), lax.axis_index("chan")
    x, core = t // 2, t % 2
    send, keep = correlate(core.reshape(1), records, templates, moveouts, uptime, hops)
    got = lax.ppermute(send, "tm", [(i, i ^ 1) for i in range(tm)])
    mine = keep + got.astype(jnp.float32)
    result = lax.dynamic_index_in_dim(mine, x, 0, keepdims=False)
    for step in range(1, hops):
        block = lax.dynamic_index_in_dim(mine, (x + step) % hops, 0, keepdims=False)
        perm = [(i, ((i // 2 + step) % hops) * 2 + i % 2) for i in range(tm)]
        result = result + lax.ppermute(block.astype(jnp.bfloat16), "tm", perm).astype(jnp.float32)
    mine = result.reshape(chan, result.shape[0] // chan, result.shape[1])
    result = lax.dynamic_index_in_dim(mine, z, 0, keepdims=False)
    for step in range(1, chan):
        block = lax.dynamic_index_in_dim(mine, (z + step) % chan, 0, keepdims=False)
        perm = [(i, (i + step) % chan) for i in range(chan)]
        result = result + lax.ppermute(block.astype(jnp.bfloat16), "chan", perm).astype(jnp.float32)
    samples, bank_size = result.shape
    result = result.reshape(samples // GROUP, GROUP, bank_size)[:, ::-1, :]
    return result.reshape(samples, bank_size).T


def solution(mesh):
    placed = (
        P(("grp", "tm", "chan"), None, None),
        P(("tm", "chan"), None, None, None),
        P(("tm", "chan"), None),
        P(("grp", "tm", "chan"), None),
    )
    return jax.shard_map(
        body, mesh=mesh, in_specs=placed, out_specs=P(None, ("grp", "tm", "chan")), check_vma=False
    )
```

```python
import functools

import jax
import jax.numpy as jnp
from jax import lax
from jax.experimental import pallas as pl
from jax.experimental.pallas import tpu as pltpu
from jax.sharding import PartitionSpec as P

MAXMO = 1000
LANES = 128
GROUP = 16


def up(value, unit):
    return -(-value // unit) * unit


def window_sum(values, window):
    width = values.shape[1]

    def ahead(array, by):
        return array if by == 0 else pltpu.roll(array, width - by, 1)

    total, offset, size, run = None, 0, 1, values
    while size <= window:
        if window & size:
            piece = ahead(run, offset)
            total = piece if total is None else total + piece
            offset += size
        size *= 2
        if size <= window:
            run = run + ahead(run, size // 2)
    return total


def correlate_kernel(
    core_ref, moveouts_ref, uptime_ref, records_ref, templates_ref,
    send_ref, keep_ref,
    masked, shifted, factor, columns, strips, windows_a, windows_b, bank_a, bank_b, total,
    *, stations, components, length, window, block_count,
):
    step = pl.program_id(0)
    channels = stations * components
    rows = masked.shape[0]
    tiles = length // LANES
    depth_tiles = up(window, LANES) // LANES
    depth = depth_tiles * LANES
    block_len = length // block_count
    span = shifted.shape[1]

    def prologue():
        masked[...] = jnp.zeros(masked.shape, jnp.float32)
        offsets = lax.broadcasted_iota(jnp.int32, (stations, block_len), 1)
        which = lax.broadcasted_iota(jnp.int32, (stations, block_len), 0)
        for b in range(block_count):
            limit = jnp.zeros((stations, block_len), jnp.int32)
            for s in range(stations):
                limit = jnp.where(which == s, uptime_ref[b, s], limit)
            part = slice(b * block_len, (b + 1) * block_len)
            for j in range(components):
                values = records_ref[j, :, part].astype(jnp.float32)
                masked[j * stations:(j + 1) * stations, part] = jnp.where(offsets < limit, values, 0.0)
        shifted[...] = jnp.zeros(shifted.shape, jnp.float32)

        def shift_one(s, carry):
            for j in range(components):
                c = j * stations + s
                moveout = moveouts_ref[j, s]
                base = pl.multiple_of(moveout // LANES * LANES, LANES)
                row = masked[pl.ds(c, 1), pl.ds(base, span)]
                shifted[pl.ds(c, 1), :] = pltpu.roll(row, span - (moveout - base), 1)
            return carry

        lax.fori_loop(0, stations, shift_one, 0)
        factor[...] = jnp.zeros(factor.shape, jnp.float32)
        for g in range(0, rows, 8):
            values = shifted[g:g + 8, :]
            energy = window_sum(values * values, window)[:, :length]
            factor[g:g + 8, :] = lax.rsqrt(jnp.maximum(energy, 1.0))
        source = lax.broadcasted_iota(jnp.int32, (LANES, LANES), 1)
        target = lax.broadcasted_iota(jnp.int32, (LANES, LANES), 0)
        mirrored = target // GROUP * GROUP + (GROUP - 1 - target % GROUP)
        swap = jnp.where(source == mirrored, 1.0, 0.0).astype(jnp.float32)
        for i in range(tiles):
            columns[i * LANES:(i + 1) * LANES, :] = lax.dot_general(
                swap, factor[:, i * LANES:(i + 1) * LANES],
                (((1,), (1,)), ((), ())),
                precision=lax.Precision.HIGHEST,
                preferred_element_type=jnp.float32,
            )
        bank_a[...] = jnp.zeros(bank_a.shape, bank_a.dtype)
        bank_b[...] = jnp.zeros(bank_b.shape, bank_b.dtype)
        total[...] = jnp.zeros(total.shape, total.dtype)

    def build(windows, bank):
        for j in range(components):
            values = templates_ref[0, j].astype(jnp.float32)
            squares = jnp.sum(values * values, axis=0, keepdims=True)
            unit = (values * lax.rsqrt(squares + 1e-06)).astype(jnp.bfloat16)
            bank[j * depth:j * depth + window, :] = unit
        for j in range(components):
            c = j * stations + step
            half = jnp.broadcast_to(shifted[pl.ds(c, 1), :], (8, span))
            strip = jnp.concatenate(
                [pltpu.roll(half, span - GROUP + 1 + b, 1, stride=1, stride_axis=0) for b in (0, 8)],
                axis=0,
            ).astype(jnp.bfloat16)
            lane = jnp.full((GROUP, LANES), c, jnp.int32)
            for a in range(LANES // GROUP):
                rolled = strip if a == 0 else pltpu.roll(strip, span - a * GROUP, 1)
                for i in range(tiles):
                    at = i * LANES + a * GROUP
                    scale = jnp.take_along_axis(columns[at:at + GROUP, :], lane, axis=1)
                    scale = scale.astype(jnp.bfloat16)
                    for d in range(depth_tiles):
                        piece = rolled[:, (i + d) * LANES:(i + d + 1) * LANES]
                        windows[at:at + GROUP, j * depth + d * LANES:j * depth + (d + 1) * LANES] = piece * scale

    def multiply(windows, bank):
        total[...] += jnp.dot(windows[...], bank[...], preferred_element_type=jnp.float32)

    @pl.when(step == 0)
    def first():
        prologue()
        build(windows_a, bank_a)

    @pl.when((step > 0) & (step < stations) & (step % 2 == 1))
    def odd():
        build(windows_b, bank_b)
        multiply(windows_a, bank_a)

    @pl.when((step > 0) & (step < stations) & (step % 2 == 0))
    def even():
        build(windows_a, bank_a)
        multiply(windows_b, bank_b)

    @pl.when(step == stations)
    def last():
        if stations % 2:
            multiply(windows_a, bank_a)
        else:
            multiply(windows_b, bank_b)
        core = core_ref[0]
        hops, region = keep_ref.shape[0], keep_ref.shape[1]
        turned = 7 - lax.broadcasted_iota(jnp.int32, (8, LANES), 0)
        for h in range(0, total.shape[1], LANES):
            for r in range(0, length, 8):
                source = r // GROUP * GROUP + (GROUP - 8 - r % GROUP)
                strips[r:r + 8, h:h + LANES] = jnp.take_along_axis(
                    total[source:source + 8, h:h + LANES], turned, axis=0)
        for x in range(hops):
            own = pl.multiple_of((2 * x + core) * region, region)
            other = pl.multiple_of((2 * x + 1 - core) * region, region)
            keep_ref[x] = strips[pl.ds(own, region), :]
            send_ref[x] = strips[pl.ds(other, region), :].astype(send_ref.dtype)


def correlate(core, records, templates, moveouts, uptime, hops):
    components, stations, length = records.shape
    window, bank_size = templates.shape[2:]
    block_count = uptime.shape[0]
    depth = up(window, LANES)
    rows = up(stations * components, 8)
    reach = length + depth + LANES + up(MAXMO, LANES)
    region = length // (2 * hops)
    body = functools.partial(
        correlate_kernel, stations=stations, components=components, length=length,
        window=window, block_count=block_count,
    )
    whole = lambda s, *_: (0, 0, 0)
    return pl.pallas_call(
        body,
        grid_spec=pltpu.PrefetchScalarGridSpec(
            num_scalar_prefetch=3,
            grid=(stations + 1,),
            in_specs=[
                pl.BlockSpec(records.shape, whole),
                pl.BlockSpec(
                    (1,) + templates.shape[1:],
                    lambda s, *_: (jnp.minimum(s, stations - 1), 0, 0, 0),
                ),
            ],
            out_specs=[
                pl.BlockSpec((hops, region, bank_size), whole),
                pl.BlockSpec((hops, region, bank_size), whole),
            ],
            scratch_shapes=[
                pltpu.VMEM((rows, reach), jnp.float32),
                pltpu.VMEM((rows, length + depth + LANES), jnp.float32),
                pltpu.VMEM((up(rows, LANES), length), jnp.float32),
                pltpu.VMEM((length, up(rows, LANES)), jnp.float32),
                pltpu.VMEM((length, bank_size), jnp.float32),
                pltpu.VMEM((length, components * depth), jnp.bfloat16),
                pltpu.VMEM((length, components * depth), jnp.bfloat16),
                pltpu.VMEM((components * depth, bank_size), jnp.bfloat16),
                pltpu.VMEM((components * depth, bank_size), jnp.bfloat16),
                pltpu.VMEM((length, bank_size), jnp.float32),
            ],
        ),
        out_shape=[
            jax.ShapeDtypeStruct((hops, region, bank_size), jnp.bfloat16),
            jax.ShapeDtypeStruct((hops, region, bank_size), jnp.float32),
        ],
        compiler_params=pltpu.CompilerParams(vmem_limit_bytes=60 * 2**20),
        name="correlate",
    )(core, moveouts, uptime, records, templates)


def body(records, templates, moveouts, uptime):
    tm, chan = lax.axis_size("tm"), lax.axis_size("chan")
    hops = tm // 2
    t, z = lax.axis_index("tm"), lax.axis_index("chan")
    x, core = t // 2, t % 2
    send, keep = correlate(
        core.reshape(1), records.transpose(1, 0, 2), templates, moveouts.T, uptime.T, hops
    )
    got = lax.ppermute(send, "tm", [(i, i ^ 1) for i in range(tm)])
    mine = keep + got.astype(jnp.float32)
    result = lax.dynamic_index_in_dim(mine, x, 0, keepdims=False)
    for step in range(1, hops):
        block = lax.dynamic_index_in_dim(mine, (x + step) % hops, 0, keepdims=False)
        perm = [(i, ((i // 2 + step) % hops) * 2 + i % 2) for i in range(tm)]
        result = result + lax.ppermute(block.astype(jnp.bfloat16), "tm", perm).astype(jnp.float32)
    mine = result.reshape(chan, result.shape[0] // chan, result.shape[1])
    result = lax.dynamic_index_in_dim(mine, z, 0, keepdims=False)
    for step in range(1, chan):
        block = lax.dynamic_index_in_dim(mine, (z + step) % chan, 0, keepdims=False)
        perm = [(i, (i + step) % chan) for i in range(chan)]
        result = result + lax.ppermute(block.astype(jnp.bfloat16), "chan", perm).astype(jnp.float32)
    return result.T


def solution(mesh):
    placed = (
        P(("grp", "tm", "chan"), None, None),
        P(("tm", "chan"), None, None, None),
        P(("tm", "chan"), None),
        P(("grp", "tm", "chan"), None),
    )
    return jax.shard_map(
        body, mesh=mesh, in_specs=placed, out_specs=P(None, ("grp", "tm", "chan")), check_vma=False
    )
```

```python
import functools

import jax
import jax.numpy as jnp
from jax import lax
from jax.experimental import pallas as pl
from jax.experimental.pallas import tpu as pltpu
from jax.sharding import PartitionSpec as P

MAXMO = 1000
LANES = 128
GROUP = 16


def up(value, unit):
    return -(-value // unit) * unit


def window_sum(values, window):
    def behind(array, by):
        return array if by == 0 else pltpu.roll(array, by, 1)

    total, offset, size, run = None, 0, 1, values
    while size <= window:
        if window & size:
            piece = behind(run, offset)
            total = piece if total is None else total + piece
            offset += size
        size *= 2
        if size <= window:
            run = run + behind(run, size // 2)
    return total


def correlate_kernel(
    core_ref, moveouts_ref, uptime_ref, records_ref, templates_ref,
    send_ref, keep_ref,
    masked, shifted, factor, bank, windows_a, windows_b, bank_a, bank_b, total,
    *, stations, components, length, window, block_count, batch,
):
    step = pl.program_id(0)
    steps = stations // batch
    rows = masked.shape[0]
    tiles = length // LANES
    groups = up(window, GROUP) // GROUP
    margin = up(window, LANES)
    block_len = length // block_count
    span = shifted.shape[1]
    lead = masked.shape[1] - length

    def prologue():
        masked[...] = jnp.zeros(masked.shape, jnp.float32)
        offsets = lax.broadcasted_iota(jnp.int32, (stations, LANES), 1)
        which = lax.broadcasted_iota(jnp.int32, (stations, LANES), 0)
        for b in range(block_count):
            limit = jnp.zeros((stations, LANES), jnp.int32)
            for s in range(stations):
                limit = jnp.where(which == s, uptime_ref[b, s], limit)
            for i in range(block_len // LANES):
                at = b * block_len + i * LANES
                live = offsets + i * LANES < limit
                for j in range(components):
                    values = records_ref[j, :, at:at + LANES].astype(jnp.float32)
                    factor[j * stations:(j + 1) * stations, at:at + LANES] = jnp.where(live, values, 0.0)
        mirror = LANES - 1 - lax.broadcasted_iota(jnp.int32, (8, LANES), 1)
        for g in range(0, rows, 8):
            for at in range(0, length, LANES):
                to = lead + length - LANES - at
                masked[g:g + 8, to:to + LANES] = jnp.take_along_axis(
                    factor[g:g + 8, at:at + LANES], mirror, axis=1)
        shifted[...] = jnp.zeros(shifted.shape, jnp.float32)

        def shift_one(s, carry):
            for j in range(components):
                c = j * stations + s
                moveout = moveouts_ref[j, s]
                whole = moveout // LANES * LANES
                base = pl.multiple_of(lead - margin - LANES - whole, LANES)
                row = masked[pl.ds(c, 1), pl.ds(base, span + LANES)]
                row = pltpu.roll(row, moveout - whole, 1)
                shifted[pl.ds(c, 1), :] = row[:, LANES:]
            return carry

        lax.fori_loop(0, stations, shift_one, 0)
        for g in range(0, rows, 8):
            values = shifted[g:g + 8, :]
            energy = window_sum(values * values, window)[:, margin:]
            factor[g:g + 8, :] = lax.rsqrt(jnp.maximum(energy, 1.0))
        bank[...] = jnp.zeros(bank.shape, bank.dtype)
        total[...] = jnp.zeros(total.shape, total.dtype)

    def build(windows, turned):
        for u in range(batch):
            for j in range(components):
                values = templates_ref[u, j].astype(jnp.float32)
                squares = jnp.sum(values * values, axis=0, keepdims=True)
                unit = (values * lax.rsqrt(squares + 1e-06)).astype(jnp.bfloat16)
                at = (u * components + j) * groups * GROUP
                bank[at:at + window, :] = unit
        turned[...] = bank[...].T
        for u in range(batch):
            for j in range(components):
                c = j * stations + step * batch + u
                half = jnp.broadcast_to(shifted[pl.ds(c, 1), :], (8, span))
                strip = jnp.concatenate(
                    [pltpu.roll(half, b, 1, stride=1, stride_axis=0) for b in (0, 8)], axis=0
                ).astype(jnp.bfloat16)
                scale = jnp.broadcast_to(factor[pl.ds(c, 1), :], (GROUP, length))
                scale = scale.astype(jnp.bfloat16)
                for a in range(min(groups, LANES // GROUP)):
                    rolled = strip if a == 0 else pltpu.roll(strip, a * GROUP, 1)
                    for g in range(a, groups, LANES // GROUP):
                        begin = margin - (g - a) * GROUP
                        at = ((u * components + j) * groups + g) * GROUP
                        windows[at:at + GROUP, :] = rolled[:, begin:begin + length] * scale

    def multiply(windows, turned):
        total[...] += jnp.dot(turned[:, :windows.shape[0]], windows[...],
                              preferred_element_type=jnp.float32)

    @pl.when(step == 0)
    def first():
        prologue()
        build(windows_a, bank_a)

    @pl.when((step > 0) & (step < steps) & (step % 2 == 1))
    def odd():
        build(windows_b, bank_b)
        multiply(windows_a, bank_a)

    @pl.when((step > 0) & (step < steps) & (step % 2 == 0))
    def even():
        build(windows_a, bank_a)
        multiply(windows_b, bank_b)

    @pl.when(step == steps)
    def last():
        if steps % 2:
            multiply(windows_a, bank_a)
        else:
            multiply(windows_b, bank_b)
        core = core_ref[0]
        hops, region = keep_ref.shape[0], keep_ref.shape[1]
        flip = LANES - 1 - lax.broadcasted_iota(jnp.int32, (LANES, LANES), 1)

        def ordered(begin, h):
            at = pl.multiple_of(length - LANES - begin, LANES)
            block = total[h:h + LANES, pl.ds(at, LANES)]
            return jnp.take_along_axis(block, flip, axis=1).T

        for x in range(hops):
            for r in range(0, region, LANES):
                for h in range(0, total.shape[0], LANES):
                    own = (2 * x + core) * region + r
                    other = (2 * x + 1 - core) * region + r
                    keep_ref[x, r:r + LANES, h:h + LANES] = ordered(own, h)
                    send_ref[x, r:r + LANES, h:h + LANES] = ordered(other, h).astype(send_ref.dtype)


def correlate(core, records, templates, moveouts, uptime, hops):
    components, stations, length = records.shape
    window, bank_size = templates.shape[2:]
    block_count = uptime.shape[0]
    margin = up(window, LANES)
    rows = up(stations * components, 8)
    region = length // (2 * hops)
    batch = 2 if stations % 2 == 0 else 1
    depth = batch * components * up(window, GROUP)
    body = functools.partial(
        correlate_kernel, stations=stations, components=components, length=length,
        window=window, block_count=block_count, batch=batch,
    )
    whole = lambda s, *_: (0, 0, 0)
    return pl.pallas_call(
        body,
        grid_spec=pltpu.PrefetchScalarGridSpec(
            num_scalar_prefetch=3,
            grid=(stations // batch + 1,),
            in_specs=[
                pl.BlockSpec(records.shape, whole),
                pl.BlockSpec(
                    (batch,) + templates.shape[1:],
                    lambda s, *_: (jnp.minimum(s, stations // batch - 1), 0, 0, 0),
                ),
            ],
            out_specs=[
                pl.BlockSpec((hops, region, bank_size), whole),
                pl.BlockSpec((hops, region, bank_size), whole),
            ],
            scratch_shapes=[
                pltpu.VMEM((rows, length + margin + LANES + up(MAXMO, LANES)), jnp.float32),
                pltpu.VMEM((rows, length + margin), jnp.float32),
                pltpu.VMEM((rows, length), jnp.float32),
                pltpu.VMEM((up(depth, LANES), bank_size), jnp.bfloat16),
                pltpu.VMEM((depth, length), jnp.bfloat16),
                pltpu.VMEM((depth, length), jnp.bfloat16),
                pltpu.VMEM((bank_size, up(depth, LANES)), jnp.bfloat16),
                pltpu.VMEM((bank_size, up(depth, LANES)), jnp.bfloat16),
                pltpu.VMEM((bank_size, length), jnp.float32),
            ],
        ),
        out_shape=[
            jax.ShapeDtypeStruct((hops, region, bank_size), jnp.bfloat16),
            jax.ShapeDtypeStruct((hops, region, bank_size), jnp.float32),
        ],
        compiler_params=pltpu.CompilerParams(vmem_limit_bytes=60 * 2**20),
        name="correlate",
    )(core, moveouts, uptime, records, templates)


def body(records, templates, moveouts, uptime):
    tm, chan = lax.axis_size("tm"), lax.axis_size("chan")
    hops = tm // 2
    t, z = lax.axis_index("tm"), lax.axis_index("chan")
    x, core = t // 2, t % 2
    send, keep = correlate(
        core.reshape(1), records.transpose(1, 0, 2), templates, moveouts.T, uptime.T, hops
    )
    got = lax.ppermute(send, "tm", [(i, i ^ 1) for i in range(tm)])
    mine = keep + got.astype(jnp.float32)
    result = lax.dynamic_index_in_dim(mine, x, 0, keepdims=False)
    for step in range(1, hops):
        block = lax.dynamic_index_in_dim(mine, (x + step) % hops, 0, keepdims=False)
        perm = [(i, ((i // 2 + step) % hops) * 2 + i % 2) for i in range(tm)]
        result = result + lax.ppermute(block.astype(jnp.bfloat16), "tm", perm).astype(jnp.float32)
    mine = result.reshape(chan, result.shape[0] // chan, result.shape[1])
    result = lax.dynamic_index_in_dim(mine, z, 0, keepdims=False)
    for step in range(1, chan):
        block = lax.dynamic_index_in_dim(mine, (z + step) % chan, 0, keepdims=False)
        perm = [(i, (i + step) % chan) for i in range(chan)]
        result = result + lax.ppermute(block.astype(jnp.bfloat16), "chan", perm).astype(jnp.float32)
    return result.T


def solution(mesh):
    placed = (
        P(("grp", "tm", "chan"), None, None),
        P(("tm", "chan"), None, None, None),
        P(("tm", "chan"), None),
        P(("grp", "tm", "chan"), None),
    )
    return jax.shard_map(
        body, mesh=mesh, in_specs=placed, out_specs=P(None, ("grp", "tm", "chan")), check_vma=False
    )
```

```python
import functools

import jax
import jax.numpy as jnp
from jax import lax
from jax.experimental import pallas as pl
from jax.experimental.pallas import tpu as pltpu
from jax.sharding import PartitionSpec as P

MAXMO = 1000
LANES = 128
GROUP = 16


def up(value, unit):
    return -(-value // unit) * unit


def window_sum(values, window):
    def behind(array, by):
        return array if by == 0 else pltpu.roll(array, by, 1)

    total, offset, size, run = None, 0, 1, values
    while size <= window:
        if window & size:
            piece = behind(run, offset)
            total = piece if total is None else total + piece
            offset += size
        size *= 2
        if size <= window:
            run = run + behind(run, size // 2)
    return total


def correlate_kernel(
    core_ref, moveouts_ref, uptime_ref, records_ref, templates_ref,
    send_ref, keep_ref,
    masked, shifted, factor, loaded, bank, windows_a, windows_b, bank_a, bank_b, total, arrived,
    *, window, batch,
):
    components, stations, length = records_ref.shape
    block_count = uptime_ref.shape[0]
    batches = stations // batch
    rows = masked.shape[0]
    groups = up(window, GROUP) // GROUP
    margin = up(window, LANES)
    block_len = length // block_count
    span = shifted.shape[1]
    lead = masked.shape[1] - length

    def fetch(i):
        at = pl.ds(i * batch, batch)
        return pltpu.make_async_copy(templates_ref.at[at], loaded.at[at], arrived.at[i])

    for i in range(batches):
        fetch(i).start()

    masked[...] = jnp.zeros(masked.shape, jnp.float32)
    offsets = lax.broadcasted_iota(jnp.int32, (stations, LANES), 1)
    which = lax.broadcasted_iota(jnp.int32, (stations, LANES), 0)
    for b in range(block_count):
        limit = jnp.zeros((stations, LANES), jnp.int32)
        for s in range(stations):
            limit = jnp.where(which == s, uptime_ref[b, s], limit)
        for i in range(block_len // LANES):
            at = b * block_len + i * LANES
            live = offsets + i * LANES < limit
            for j in range(components):
                values = records_ref[j, :, at:at + LANES].astype(jnp.float32)
                factor[j * stations:(j + 1) * stations, at:at + LANES] = jnp.where(live, values, 0.0)
    mirror = LANES - 1 - lax.broadcasted_iota(jnp.int32, (8, LANES), 1)
    for g in range(0, rows, 8):
        for at in range(0, length, LANES):
            to = lead + length - LANES - at
            masked[g:g + 8, to:to + LANES] = jnp.take_along_axis(
                factor[g:g + 8, at:at + LANES], mirror, axis=1)
    shifted[...] = jnp.zeros(shifted.shape, jnp.float32)
    for j in range(components):
        for s in range(stations):
            c = j * stations + s
            moveout = moveouts_ref[j, s]
            whole = moveout // LANES * LANES
            base = pl.multiple_of(lead - margin - LANES - whole, LANES)
            row = masked[c:c + 1, pl.ds(base, span + LANES)]
            row = pltpu.roll(row, moveout - whole, 1)
            shifted[c:c + 1, :] = row[:, LANES:]
    for g in range(0, rows, 8):
        values = shifted[g:g + 8, :]
        energy = window_sum(values * values, window)[:, margin:]
        factor[g:g + 8, :] = lax.rsqrt(jnp.maximum(energy, 1.0))
    bank[...] = jnp.zeros(bank.shape, bank.dtype)
    total[...] = jnp.zeros(total.shape, total.dtype)
    depth = batch * components * groups * GROUP
    for windows in (windows_a, windows_b):
        if windows.shape[0] > depth:
            windows[depth:, :] = jnp.zeros((windows.shape[0] - depth, length), windows.dtype)

    def build(i, windows, turned):
        fetch(i).wait()
        for u in range(batch):
            for j in range(components):
                values = loaded[i * batch + u, j].astype(jnp.float32)
                squares = jnp.sum(values * values, axis=0, keepdims=True)
                unit = (values * lax.rsqrt(squares + 1e-06)).astype(jnp.bfloat16)
                at = (u * components + j) * groups * GROUP
                bank[at:at + window, :] = unit
        turned[...] = bank[...].T
        for u in range(batch):
            for j in range(components):
                c = j * stations + i * batch + u
                half = jnp.broadcast_to(shifted[pl.ds(c, 1), :], (8, span))
                strip = jnp.concatenate(
                    [pltpu.roll(half, b, 1, stride=1, stride_axis=0) for b in (0, 8)], axis=0
                ).astype(jnp.bfloat16)
                scale = jnp.broadcast_to(factor[pl.ds(c, 1), :], (GROUP, length))
                scale = scale.astype(jnp.bfloat16)
                for a in range(min(groups, LANES // GROUP)):
                    rolled = strip if a == 0 else pltpu.roll(strip, a * GROUP, 1)
                    for g in range(a, groups, LANES // GROUP):
                        begin = margin - (g - a) * GROUP
                        at = ((u * components + j) * groups + g) * GROUP
                        windows[at:at + GROUP, :] = rolled[:, begin:begin + length] * scale

    def multiply(windows, turned):
        width = min(2 * LANES, length)
        for n in range(0, length, width):
            total[:, n:n + width] += jnp.dot(
                turned[...], windows[:, n:n + width], preferred_element_type=jnp.float32)

    build(0, windows_a, bank_a)

    def two_batches(i, carry):
        build(2 * i + 1, windows_b, bank_b)
        multiply(windows_a, bank_a)
        build(2 * i + 2, windows_a, bank_a)
        multiply(windows_b, bank_b)
        return carry

    if batches > 2:
        lax.fori_loop(0, (batches - 1) // 2, two_batches, 0)
    if batches % 2 == 0:
        build(batches - 1, windows_b, bank_b)
        multiply(windows_a, bank_a)
        multiply(windows_b, bank_b)
    else:
        multiply(windows_a, bank_a)

    core = core_ref[0]
    hops, region = keep_ref.shape[0], keep_ref.shape[1]
    flip = LANES - 1 - lax.broadcasted_iota(jnp.int32, (LANES, LANES), 1)

    def ordered(begin, h):
        at = pl.multiple_of(length - LANES - begin, LANES)
        block = total[h:h + LANES, pl.ds(at, LANES)]
        return jnp.take_along_axis(block, flip, axis=1).T

    for x in range(hops):
        for r in range(0, region, LANES):
            for h in range(0, total.shape[0], LANES):
                own = (2 * x + core) * region + r
                other = (2 * x + 1 - core) * region + r
                keep_ref[x, r:r + LANES, h:h + LANES] = ordered(own, h)
                send_ref[x, r:r + LANES, h:h + LANES] = ordered(other, h).astype(send_ref.dtype)


def correlate(core, records, templates, moveouts, uptime, hops):
    components, stations, length = records.shape
    window, bank_size = templates.shape[2:]
    margin = up(window, LANES)
    rows = up(stations * components, 8)
    region = length // (2 * hops)
    batch = 2 if stations % 2 == 0 else 1
    depth = up(batch * components * up(window, GROUP), LANES)
    scalars = pl.BlockSpec(memory_space=pltpu.SMEM)
    vectors = pl.BlockSpec(memory_space=pltpu.VMEM)
    return pl.pallas_call(
        functools.partial(correlate_kernel, window=window, batch=batch),
        in_specs=[scalars, scalars, scalars, vectors, pl.BlockSpec(memory_space=pl.ANY)],
        out_specs=[vectors, vectors],
        scratch_shapes=[
            pltpu.VMEM((rows, length + margin + LANES + up(MAXMO, LANES)), jnp.float32),
            pltpu.VMEM((rows, length + margin), jnp.float32),
            pltpu.VMEM((rows, length), jnp.float32),
            pltpu.VMEM(templates.shape, templates.dtype),
            pltpu.VMEM((depth, bank_size), jnp.bfloat16),
            pltpu.VMEM((depth, length), jnp.bfloat16),
            pltpu.VMEM((depth, length), jnp.bfloat16),
            pltpu.VMEM((bank_size, depth), jnp.bfloat16),
            pltpu.VMEM((bank_size, depth), jnp.bfloat16),
            pltpu.VMEM((bank_size, length), jnp.float32),
            pltpu.SemaphoreType.DMA((stations // batch,)),
        ],
        out_shape=[
            jax.ShapeDtypeStruct((hops, region, bank_size), jnp.bfloat16),
            jax.ShapeDtypeStruct((hops, region, bank_size), jnp.float32),
        ],
        compiler_params=pltpu.CompilerParams(vmem_limit_bytes=60 * 2**20),
        name="correlate",
    )(core, moveouts, uptime, records, templates)


def body(records, templates, moveouts, uptime):
    tm, chan = lax.axis_size("tm"), lax.axis_size("chan")
    hops = tm // 2
    t, z = lax.axis_index("tm"), lax.axis_index("chan")
    x, core = t // 2, t % 2
    send, keep = correlate(
        core.reshape(1), records.transpose(1, 0, 2), templates, moveouts.T, uptime.T, hops
    )
    got = lax.ppermute(send, "tm", [(i, i ^ 1) for i in range(tm)])
    mine = keep + got.astype(jnp.float32)
    result = lax.dynamic_index_in_dim(mine, x, 0, keepdims=False)
    for step in range(1, hops):
        block = lax.dynamic_index_in_dim(mine, (x + step) % hops, 0, keepdims=False)
        perm = [(i, ((i // 2 + step) % hops) * 2 + i % 2) for i in range(tm)]
        result = result + lax.ppermute(block.astype(jnp.bfloat16), "tm", perm).astype(jnp.float32)
    mine = result.reshape(chan, result.shape[0] // chan, result.shape[1])
    result = lax.dynamic_index_in_dim(mine, z, 0, keepdims=False)
    for step in range(1, chan):
        block = lax.dynamic_index_in_dim(mine, (z + step) % chan, 0, keepdims=False)
        perm = [(i, (i + step) % chan) for i in range(chan)]
        result = result + lax.ppermute(block.astype(jnp.bfloat16), "chan", perm).astype(jnp.float32)
    return result.T


def solution(mesh):
    placed = (
        P(("grp", "tm", "chan"), None, None),
        P(("tm", "chan"), None, None, None),
        P(("tm", "chan"), None),
        P(("grp", "tm", "chan"), None),
    )
    return jax.shard_map(
        body, mesh=mesh, in_specs=placed, out_specs=P(None, ("grp", "tm", "chan")), check_vma=False
    )
```

```python
import functools

import jax
import jax.numpy as jnp
from jax import lax
from jax.experimental import pallas as pl
from jax.experimental.pallas import tpu as pltpu
from jax.sharding import PartitionSpec as P

MAXMO = 1000
LANES = 128
GROUP = 16


def up(value, unit):
    return -(-value // unit) * unit


def window_sum(values, window):
    def behind(array, by):
        return array if by == 0 else pltpu.roll(array, by, 1)

    total, offset, size, run = None, 0, 1, values
    while size <= window:
        if window & size:
            piece = behind(run, offset)
            total = piece if total is None else total + piece
            offset += size
        size *= 2
        if size <= window:
            run = run + behind(run, size // 2)
    return total


def correlate_kernel(
    core_ref, moveouts_ref, uptime_ref, records_ref, templates_ref,
    send_ref, keep_ref,
    masked, shifted, factor, loaded, bank, windows_a, windows_b, bank_a, bank_b, total, arrived,
    *, window, batch,
):
    components, stations, length = records_ref.shape
    block_count = uptime_ref.shape[0]
    batches = stations // batch
    rows = masked.shape[0]
    groups = up(window, GROUP) // GROUP
    margin = up(window, LANES)
    block_len = length // block_count
    span = shifted.shape[1]
    lead = masked.shape[1] - length

    def fetch(i):
        at = pl.ds(i * batch, batch)
        return pltpu.make_async_copy(templates_ref.at[at], loaded.at[at], arrived.at[i])

    for i in range(batches):
        fetch(i).start()

    masked[...] = jnp.zeros(masked.shape, jnp.float32)
    offsets = lax.broadcasted_iota(jnp.int32, (stations, LANES), 1)
    which = lax.broadcasted_iota(jnp.int32, (stations, LANES), 0)
    for b in range(block_count):
        limit = jnp.zeros((stations, LANES), jnp.int32)
        for s in range(stations):
            limit = jnp.where(which == s, uptime_ref[b, s], limit)
        for i in range(block_len // LANES):
            at = b * block_len + i * LANES
            live = offsets + i * LANES < limit
            for j in range(components):
                values = records_ref[j, :, at:at + LANES].astype(jnp.float32)
                factor[j * stations:(j + 1) * stations, at:at + LANES] = jnp.where(live, values, 0.0)
    mirror = LANES - 1 - lax.broadcasted_iota(jnp.int32, (8, LANES), 1)
    for g in range(0, rows, 8):
        for at in range(0, length, LANES):
            to = lead + length - LANES - at
            masked[g:g + 8, to:to + LANES] = jnp.take_along_axis(
                factor[g:g + 8, at:at + LANES], mirror, axis=1)
    shifted[...] = jnp.zeros(shifted.shape, jnp.float32)
    for j in range(components):
        for s in range(stations):
            c = j * stations + s
            moveout = moveouts_ref[j, s]
            whole = moveout // LANES * LANES
            base = pl.multiple_of(lead - margin - LANES - whole, LANES)
            row = masked[c:c + 1, pl.ds(base, span + LANES)]
            row = pltpu.roll(row, moveout - whole, 1)
            shifted[c:c + 1, :] = row[:, LANES:]
    for g in range(0, rows, 8):
        values = shifted[g:g + 8, :]
        energy = window_sum(values * values, window)[:, margin:]
        factor[g:g + 8, :] = lax.rsqrt(jnp.maximum(energy, 1.0))
    bank[...] = jnp.zeros(bank.shape, bank.dtype)
    total[...] = jnp.zeros(total.shape, total.dtype)
    depth = batch * components * groups * GROUP
    for windows in (windows_a, windows_b):
        if windows.shape[0] > depth:
            windows[depth:, :] = jnp.zeros((windows.shape[0] - depth, length), windows.dtype)

    width = min(2 * LANES, length)

    def multiply(n, windows, turned):
        total[:, n:n + width] += jnp.dot(
            turned[...], windows[:, n:n + width], preferred_element_type=jnp.float32)

    def build(i, windows, turned, pending=None):
        fetch(i).wait()
        left = list(range(0, length, width)) if pending else []
        share = up(len(left), batch * components) // (batch * components)
        for u in range(batch):
            for j in range(components):
                values = loaded[i * batch + u, j].astype(jnp.float32)
                squares = jnp.sum(values * values, axis=0, keepdims=True)
                unit = (values * lax.rsqrt(squares + 1e-06)).astype(jnp.bfloat16)
                at = (u * components + j) * groups * GROUP
                bank[at:at + window, :] = unit
        turned[...] = bank[...].T
        for u in range(batch):
            for j in range(components):
                c = j * stations + i * batch + u
                half = jnp.broadcast_to(shifted[pl.ds(c, 1), :], (8, span))
                strip = jnp.concatenate(
                    [pltpu.roll(half, b, 1, stride=1, stride_axis=0) for b in (0, 8)], axis=0
                ).astype(jnp.bfloat16)
                scale = jnp.broadcast_to(factor[pl.ds(c, 1), :], (GROUP, length))
                scale = scale.astype(jnp.bfloat16)
                for a in range(min(groups, LANES // GROUP)):
                    rolled = strip if a == 0 else pltpu.roll(strip, a * GROUP, 1)
                    for g in range(a, groups, LANES // GROUP):
                        begin = margin - (g - a) * GROUP
                        at = ((u * components + j) * groups + g) * GROUP
                        windows[at:at + GROUP, :] = rolled[:, begin:begin + length] * scale
                for n in left[:share]:
                    multiply(n, *pending)
                left = left[share:]
        for n in left:
            multiply(n, *pending)

    def finish(windows, turned):
        for n in range(0, length, width):
            multiply(n, windows, turned)

    a, b = (windows_a, bank_a), (windows_b, bank_b)
    build(0, *a)

    def two_batches(i, carry):
        build(2 * i + 1, *b, a)
        build(2 * i + 2, *a, b)
        return carry

    if batches > 2:
        lax.fori_loop(0, (batches - 1) // 2, two_batches, 0)
    if batches % 2 == 0:
        build(batches - 1, *b, a)
        finish(*b)
    else:
        finish(*a)

    core = core_ref[0]
    hops, region = keep_ref.shape[0], keep_ref.shape[1]
    flip = LANES - 1 - lax.broadcasted_iota(jnp.int32, (LANES, LANES), 1)

    def ordered(begin, h):
        at = pl.multiple_of(length - LANES - begin, LANES)
        block = total[h:h + LANES, pl.ds(at, LANES)]
        return jnp.take_along_axis(block, flip, axis=1).T

    for x in range(hops):
        for r in range(0, region, LANES):
            for h in range(0, total.shape[0], LANES):
                own = (2 * x + core) * region + r
                other = (2 * x + 1 - core) * region + r
                keep_ref[x, r:r + LANES, h:h + LANES] = ordered(own, h)
                send_ref[x, r:r + LANES, h:h + LANES] = ordered(other, h).astype(send_ref.dtype)


def correlate(core, records, templates, moveouts, uptime, hops):
    components, stations, length = records.shape
    window, bank_size = templates.shape[2:]
    margin = up(window, LANES)
    rows = up(stations * components, 8)
    region = length // (2 * hops)
    batch = 2 if stations % 2 == 0 else 1
    depth = up(batch * components * up(window, GROUP), LANES)
    scalars = pl.BlockSpec(memory_space=pltpu.SMEM)
    vectors = pl.BlockSpec(memory_space=pltpu.VMEM)
    return pl.pallas_call(
        functools.partial(correlate_kernel, window=window, batch=batch),
        in_specs=[scalars, scalars, scalars, vectors, pl.BlockSpec(memory_space=pl.ANY)],
        out_specs=[vectors, vectors],
        scratch_shapes=[
            pltpu.VMEM((rows, length + margin + LANES + up(MAXMO, LANES)), jnp.float32),
            pltpu.VMEM((rows, length + margin), jnp.float32),
            pltpu.VMEM((rows, length), jnp.float32),
            pltpu.VMEM(templates.shape, templates.dtype),
            pltpu.VMEM((depth, bank_size), jnp.bfloat16),
            pltpu.VMEM((depth, length), jnp.bfloat16),
            pltpu.VMEM((depth, length), jnp.bfloat16),
            pltpu.VMEM((bank_size, depth), jnp.bfloat16),
            pltpu.VMEM((bank_size, depth), jnp.bfloat16),
            pltpu.VMEM((bank_size, length), jnp.float32),
            pltpu.SemaphoreType.DMA((stations // batch,)),
        ],
        out_shape=[
            jax.ShapeDtypeStruct((hops, region, bank_size), jnp.bfloat16),
            jax.ShapeDtypeStruct((hops, region, bank_size), jnp.float32),
        ],
        compiler_params=pltpu.CompilerParams(vmem_limit_bytes=60 * 2**20),
        name="correlate",
    )(core, moveouts, uptime, records, templates)


def body(records, templates, moveouts, uptime):
    tm, chan = lax.axis_size("tm"), lax.axis_size("chan")
    hops = tm // 2
    t, z = lax.axis_index("tm"), lax.axis_index("chan")
    x, core = t // 2, t % 2
    send, keep = correlate(
        core.reshape(1), records.transpose(1, 0, 2), templates, moveouts.T, uptime.T, hops
    )
    got = lax.ppermute(send, "tm", [(i, i ^ 1) for i in range(tm)])
    mine = keep + got.astype(jnp.float32)
    result = lax.dynamic_index_in_dim(mine, x, 0, keepdims=False)
    for step in range(1, hops):
        block = lax.dynamic_index_in_dim(mine, (x + step) % hops, 0, keepdims=False)
        perm = [(i, ((i // 2 + step) % hops) * 2 + i % 2) for i in range(tm)]
        result = result + lax.ppermute(block.astype(jnp.bfloat16), "tm", perm).astype(jnp.float32)
    mine = result.reshape(chan, result.shape[0] // chan, result.shape[1])
    result = lax.dynamic_index_in_dim(mine, z, 0, keepdims=False)
    for step in range(1, chan):
        block = lax.dynamic_index_in_dim(mine, (z + step) % chan, 0, keepdims=False)
        perm = [(i, (i + step) % chan) for i in range(chan)]
        result = result + lax.ppermute(block.astype(jnp.bfloat16), "chan", perm).astype(jnp.float32)
    return result.T


def solution(mesh):
    placed = (
        P(("grp", "tm", "chan"), None, None),
        P(("tm", "chan"), None, None, None),
        P(("tm", "chan"), None),
        P(("grp", "tm", "chan"), None),
    )
    return jax.shard_map(
        body, mesh=mesh, in_specs=placed, out_specs=P(None, ("grp", "tm", "chan")), check_vma=False
    )
```

```python
import functools

import jax
import jax.numpy as jnp
from jax import lax
from jax.experimental import pallas as pl
from jax.experimental.pallas import tpu as pltpu
from jax.sharding import PartitionSpec as P

MAXMO = 1000
LANES = 128
GROUP = 16


def up(value, unit):
    return -(-value // unit) * unit


def window_sum(values, window):
    def behind(array, by):
        return array if by == 0 else pltpu.roll(array, by, 1)

    total, offset, size, run = None, 0, 1, values
    while size <= window:
        if window & size:
            piece = behind(run, offset)
            total = piece if total is None else total + piece
            offset += size
        size *= 2
        if size <= window:
            run = run + behind(run, size // 2)
    return total


def mirrored(array, region, size):
    return pl.multiple_of(array - (region + 1) * size, LANES)


def build_windows(shifted, factor, windows, channel, row, begins, size, groups, margin):
    for n, begin in enumerate(begins):
        half = jnp.broadcast_to(
            shifted[pl.ds(channel, 1), pl.ds(begin, size + margin)], (8, size + margin))
        strip = jnp.concatenate(
            [pltpu.roll(half, b, 1, stride=1, stride_axis=0) for b in (0, 8)], axis=0
        ).astype(jnp.bfloat16)
        scale = jnp.broadcast_to(factor[pl.ds(channel, 1), pl.ds(begin, size)], (GROUP, size))
        scale = scale.astype(jnp.bfloat16)
        for a in range(min(groups, LANES // GROUP)):
            deepest = list(range(a, groups, LANES // GROUP))[-1]
            first = margin - (deepest - a) * GROUP
            cut = max(first - LANES, 0)
            rolled = strip[:, cut:]
            rolled = rolled if a == 0 else pltpu.roll(rolled, a * GROUP, 1)
            for g in range(a, groups, LANES // GROUP):
                lane = margin - (g - a) * GROUP - cut
                windows[row + g * GROUP:row + (g + 1) * GROUP, n * size:(n + 1) * size] = (
                    rolled[:, lane:lane + size] * scale)


def multiply(total, windows, banks, width):
    for n in range(0, total.shape[1], width):
        result = total[:, n:n + width]
        for k, bank in enumerate(banks):
            depth = bank.shape[1]
            result += jnp.dot(
                bank[...], windows[k * depth:(k + 1) * depth, n:n + width],
                preferred_element_type=jnp.float32)
        total[:, n:n + width] = result


def in_order(total, at, h):
    flip = LANES - 1 - lax.broadcasted_iota(jnp.int32, (LANES, LANES), 1)
    return jnp.take_along_axis(total[h:h + LANES, at:at + LANES], flip, axis=1).T


def write_regions(total, out_ref, extra=None):
    count, size, bank_size = out_ref.shape
    for n in range(count):
        for r in range(0, size, LANES):
            for h in range(0, bank_size, LANES):
                block = in_order(total, n * size + size - LANES - r, h)
                if extra is not None:
                    block = block + extra(r, h)
                out_ref[n, r:r + LANES, h:h + LANES] = block.astype(out_ref.dtype)


def first_kernel(
    place_ref, moveouts_ref, uptime_ref, records_ref, templates_ref,
    send_ref, shifted, factor, banks_ref,
    masked, loaded, bank, windows_a, windows_b, bank_a, bank_b, total, arrived, stored,
    *, window, batch,
):
    components, stations, length = records_ref.shape
    block_count = uptime_ref.shape[0]
    batches = stations // batch
    rows = masked.shape[0]
    groups = up(window, GROUP) // GROUP
    margin = up(window, LANES)
    block_len = length // block_count
    span = shifted.shape[1]
    lead = masked.shape[1] - length

    def fetch(i):
        at = pl.ds(i * batch, batch)
        return pltpu.make_async_copy(templates_ref.at[at], loaded.at[at], arrived.at[i])

    for i in range(batches):
        fetch(i).start()

    masked[...] = jnp.zeros(masked.shape, jnp.float32)
    offsets = lax.broadcasted_iota(jnp.int32, (stations, LANES), 1)
    which = lax.broadcasted_iota(jnp.int32, (stations, LANES), 0)
    for b in range(block_count):
        limit = jnp.zeros((stations, LANES), jnp.int32)
        for s in range(stations):
            limit = jnp.where(which == s, uptime_ref[b, s], limit)
        for i in range(block_len // LANES):
            at = b * block_len + i * LANES
            live = offsets + i * LANES < limit
            for j in range(components):
                values = records_ref[j, :, at:at + LANES].astype(jnp.float32)
                factor[j * stations:(j + 1) * stations, at:at + LANES] = jnp.where(live, values, 0.0)
    mirror = LANES - 1 - lax.broadcasted_iota(jnp.int32, (8, LANES), 1)
    for g in range(0, rows, 8):
        for at in range(0, length, LANES):
            to = lead + length - LANES - at
            masked[g:g + 8, to:to + LANES] = jnp.take_along_axis(
                factor[g:g + 8, at:at + LANES], mirror, axis=1)
    shifted[...] = jnp.zeros(shifted.shape, jnp.float32)
    for j in range(components):
        for s in range(stations):
            c = j * stations + s
            moveout = moveouts_ref[j, s]
            whole = moveout // LANES * LANES
            base = pl.multiple_of(lead - margin - LANES - whole, LANES)
            row = masked[c:c + 1, pl.ds(base, span + LANES)]
            row = pltpu.roll(row, moveout - whole, 1)
            shifted[c:c + 1, :] = row[:, LANES:]
    for g in range(0, rows, 8):
        values = shifted[g:g + 8, :]
        energy = window_sum(values * values, window)[:, margin:]
        factor[g:g + 8, :] = lax.rsqrt(jnp.maximum(energy, 1.0))
    bank[...] = jnp.zeros(bank.shape, bank.dtype)
    total[...] = jnp.zeros(total.shape, total.dtype)
    depth = batch * components * groups * GROUP
    for windows in (windows_a, windows_b):
        if windows.shape[0] > depth:
            windows[depth:, :] = jnp.zeros((windows.shape[0] - depth, windows.shape[1]), windows.dtype)

    count, size = send_ref.shape[:2]
    core = place_ref[0] % 2
    begins = [mirrored(length, 2 * x + 1 - core, size) for x in range(count)]
    width = min(2 * LANES, size)

    def store(i, turned, which):
        return pltpu.make_async_copy(turned, banks_ref.at[i], stored.at[which])

    def build(i, windows, turned, which):
        fetch(i).wait()
        for u in range(batch):
            for j in range(components):
                values = loaded[i * batch + u, j].astype(jnp.float32)
                squares = jnp.sum(values * values, axis=0, keepdims=True)
                unit = (values * lax.rsqrt(squares + 1e-06)).astype(jnp.bfloat16)
                at = (u * components + j) * groups * GROUP
                bank[at:at + window, :] = unit
        turned[...] = bank[...].T
        for u in range(batch):
            for j in range(components):
                build_windows(
                    shifted, factor, windows, j * stations + i * batch + u,
                    (u * components + j) * groups * GROUP, begins, size, groups, margin)
        store(i, turned, which).start()

    build(0, windows_a, bank_a, 0)

    def two_batches(i, carry):
        @pl.when(i > 0)
        def _():
            store(2 * i - 1, bank_b, 1).wait()
        build(2 * i + 1, windows_b, bank_b, 1)
        multiply(total, windows_a, [bank_a], width)
        store(2 * i, bank_a, 0).wait()
        build(2 * i + 2, windows_a, bank_a, 0)
        multiply(total, windows_b, [bank_b], width)
        return carry

    if batches > 2:
        lax.fori_loop(0, (batches - 1) // 2, two_batches, 0)
    if batches % 2 == 0:
        if batches > 2:
            store(batches - 3, bank_b, 1).wait()
        build(batches - 1, windows_b, bank_b, 1)
        multiply(total, windows_a, [bank_a], width)
        multiply(total, windows_b, [bank_b], width)
        store(batches - 2, bank_a, 0).wait()
        store(batches - 1, bank_b, 1).wait()
    else:
        multiply(total, windows_a, [bank_a], width)
        store(batches - 1, bank_a, 0).wait()
        if batches > 1:
            store(batches - 2, bank_b, 1).wait()
    write_regions(total, send_ref)


def next_kernel(
    place_ref, shifted, factor, banks_ref, *refs,
    components, window, batch, own, phases,
):
    if own:
        came_ref, *refs = refs
    out_ref, loaded, windows_a, windows_b, total, arrived = refs
    length = factor.shape[1]
    batches = banks_ref.shape[0]
    slabs = batches // phases
    stations = batches * batch
    groups = up(window, GROUP) // GROUP
    margin = up(window, LANES)
    count, size = out_ref.shape[:2]
    slab = loaded.shape[2]

    def fetch(i):
        return pltpu.make_async_copy(banks_ref.at[i], loaded.at[i], arrived.at[i])

    for i in range(batches):
        fetch(i).start()
    total[...] = jnp.zeros(total.shape, total.dtype)
    depth = batch * components * groups * GROUP
    for windows in (windows_a, windows_b):
        for k in range(slabs):
            if slab > depth:
                windows[k * slab + depth:(k + 1) * slab, :] = jnp.zeros(
                    (slab - depth, windows.shape[1]), windows.dtype)
    core, x = place_ref[0] % 2, place_ref[0] // 2
    hops = length // (2 * size)
    if own:
        begins = [mirrored(length, 2 * x + core, size)]
    else:
        begins = [mirrored(length, 2 * ((x + n) % hops) + core, size) for n in range(1, hops)]
    width = min(2 * LANES, size)

    def build(p, windows):
        for k in range(slabs):
            for u in range(batch):
                for j in range(components):
                    build_windows(
                        shifted, factor, windows,
                        j * stations + (p * slabs + k) * batch + u,
                        k * slab + (u * components + j) * groups * GROUP,
                        begins, size, groups, margin)

    def product(p, windows):
        multiply(total, windows, [loaded.at[p * slabs + k] for k in range(slabs)], width)

    def ready(p):
        for k in range(slabs):
            fetch(p * slabs + k).wait()

    build(0, windows_a)

    def two_phases(i, carry):
        ready(2 * i)
        build(2 * i + 1, windows_b)
        product(2 * i, windows_a)
        ready(2 * i + 1)
        build(2 * i + 2, windows_a)
        product(2 * i + 1, windows_b)
        return carry

    if phases > 2:
        lax.fori_loop(0, (phases - 1) // 2, two_phases, 0)
    if phases % 2 == 0:
        ready(phases - 2)
        build(phases - 1, windows_b)
        product(phases - 2, windows_a)
        ready(phases - 1)
        product(phases - 1, windows_b)
    else:
        ready(phases - 1)
        product(phases - 1, windows_a)
    if own:
        write_regions(total, out_ref, lambda r, h: came_ref[
            x, r:r + LANES, h:h + LANES].astype(jnp.float32))
    else:
        write_regions(total, out_ref)


SCALARS = pl.BlockSpec(memory_space=pltpu.SMEM)
VECTORS = pl.BlockSpec(memory_space=pltpu.VMEM)
FAR = pl.BlockSpec(memory_space=pl.ANY)


def cost(stations, components, window, bank_size, samples, read):
    return pl.CostEstimate(
        flops=2 * stations * components * window * bank_size * samples,
        bytes_accessed=read, transcendentals=0)


def first_part(place, records, templates, moveouts, uptime, hops, batch):
    components, stations, length = records.shape
    window, bank_size = templates.shape[2:]
    margin = up(window, LANES)
    rows = up(stations * components, 8)
    region = length // (2 * hops)
    depth = up(batch * components * up(window, GROUP), LANES)
    return pl.pallas_call(
        functools.partial(first_kernel, window=window, batch=batch),
        in_specs=[SCALARS, SCALARS, SCALARS, VECTORS, FAR],
        out_specs=[VECTORS, VECTORS, VECTORS, FAR],
        scratch_shapes=[
            pltpu.VMEM((rows, length + margin + LANES + up(MAXMO, LANES)), jnp.float32),
            pltpu.VMEM(templates.shape, templates.dtype),
            pltpu.VMEM((depth, bank_size), jnp.bfloat16),
            pltpu.VMEM((depth, hops * region), jnp.bfloat16),
            pltpu.VMEM((depth, hops * region), jnp.bfloat16),
            pltpu.VMEM((bank_size, depth), jnp.bfloat16),
            pltpu.VMEM((bank_size, depth), jnp.bfloat16),
            pltpu.VMEM((bank_size, hops * region), jnp.float32),
            pltpu.SemaphoreType.DMA((stations // batch,)),
            pltpu.SemaphoreType.DMA((2,)),
        ],
        out_shape=[
            jax.ShapeDtypeStruct((hops, region, bank_size), jnp.bfloat16),
            jax.ShapeDtypeStruct((rows, length + margin), jnp.float32),
            jax.ShapeDtypeStruct((rows, length), jnp.float32),
            jax.ShapeDtypeStruct((stations // batch, bank_size, depth), jnp.bfloat16),
        ],
        compiler_params=pltpu.CompilerParams(vmem_limit_bytes=60 * 2**20),
        cost_estimate=cost(stations, components, window, bank_size, hops * region,
                           2 * templates.size * 2),
        name="other_core",
    )(place, moveouts, uptime, records, templates)


def next_part(place, shifted, factor, banks, came, count, region, components, window, batch):
    batches, bank_size, depth = banks.shape
    phases = batches // 2 if batches % 2 == 0 else batches
    slabs = batches // phases
    own = came is not None
    return pl.pallas_call(
        functools.partial(next_kernel, components=components, window=window, batch=batch,
                          own=own, phases=phases),
        in_specs=[SCALARS, VECTORS, VECTORS, FAR] + [VECTORS] * own,
        out_specs=VECTORS,
        scratch_shapes=[
            pltpu.VMEM(banks.shape, banks.dtype),
            pltpu.VMEM((slabs * depth, count * region), jnp.bfloat16),
            pltpu.VMEM((slabs * depth, count * region), jnp.bfloat16),
            pltpu.VMEM((bank_size, count * region), jnp.float32),
            pltpu.SemaphoreType.DMA((batches,)),
        ],
        out_shape=jax.ShapeDtypeStruct((count, region, bank_size), jnp.float32),
        compiler_params=pltpu.CompilerParams(vmem_limit_bytes=60 * 2**20),
        cost_estimate=cost(batches * batch, components, window, bank_size, count * region,
                           banks.size * 2),
        name="own_region" if own else "other_chips",
    )(place, shifted, factor, banks, *([came] if own else []))


def body(records, templates, moveouts, uptime):
    tm, chan = lax.axis_size("tm"), lax.axis_size("chan")
    hops = tm // 2
    t, z = lax.axis_index("tm"), lax.axis_index("chan")
    x = t // 2
    place = t.reshape(1)
    stations, components, length = records.shape
    window = templates.shape[2]
    region = length // tm
    batch = 2 if stations % 2 == 0 else 1
    send, shifted, factor, banks = first_part(
        place, records.transpose(1, 0, 2), templates, moveouts.T, uptime.T, hops, batch)
    came = lax.ppermute(send, "tm", [(i, i ^ 1) for i in range(tm)])
    arriving = []
    if hops > 1:
        others = next_part(
            place, shifted, factor, banks, None, hops - 1, region, components, window, batch)
        for step in range(1, hops):
            piece = lax.dynamic_index_in_dim(came, (x + step) % hops, 0, keepdims=False)
            piece = (others[step - 1] + piece.astype(jnp.float32)).astype(jnp.bfloat16)
            perm = [(i, ((i // 2 + step) % hops) * 2 + i % 2) for i in range(tm)]
            arriving.append(lax.ppermute(piece, "tm", perm))
    result = next_part(
        place, shifted, factor, banks, came, 1, region, components, window, batch)[0]
    for piece in arriving:
        result = result + piece.astype(jnp.float32)
    mine = result.reshape(chan, result.shape[0] // chan, result.shape[1])
    result = lax.dynamic_index_in_dim(mine, z, 0, keepdims=False)
    for step in range(1, chan):
        block = lax.dynamic_index_in_dim(mine, (z + step) % chan, 0, keepdims=False)
        perm = [(i, (i + step) % chan) for i in range(chan)]
        result = result + lax.ppermute(block.astype(jnp.bfloat16), "chan", perm).astype(jnp.float32)
    return result.T


def solution(mesh):
    placed = (
        P(("grp", "tm", "chan"), None, None),
        P(("tm", "chan"), None, None, None),
        P(("tm", "chan"), None),
        P(("grp", "tm", "chan"), None),
    )
    return jax.shard_map(
        body, mesh=mesh, in_specs=placed, out_specs=P(None, ("grp", "tm", "chan")), check_vma=False
    )
```

```python
import functools

import jax
import jax.numpy as jnp
from jax import lax
from jax.experimental import pallas as pl
from jax.experimental.pallas import tpu as pltpu
from jax.sharding import PartitionSpec as P

MAXMO = 1000
LANES = 128
GROUP = 16


def up(value, unit):
    return -(-value // unit) * unit


def window_sum(values, window):
    def behind(array, by):
        return array if by == 0 else pltpu.roll(array, by, 1)

    total, offset, size, run = None, 0, 1, values
    while size <= window:
        if window & size:
            piece = behind(run, offset)
            total = piece if total is None else total + piece
            offset += size
        size *= 2
        if size <= window:
            run = run + behind(run, size // 2)
    return total


def correlate_kernel(
    core_ref, moveouts_ref, uptime_ref, records_ref, templates_ref,
    send_ref, keep_ref,
    masked, shifted, factor, loaded, bank, windows_a, windows_b, bank_a, bank_b, total, arrived,
    *, window,
):
    components, stations, length = records_ref.shape
    block_count = uptime_ref.shape[0]
    rows = masked.shape[0]
    groups = up(window, GROUP) // GROUP
    margin = up(window, LANES)
    block_len = length // block_count
    span = shifted.shape[1]
    lead = masked.shape[1] - length

    def fetch(i):
        return pltpu.make_async_copy(templates_ref.at[i], loaded.at[i], arrived.at[i])

    def start(i, carry):
        fetch(i).start()
        return carry

    lax.fori_loop(0, stations, start, 0)

    masked[:, :lead] = jnp.zeros((rows, lead), jnp.float32)
    shifted[...] = jnp.zeros(shifted.shape, jnp.float32)
    total[...] = jnp.zeros(total.shape, total.dtype)
    for ref in (bank, bank_a, bank_b, windows_b):
        ref[...] = jnp.zeros(ref.shape, ref.dtype)
    depth = components * groups * GROUP
    if windows_a.shape[0] > depth:
        windows_a[depth:, :] = jnp.zeros((windows_a.shape[0] - depth, length), windows_a.dtype)
    offsets = lax.broadcasted_iota(jnp.int32, (stations, LANES), 1)
    which = lax.broadcasted_iota(jnp.int32, (stations, LANES), 0)
    mirror = LANES - 1 - lax.broadcasted_iota(jnp.int32, (up(stations, 8), LANES), 1)

    def mask_tile(i, carry):
        at = pl.multiple_of(i * LANES, LANES)
        to = pl.multiple_of(lead + length - LANES - at, LANES)
        block = at // block_len
        limit = jnp.zeros((stations, LANES), jnp.int32)
        for s in range(stations):
            limit = jnp.where(which == s, uptime_ref[block, s], limit)
        live = offsets + (at - block * block_len) < limit
        for j in range(components):
            values = records_ref[j, :, pl.ds(at, LANES)].astype(jnp.float32)
            values = jnp.where(live, values, 0.0)
            if stations % 8:
                rest = jnp.zeros((up(stations, 8) - stations, LANES), jnp.float32)
                values = jnp.concatenate([values, rest], axis=0)
            values = jnp.take_along_axis(values, mirror, axis=1)
            masked[j * stations:(j + 1) * stations, pl.ds(to, LANES)] = values[:stations]
        return carry

    lax.fori_loop(0, length // LANES, mask_tile, 0)
    burst = 4 if stations % 4 == 0 else 1

    def shift_some(i, carry):
        shifts = []
        for u in range(burst):
            for j in range(components):
                c = j * stations + i * burst + u
                moveout = moveouts_ref[j, i * burst + u]
                whole = moveout // LANES * LANES
                base = pl.multiple_of(lead - margin - LANES - whole, LANES)
                row = masked[pl.ds(c, 1), pl.ds(base, span + LANES)]
                shifts.append((c, pltpu.roll(row, moveout - whole, 1)))
        for c, row in shifts:
            shifted[pl.ds(c, 1), :] = row[:, LANES:]
        return carry

    lax.fori_loop(0, stations // burst, shift_some, 0)
    chunk = rows // 2 if rows % 16 == 0 else 8

    def energy_some(i, carry):
        at = pl.ds(pl.multiple_of(i * chunk, 8), chunk)
        values = shifted[at, :]
        energy = window_sum(values * values, window)[:, margin:]
        factor[at, :] = lax.rsqrt(jnp.maximum(energy, 1.0))
        return carry

    lax.fori_loop(0, rows // chunk, energy_some, 0)
    width = min(2 * LANES, length)

    def multiply(n, windows, turned):
        total[:, n:n + width] += jnp.dot(
            turned[...], windows[:, n:n + width], preferred_element_type=jnp.float32)

    def build(i, windows, turned, pending):
        strips, scales = [], []
        for j in range(components):
            c = j * stations + i
            half = jnp.broadcast_to(shifted[pl.ds(c, 1), :], (8, span))
            strips.append(jnp.concatenate(
                [pltpu.roll(half, b, 1, stride=1, stride_axis=0) for b in (0, 8)], axis=0
            ).astype(jnp.bfloat16))
            scale = jnp.broadcast_to(factor[pl.ds(c, 1), :], (GROUP, length))
            scales.append(scale.astype(jnp.bfloat16))
        for j in range(components):
            values = loaded[i, j].astype(jnp.float32)
            squares = jnp.sum(values * values, axis=0, keepdims=True)
            unit = (values * lax.rsqrt(squares + 1e-06)).astype(jnp.bfloat16)
            at = j * groups * GROUP
            bank[at:at + window, :] = unit
        turned[...] = bank[...].T
        left = list(range(0, length, width))
        share = up(len(left), components) // components
        for j in range(components):
            for a in range(min(groups, LANES // GROUP)):
                rolled = strips[j] if a == 0 else pltpu.roll(strips[j], a * GROUP, 1)
                for g in range(a, groups, LANES // GROUP):
                    begin = margin - (g - a) * GROUP
                    at = (j * groups + g) * GROUP
                    windows[at:at + GROUP, :] = rolled[:, begin:begin + length] * scales[j]
            for n in left[:share]:
                multiply(n, *pending)
            left = left[share:]

    def two_stations(i, carry):
        station = jnp.minimum(2 * i, stations - 1)

        @pl.when(2 * i < stations)
        def _():
            fetch(2 * i).wait()

        build(station, windows_a, bank_a, (windows_b, bank_b))

        @pl.when(2 * i < stations)
        def _():
            later = jnp.minimum(2 * i + 1, stations - 1)

            @pl.when(2 * i + 1 < stations)
            def _():
                fetch(2 * i + 1).wait()

            build(later, windows_b, bank_b, (windows_a, bank_a))

        return carry

    lax.fori_loop(0, stations // 2 + 1, two_stations, 0)

    core = core_ref[0]
    hops, region = keep_ref.shape[0], keep_ref.shape[1]
    flip = LANES - 1 - lax.broadcasted_iota(jnp.int32, (LANES, LANES), 1)

    def ordered(begin, h):
        at = pl.multiple_of(length - LANES - begin, LANES)
        block = total[h:h + LANES, pl.ds(at, LANES)]
        return jnp.take_along_axis(block, flip, axis=1).T

    def write(i, carry):
        x = i // (region // LANES)
        r = pl.multiple_of(i % (region // LANES) * LANES, LANES)
        own = (2 * x + core) * region + r
        other = (2 * x + 1 - core) * region + r
        for h in range(0, total.shape[0], LANES):
            keep_ref[x, pl.ds(r, LANES), h:h + LANES] = ordered(own, h)
            send_ref[x, pl.ds(r, LANES), h:h + LANES] = ordered(other, h).astype(send_ref.dtype)
        return carry

    lax.fori_loop(0, hops * (region // LANES), write, 0)


def correlate(core, records, templates, moveouts, uptime, hops):
    components, stations, length = records.shape
    window, bank_size = templates.shape[2:]
    margin = up(window, LANES)
    rows = up(stations * components, 8)
    region = length // (2 * hops)
    depth = up(components * up(window, GROUP), LANES)
    scalars = pl.BlockSpec(memory_space=pltpu.SMEM)
    vectors = pl.BlockSpec(memory_space=pltpu.VMEM)
    return pl.pallas_call(
        functools.partial(correlate_kernel, window=window),
        in_specs=[scalars, scalars, scalars, vectors, pl.BlockSpec(memory_space=pl.ANY)],
        out_specs=[vectors, vectors],
        scratch_shapes=[
            pltpu.VMEM((rows, length + margin + LANES + up(MAXMO, LANES)), jnp.float32),
            pltpu.VMEM((rows, length + margin), jnp.float32),
            pltpu.VMEM((rows, length), jnp.float32),
            pltpu.VMEM(templates.shape, templates.dtype),
            pltpu.VMEM((depth, bank_size), jnp.bfloat16),
            pltpu.VMEM((depth, length), jnp.bfloat16),
            pltpu.VMEM((depth, length), jnp.bfloat16),
            pltpu.VMEM((bank_size, depth), jnp.bfloat16),
            pltpu.VMEM((bank_size, depth), jnp.bfloat16),
            pltpu.VMEM((bank_size, length), jnp.float32),
            pltpu.SemaphoreType.DMA((stations,)),
        ],
        out_shape=[
            jax.ShapeDtypeStruct((hops, region, bank_size), jnp.bfloat16),
            jax.ShapeDtypeStruct((hops, region, bank_size), jnp.float32),
        ],
        compiler_params=pltpu.CompilerParams(vmem_limit_bytes=52 * 2**20),
        name="correlate",
    )(core, moveouts, uptime, records, templates)


def body(records, templates, moveouts, uptime):
    tm, chan = lax.axis_size("tm"), lax.axis_size("chan")
    hops = tm // 2
    t, z = lax.axis_index("tm"), lax.axis_index("chan")
    x, core = t // 2, t % 2
    send, keep = correlate(
        core.reshape(1), records.transpose(1, 0, 2), templates, moveouts.T, uptime.T, hops
    )
    got = lax.ppermute(send, "tm", [(i, i ^ 1) for i in range(tm)])
    mine = keep + got.astype(jnp.float32)
    result = lax.dynamic_index_in_dim(mine, x, 0, keepdims=False)
    for step in range(1, hops):
        block = lax.dynamic_index_in_dim(mine, (x + step) % hops, 0, keepdims=False)
        perm = [(i, ((i // 2 + step) % hops) * 2 + i % 2) for i in range(tm)]
        result = result + lax.ppermute(block.astype(jnp.bfloat16), "tm", perm).astype(jnp.float32)
    mine = result.reshape(chan, result.shape[0] // chan, result.shape[1])
    result = lax.dynamic_index_in_dim(mine, z, 0, keepdims=False)
    for step in range(1, chan):
        block = lax.dynamic_index_in_dim(mine, (z + step) % chan, 0, keepdims=False)
        perm = [(i, (i + step) % chan) for i in range(chan)]
        result = result + lax.ppermute(block.astype(jnp.bfloat16), "chan", perm).astype(jnp.float32)
    return result.T


def solution(mesh):
    placed = (
        P(("grp", "tm", "chan"), None, None),
        P(("tm", "chan"), None, None, None),
        P(("tm", "chan"), None),
        P(("grp", "tm", "chan"), None),
    )
    return jax.shard_map(
        body, mesh=mesh, in_specs=placed, out_specs=P(None, ("grp", "tm", "chan")), check_vma=False
    )
```

```python
import functools

import jax
import jax.numpy as jnp
from jax import lax
from jax.experimental import pallas as pl
from jax.experimental.pallas import tpu as pltpu
from jax.sharding import PartitionSpec as P

MAXMO = 1000
LANES = 128
GROUP = 16


def up(value, unit):
    return -(-value // unit) * unit


def window_sum(values, window):
    def behind(array, by):
        return array if by == 0 else pltpu.roll(array, by, 1)

    total, offset, size, run = None, 0, 1, values
    while size <= window:
        if window & size:
            piece = behind(run, offset)
            total = piece if total is None else total + piece
            offset += size
        size *= 2
        if size <= window:
            run = run + behind(run, size // 2)
    return total


def mirrored(array, region, size):
    return pl.multiple_of(array - (region + 1) * size, LANES)


def read_rows(shifted, factor, channels, begins, size, margin):
    rows = []
    for channel in channels:
        for begin in begins:
            rows.append((
                jnp.broadcast_to(
                    shifted[pl.ds(channel, 1), pl.ds(begin, size + margin)], (8, size + margin)),
                jnp.broadcast_to(factor[pl.ds(channel, 1), pl.ds(begin, size)], (GROUP, size)),
            ))
    return rows


def build_windows(rows, windows, bases, regions, size, groups, margin):
    for m, (half, scale) in enumerate(rows):
        base, n = bases[m // regions], m % regions
        strip = jnp.concatenate(
            [pltpu.roll(half, b, 1, stride=1, stride_axis=0) for b in (0, 8)], axis=0
        ).astype(jnp.bfloat16)
        scale = scale.astype(jnp.bfloat16)
        for a in range(min(groups, LANES // GROUP)):
            deepest = list(range(a, groups, LANES // GROUP))[-1]
            first = margin - (deepest - a) * GROUP
            cut = max(first - LANES, 0)
            rolled = strip[:, cut:]
            rolled = rolled if a == 0 else pltpu.roll(rolled, a * GROUP, 1)
            for g in range(a, groups, LANES // GROUP):
                lane = margin - (g - a) * GROUP - cut
                windows[base + g * GROUP:base + (g + 1) * GROUP, n * size:(n + 1) * size] = (
                    rolled[:, lane:lane + size] * scale)


def multiply(total, windows, banks, width):
    for n in range(0, total.shape[1], width):
        result = total[:, n:n + width]
        for k, bank in enumerate(banks):
            depth = bank.shape[1]
            result += jnp.dot(
                bank[...], windows[k * depth:(k + 1) * depth, n:n + width],
                preferred_element_type=jnp.float32)
        total[:, n:n + width] = result


def in_order(total, at, h):
    flip = LANES - 1 - lax.broadcasted_iota(jnp.int32, (LANES, LANES), 1)
    return jnp.take_along_axis(total[h:h + LANES, at:at + LANES], flip, axis=1).T


def write_regions(total, out_ref, extra=None):
    count, size, bank_size = out_ref.shape
    for n in range(count):
        for r in range(0, size, LANES):
            for h in range(0, bank_size, LANES):
                block = in_order(total, n * size + size - LANES - r, h)
                if extra is not None:
                    block = block + extra(r, h)
                out_ref[n, r:r + LANES, h:h + LANES] = block.astype(out_ref.dtype)


def first_kernel(
    place_ref, moveouts_ref, uptime_ref, records_ref, templates_ref,
    send_ref, shifted, factor, banks_ref,
    masked, loaded_a, loaded_b, bank, windows_a, windows_b, bank_a, bank_b, total, arrived, stored,
    *, window, batch,
):
    components, stations, length = records_ref.shape
    block_count = uptime_ref.shape[0]
    batches = stations // batch
    rows = masked.shape[0]
    groups = up(window, GROUP) // GROUP
    margin = up(window, LANES)
    block_len = length // block_count
    span = shifted.shape[1]
    lead = masked.shape[1] - length

    def fetch(i, which):
        return pltpu.make_async_copy(
            templates_ref.at[pl.ds(i * batch, batch)], (loaded_a, loaded_b)[which], arrived.at[which])

    for i in range(min(batches, 2)):
        fetch(i, i).start()

    masked[...] = jnp.zeros(masked.shape, jnp.float32)
    offsets = lax.broadcasted_iota(jnp.int32, (stations, LANES), 1)
    which = lax.broadcasted_iota(jnp.int32, (stations, LANES), 0)
    for b in range(block_count):
        limit = jnp.zeros((stations, LANES), jnp.int32)
        for s in range(stations):
            limit = jnp.where(which == s, uptime_ref[b, s], limit)
        for i in range(block_len // LANES):
            at = b * block_len + i * LANES
            live = offsets + i * LANES < limit
            for j in range(components):
                values = records_ref[j, :, at:at + LANES].astype(jnp.float32)
                factor[j * stations:(j + 1) * stations, at:at + LANES] = jnp.where(live, values, 0.0)
    mirror = LANES - 1 - lax.broadcasted_iota(jnp.int32, (8, LANES), 1)
    for g in range(0, rows, 8):
        for at in range(0, length, LANES):
            to = lead + length - LANES - at
            masked[g:g + 8, to:to + LANES] = jnp.take_along_axis(
                factor[g:g + 8, at:at + LANES], mirror, axis=1)
    shifted[...] = jnp.zeros(shifted.shape, jnp.float32)
    for j in range(components):
        for s in range(stations):
            c = j * stations + s
            moveout = moveouts_ref[j, s]
            whole = moveout // LANES * LANES
            base = pl.multiple_of(lead - margin - LANES - whole, LANES)
            row = masked[c:c + 1, pl.ds(base, span + LANES)]
            row = pltpu.roll(row, moveout - whole, 1)
            shifted[c:c + 1, :] = row[:, LANES:]
    for g in range(0, rows, 8):
        values = shifted[g:g + 8, :]
        energy = window_sum(values * values, window)[:, margin:]
        factor[g:g + 8, :] = lax.rsqrt(jnp.maximum(energy, 1.0))
    bank[...] = jnp.zeros(bank.shape, bank.dtype)
    total[...] = jnp.zeros(total.shape, total.dtype)
    depth = batch * components * groups * GROUP
    for windows in (windows_a, windows_b):
        if windows.shape[0] > depth:
            windows[depth:, :] = jnp.zeros((windows.shape[0] - depth, windows.shape[1]), windows.dtype)

    count, size = send_ref.shape[:2]
    core = place_ref[0] % 2
    begins = [mirrored(length, 2 * x + 1 - core, size) for x in range(count)]
    width = min(2 * LANES, size)

    def store(i, turned, which):
        return pltpu.make_async_copy(turned, banks_ref.at[i], stored.at[which])

    bases = [m * groups * GROUP for m in range(batch * components)]

    def build(i, windows, turned, which):
        fetch(i, which).wait()
        loaded = (loaded_a, loaded_b)[which]
        rows = read_rows(
            shifted, factor,
            [j * stations + i * batch + u for u in range(batch) for j in range(components)],
            begins, size, margin)
        for u in range(batch):
            for j in range(components):
                values = loaded[u, j].astype(jnp.float32)
                squares = jnp.sum(values * values, axis=0, keepdims=True)
                unit = (values * lax.rsqrt(squares + 1e-06)).astype(jnp.bfloat16)
                at = bases[u * components + j]
                bank[at:at + window, :] = unit
        turned[...] = bank[...].T
        build_windows(rows, windows, bases, count, size, groups, margin)

    def pass_on(i, turned, which, more):
        store(i, turned, which).start()
        if more is True:
            fetch(i + 2, which).start()
        elif more is not False:
            @pl.when(more)
            def _():
                fetch(i + 2, which).start()

    build(0, windows_a, bank_a, 0)
    pass_on(0, bank_a, 0, batches > 2)

    def two_batches(i, carry):
        @pl.when(i > 0)
        def _():
            store(2 * i - 1, bank_b, 1).wait()
        build(2 * i + 1, windows_b, bank_b, 1)
        multiply(total, windows_a, [bank_a], width)
        pass_on(2 * i + 1, bank_b, 1, 2 * i + 3 < batches)
        store(2 * i, bank_a, 0).wait()
        build(2 * i + 2, windows_a, bank_a, 0)
        multiply(total, windows_b, [bank_b], width)
        pass_on(2 * i + 2, bank_a, 0, 2 * i + 4 < batches)
        return carry

    if batches > 2:
        lax.fori_loop(0, (batches - 1) // 2, two_batches, 0)
    if batches % 2 == 0:
        if batches > 2:
            store(batches - 3, bank_b, 1).wait()
        build(batches - 1, windows_b, bank_b, 1)
        multiply(total, windows_a, [bank_a], width)
        pass_on(batches - 1, bank_b, 1, False)
        multiply(total, windows_b, [bank_b], width)
        store(batches - 2, bank_a, 0).wait()
        store(batches - 1, bank_b, 1).wait()
    else:
        multiply(total, windows_a, [bank_a], width)
        store(batches - 1, bank_a, 0).wait()
        if batches > 1:
            store(batches - 2, bank_b, 1).wait()
    write_regions(total, send_ref)


def next_kernel(
    place_ref, shifted, factor, banks_ref, *refs,
    components, window, batch, own, phases,
):
    if own:
        came_ref, *refs = refs
    out_ref, loaded, windows_a, windows_b, total, arrived = refs
    length = factor.shape[1]
    batches = banks_ref.shape[0]
    slabs = batches // phases
    stations = batches * batch
    groups = up(window, GROUP) // GROUP
    margin = up(window, LANES)
    count, size = out_ref.shape[:2]
    slab = loaded.shape[2]

    def fetch(i):
        return pltpu.make_async_copy(banks_ref.at[i], loaded.at[i], arrived.at[i])

    for i in range(batches):
        fetch(i).start()
    total[...] = jnp.zeros(total.shape, total.dtype)
    depth = batch * components * groups * GROUP
    for windows in (windows_a, windows_b):
        for k in range(slabs):
            if slab > depth:
                windows[k * slab + depth:(k + 1) * slab, :] = jnp.zeros(
                    (slab - depth, windows.shape[1]), windows.dtype)
    core, x = place_ref[0] % 2, place_ref[0] // 2
    hops = length // (2 * size)
    if own:
        begins = [mirrored(length, 2 * x + core, size)]
    else:
        begins = [mirrored(length, 2 * ((x + n) % hops) + core, size) for n in range(1, hops)]
    width = min(2 * LANES, size)

    places = [(k, u, j) for k in range(slabs) for u in range(batch) for j in range(components)]
    bases = [k * slab + (u * components + j) * groups * GROUP for k, u, j in places]

    def read(p):
        return read_rows(
            shifted, factor, [j * stations + (p * slabs + k) * batch + u for k, u, j in places],
            begins, size, margin)

    build_windows(read(0), windows_a, bases, len(begins), size, groups, margin)
    for p in range(phases):
        now, later = (windows_a, windows_b) if p % 2 == 0 else (windows_b, windows_a)
        for k in range(slabs):
            fetch(p * slabs + k).wait()
        if p + 1 < phases:
            build_windows(read(p + 1), later, bases, len(begins), size, groups, margin)
        multiply(total, now, [loaded.at[p * slabs + k] for k in range(slabs)], width)
    if own:
        write_regions(total, out_ref, lambda r, h: came_ref[
            x, r:r + LANES, h:h + LANES].astype(jnp.float32))
    else:
        write_regions(total, out_ref)


SCALARS = pl.BlockSpec(memory_space=pltpu.SMEM)
VECTORS = pl.BlockSpec(memory_space=pltpu.VMEM)
FAR = pl.BlockSpec(memory_space=pl.ANY)


def cost(stations, components, window, bank_size, samples, read):
    return pl.CostEstimate(
        flops=2 * stations * components * window * bank_size * samples,
        bytes_accessed=read, transcendentals=0)


def first_part(place, records, templates, moveouts, uptime, hops, batch):
    components, stations, length = records.shape
    window, bank_size = templates.shape[2:]
    margin = up(window, LANES)
    rows = up(stations * components, 8)
    region = length // (2 * hops)
    depth = up(batch * components * up(window, GROUP), LANES)
    return pl.pallas_call(
        functools.partial(first_kernel, window=window, batch=batch),
        in_specs=[SCALARS, SCALARS, SCALARS, VECTORS, FAR],
        out_specs=[VECTORS, VECTORS, VECTORS, FAR],
        scratch_shapes=[
            pltpu.VMEM((rows, length + margin + LANES + up(MAXMO, LANES)), jnp.float32),
            pltpu.VMEM((batch,) + templates.shape[1:], templates.dtype),
            pltpu.VMEM((batch,) + templates.shape[1:], templates.dtype),
            pltpu.VMEM((depth, bank_size), jnp.bfloat16),
            pltpu.VMEM((depth, hops * region), jnp.bfloat16),
            pltpu.VMEM((depth, hops * region), jnp.bfloat16),
            pltpu.VMEM((bank_size, depth), jnp.bfloat16),
            pltpu.VMEM((bank_size, depth), jnp.bfloat16),
            pltpu.VMEM((bank_size, hops * region), jnp.float32),
            pltpu.SemaphoreType.DMA((2,)),
            pltpu.SemaphoreType.DMA((2,)),
        ],
        out_shape=[
            jax.ShapeDtypeStruct((hops, region, bank_size), jnp.bfloat16),
            jax.ShapeDtypeStruct((rows, length + margin), jnp.float32),
            jax.ShapeDtypeStruct((rows, length), jnp.float32),
            jax.ShapeDtypeStruct((stations // batch, bank_size, depth), jnp.bfloat16),
        ],
        compiler_params=pltpu.CompilerParams(vmem_limit_bytes=60 * 2**20),
        cost_estimate=cost(stations, components, window, bank_size, hops * region,
                           2 * templates.size * 2),
        name="other_core",
    )(place, moveouts, uptime, records, templates)


def next_part(place, shifted, factor, banks, came, count, region, components, window, batch):
    batches, bank_size, depth = banks.shape
    phases = batches // 2 if batches % 2 == 0 else batches
    slabs = batches // phases
    own = came is not None
    return pl.pallas_call(
        functools.partial(next_kernel, components=components, window=window, batch=batch,
                          own=own, phases=phases),
        in_specs=[SCALARS, VECTORS, VECTORS, FAR] + [VECTORS] * own,
        out_specs=VECTORS,
        scratch_shapes=[
            pltpu.VMEM(banks.shape, banks.dtype),
            pltpu.VMEM((slabs * depth, count * region), jnp.bfloat16),
            pltpu.VMEM((slabs * depth, count * region), jnp.bfloat16),
            pltpu.VMEM((bank_size, count * region), jnp.float32),
            pltpu.SemaphoreType.DMA((batches,)),
        ],
        out_shape=jax.ShapeDtypeStruct((count, region, bank_size), jnp.float32),
        compiler_params=pltpu.CompilerParams(vmem_limit_bytes=60 * 2**20),
        cost_estimate=cost(batches * batch, components, window, bank_size, count * region,
                           banks.size * 2),
        name="own_region" if own else "other_chips",
    )(place, shifted, factor, banks, *([came] if own else []))


def body(records, templates, moveouts, uptime):
    tm, chan = lax.axis_size("tm"), lax.axis_size("chan")
    hops = tm // 2
    t, z = lax.axis_index("tm"), lax.axis_index("chan")
    x = t // 2
    place = t.reshape(1)
    stations, components, length = records.shape
    window = templates.shape[2]
    region = length // tm
    batch = 2 if stations % 2 == 0 else 1
    send, shifted, factor, banks = first_part(
        place, records.transpose(1, 0, 2), templates, moveouts.T, uptime.T, hops, batch)
    came = lax.ppermute(send, "tm", [(i, i ^ 1) for i in range(tm)])
    arriving = []
    if hops > 1:
        others = next_part(
            place, shifted, factor, banks, None, hops - 1, region, components, window, batch)
        for step in range(1, hops):
            piece = lax.dynamic_index_in_dim(came, (x + step) % hops, 0, keepdims=False)
            piece = (others[step - 1] + piece.astype(jnp.float32)).astype(jnp.bfloat16)
            perm = [(i, ((i // 2 + step) % hops) * 2 + i % 2) for i in range(tm)]
            arriving.append(lax.ppermute(piece, "tm", perm))
    result = next_part(
        place, shifted, factor, banks, came, 1, region, components, window, batch)[0]
    for piece in arriving:
        result = result + piece.astype(jnp.float32)
    mine = result.reshape(chan, result.shape[0] // chan, result.shape[1])
    result = lax.dynamic_index_in_dim(mine, z, 0, keepdims=False)
    for step in range(1, chan):
        block = lax.dynamic_index_in_dim(mine, (z + step) % chan, 0, keepdims=False)
        perm = [(i, (i + step) % chan) for i in range(chan)]
        result = result + lax.ppermute(block.astype(jnp.bfloat16), "chan", perm).astype(jnp.float32)
    return result.T


def solution(mesh):
    placed = (
        P(("grp", "tm", "chan"), None, None),
        P(("tm", "chan"), None, None, None),
        P(("tm", "chan"), None),
        P(("grp", "tm", "chan"), None),
    )
    return jax.shard_map(
        body, mesh=mesh, in_specs=placed, out_specs=P(None, ("grp", "tm", "chan")), check_vma=False
    )
```

```python
import functools

import jax
import jax.numpy as jnp
from jax import lax
from jax.experimental import pallas as pl
from jax.experimental.pallas import tpu as pltpu
from jax.sharding import PartitionSpec as P

MAXMO = 1000
LANES = 128
GROUP = 16


def up(value, unit):
    return -(-value // unit) * unit


def window_sum(values, window):
    def behind(array, by):
        return array if by == 0 else pltpu.roll(array, by, 1)

    total, offset, size, run = None, 0, 1, values
    while size <= window:
        if window & size:
            piece = behind(run, offset)
            total = piece if total is None else total + piece
            offset += size
        size *= 2
        if size <= window:
            run = run + behind(run, size // 2)
    return total


def correlate_kernel(
    place_ref, moveouts_ref, uptime_ref, records_ref, templates_ref, *refs, window,
):
    *out_refs, masked, shifted, factor, loaded, bank, windows_a, windows_b, bank_a, bank_b, total, arrived = refs
    components, stations, length = records_ref.shape
    block_count = uptime_ref.shape[0]
    rows = masked.shape[0]
    groups = up(window, GROUP) // GROUP
    margin = up(window, LANES)
    block_len = length // block_count
    span = shifted.shape[1]
    lead = masked.shape[1] - length

    def fetch(i):
        return pltpu.make_async_copy(templates_ref.at[i], loaded.at[i], arrived.at[i])

    def start(i, carry):
        fetch(i).start()
        return carry

    lax.fori_loop(0, stations, start, 0)

    masked[:, :lead] = jnp.zeros((rows, lead), jnp.float32)
    shifted[...] = jnp.zeros(shifted.shape, jnp.float32)
    total[...] = jnp.zeros(total.shape, total.dtype)
    for ref in (bank, bank_a, bank_b, windows_b):
        ref[...] = jnp.zeros(ref.shape, ref.dtype)
    depth = components * groups * GROUP
    if windows_a.shape[0] > depth:
        windows_a[depth:, :] = jnp.zeros((windows_a.shape[0] - depth, length), windows_a.dtype)
    offsets = lax.broadcasted_iota(jnp.int32, (stations, LANES), 1)
    which = lax.broadcasted_iota(jnp.int32, (stations, LANES), 0)
    mirror = LANES - 1 - lax.broadcasted_iota(jnp.int32, (up(stations, 8), LANES), 1)

    def mask_tile(i, carry):
        at = pl.multiple_of(i * LANES, LANES)
        to = pl.multiple_of(lead + length - LANES - at, LANES)
        block = at // block_len
        limit = jnp.zeros((stations, LANES), jnp.int32)
        for s in range(stations):
            limit = jnp.where(which == s, uptime_ref[block, s], limit)
        live = offsets + (at - block * block_len) < limit
        for j in range(components):
            values = records_ref[j, :, pl.ds(at, LANES)].astype(jnp.float32)
            values = jnp.where(live, values, 0.0)
            if stations % 8:
                rest = jnp.zeros((up(stations, 8) - stations, LANES), jnp.float32)
                values = jnp.concatenate([values, rest], axis=0)
            values = jnp.take_along_axis(values, mirror, axis=1)
            masked[j * stations:(j + 1) * stations, pl.ds(to, LANES)] = values[:stations]
        return carry

    lax.fori_loop(0, length // LANES, mask_tile, 0, unroll=length // LANES <= 8)
    burst = stations

    def shift_some(i, carry):
        shifts = []
        for u in range(burst):
            for j in range(components):
                c = j * stations + i * burst + u
                moveout = moveouts_ref[j, i * burst + u]
                whole = moveout // LANES * LANES
                base = pl.multiple_of(lead - margin - LANES - whole, LANES)
                row = masked[pl.ds(c, 1), pl.ds(base, span + LANES)]
                shifts.append((c, pltpu.roll(row, moveout - whole, 1)))
        for c, row in shifts:
            shifted[pl.ds(c, 1), :] = row[:, LANES:]
        return carry

    lax.fori_loop(0, stations // burst, shift_some, 0)
    chunk = rows

    def energy_some(i, carry):
        at = pl.ds(pl.multiple_of(i * chunk, 8), chunk)
        values = shifted[at, :]
        energy = window_sum(values * values, window)[:, margin:]
        factor[at, :] = lax.rsqrt(jnp.maximum(energy, 1.0))
        return carry

    lax.fori_loop(0, rows // chunk, energy_some, 0)
    width = min(2 * LANES, length)

    def multiply(n, windows, turned):
        total[:, n:n + width] += jnp.dot(
            turned[...], windows[:, n:n + width], preferred_element_type=jnp.float32)

    def build(i, windows, turned, pending):
        strips, scales = [], []
        for j in range(components):
            c = j * stations + i
            half = jnp.broadcast_to(shifted[pl.ds(c, 1), :], (8, span))
            strips.append(jnp.concatenate(
                [pltpu.roll(half, b, 1, stride=1, stride_axis=0) for b in (0, 8)], axis=0
            ).astype(jnp.bfloat16))
            scale = jnp.broadcast_to(factor[pl.ds(c, 1), :], (GROUP, length))
            scales.append(scale.astype(jnp.bfloat16))
        for j in range(components):
            values = loaded[i, j].astype(jnp.float32)
            squares = jnp.sum(values * values, axis=0, keepdims=True)
            unit = (values * lax.rsqrt(squares + 1e-06)).astype(jnp.bfloat16)
            at = j * groups * GROUP
            bank[at:at + window, :] = unit
        turned[...] = bank[...].T
        left = list(range(0, length, width))
        share = up(len(left), components) // components
        for j in range(components):
            for a in range(min(groups, LANES // GROUP)):
                rolled = strips[j] if a == 0 else pltpu.roll(strips[j], a * GROUP, 1)
                for g in range(a, groups, LANES // GROUP):
                    begin = margin - (g - a) * GROUP
                    at = (j * groups + g) * GROUP
                    windows[at:at + GROUP, :] = rolled[:, begin:begin + length] * scales[j]
            for n in left[:share]:
                multiply(n, *pending)
            left = left[share:]

    def two_stations(i, carry):
        station = jnp.minimum(2 * i, stations - 1)

        @pl.when(2 * i < stations)
        def _():
            fetch(2 * i).wait()

        build(station, windows_a, bank_a, (windows_b, bank_b))

        @pl.when(2 * i < stations)
        def _():
            later = jnp.minimum(2 * i + 1, stations - 1)

            @pl.when(2 * i + 1 < stations)
            def _():
                fetch(2 * i + 1).wait()

            build(later, windows_b, bank_b, (windows_a, bank_a))

        return carry

    lax.fori_loop(0, stations // 2 + 1, two_stations, 0)

    size = out_refs[0].shape[0]
    flip = LANES - 1 - lax.broadcasted_iota(jnp.int32, (LANES, LANES), 1)
    for step, out_ref in enumerate(out_refs, 1):
        region = partner(place_ref[0], step % len(out_refs), len(out_refs))
        for r in range(0, size, LANES):
            at = pl.multiple_of(length - LANES - region * size - r, LANES)
            for h in range(0, total.shape[0], LANES):
                block = total[h:h + LANES, pl.ds(at, LANES)]
                block = jnp.take_along_axis(block, flip, axis=1).T
                out_ref[r:r + LANES, h:h + LANES] = block.astype(out_ref.dtype)


def partner(place, step, count):
    return place ^ step if count & (count - 1) == 0 else (place + step) % count


def correlate(place, records, templates, moveouts, uptime, count):
    components, stations, length = records.shape
    window, bank_size = templates.shape[2:]
    margin = up(window, LANES)
    rows = up(stations * components, 8)
    region = length // count
    depth = up(components * up(window, GROUP), LANES)
    scalars = pl.BlockSpec(memory_space=pltpu.SMEM)
    vectors = pl.BlockSpec(memory_space=pltpu.VMEM)
    return pl.pallas_call(
        functools.partial(correlate_kernel, window=window),
        in_specs=[scalars, scalars, scalars, vectors, pl.BlockSpec(memory_space=pl.ANY)],
        out_specs=[vectors] * count,
        scratch_shapes=[
            pltpu.VMEM((rows, length + margin + LANES + up(MAXMO, LANES)), jnp.float32),
            pltpu.VMEM((rows, length + margin), jnp.float32),
            pltpu.VMEM((rows, length), jnp.float32),
            pltpu.VMEM(templates.shape, templates.dtype),
            pltpu.VMEM((depth, bank_size), jnp.bfloat16),
            pltpu.VMEM((depth, length), jnp.bfloat16),
            pltpu.VMEM((depth, length), jnp.bfloat16),
            pltpu.VMEM((bank_size, depth), jnp.bfloat16),
            pltpu.VMEM((bank_size, depth), jnp.bfloat16),
            pltpu.VMEM((bank_size, length), jnp.float32),
            pltpu.SemaphoreType.DMA((stations,)),
        ],
        out_shape=[jax.ShapeDtypeStruct((region, bank_size), jnp.bfloat16)] * (count - 1)
        + [jax.ShapeDtypeStruct((region, bank_size), jnp.float32)],
        compiler_params=pltpu.CompilerParams(vmem_limit_bytes=58 * 2**20),
        name="correlate",
    )(place, moveouts, uptime, records, templates)


def body(records, templates, moveouts, uptime):
    tm, chan = lax.axis_size("tm"), lax.axis_size("chan")
    t, z = lax.axis_index("tm"), lax.axis_index("chan")
    *sent, result = correlate(
        t.reshape(1), records.transpose(1, 0, 2), templates, moveouts.T, uptime.T, tm
    )
    for step in range(tm - 1, 0, -1):
        perm = [(i, partner(i, step, tm)) for i in range(tm)]
        result = result + lax.ppermute(sent[step - 1], "tm", perm).astype(jnp.float32)
    mine = result.reshape(chan, result.shape[0] // chan, result.shape[1])
    result = lax.dynamic_index_in_dim(mine, z, 0, keepdims=False)
    for step in range(1, chan):
        block = lax.dynamic_index_in_dim(mine, (z + step) % chan, 0, keepdims=False)
        perm = [(i, (i + step) % chan) for i in range(chan)]
        result = result + lax.ppermute(block.astype(jnp.bfloat16), "chan", perm).astype(jnp.float32)
    return result.T


def solution(mesh):
    placed = (
        P(("grp", "tm", "chan"), None, None),
        P(("tm", "chan"), None, None, None),
        P(("tm", "chan"), None),
        P(("grp", "tm", "chan"), None),
    )
    return jax.shard_map(
        body, mesh=mesh, in_specs=placed, out_specs=P(None, ("grp", "tm", "chan")), check_vma=False
    )
```

```python
import functools

import jax
import jax.numpy as jnp
from jax import lax
from jax.experimental import pallas as pl
from jax.experimental.pallas import tpu as pltpu
from jax.sharding import PartitionSpec as P

MAXMO = 1000
LANES = 128
GROUP = 16


def up(value, unit):
    return -(-value // unit) * unit


def window_sum(values, window):
    def behind(array, by):
        return array if by == 0 else pltpu.roll(array, by, 1)

    total, offset, size, run = None, 0, 1, values
    while size <= window:
        if window & size:
            piece = behind(run, offset)
            total = piece if total is None else total + piece
            offset += size
        size *= 2
        if size <= window:
            run = run + behind(run, size // 2)
    return total


def correlate_kernel(
    place_ref, moveouts_ref, uptime_ref, records_ref, templates_ref, *refs, window,
):
    *out_refs, masked, shifted, factor, loaded, unit_matrix, bank, windows_a, windows_b, bank_a, bank_b, total, arrived = refs
    components, stations, length = records_ref.shape
    block_count = uptime_ref.shape[0]
    rows = masked.shape[0]
    groups = up(window, GROUP) // GROUP
    margin = up(window, LANES)
    block_len = length // block_count
    span = shifted.shape[1]
    lead = masked.shape[1] - length

    def fetch(i):
        return pltpu.make_async_copy(templates_ref.at[i], loaded.at[i], arrived.at[i])

    def start(i, carry):
        fetch(i).start()
        return carry

    lax.fori_loop(0, stations, start, 0)

    masked[:, :lead] = jnp.zeros((rows, lead), jnp.float32)
    shifted[...] = jnp.zeros(shifted.shape, jnp.float32)
    total[...] = jnp.zeros(total.shape, total.dtype)
    for ref in (bank, bank_a, bank_b, windows_b):
        ref[...] = jnp.zeros(ref.shape, ref.dtype)
    across = lax.broadcasted_iota(jnp.int32, unit_matrix.shape, 1)
    down = lax.broadcasted_iota(jnp.int32, unit_matrix.shape, 0)
    unit_matrix[...] = jnp.where(across == down, 1.0, 0.0).astype(unit_matrix.dtype)
    depth = components * groups * GROUP
    if windows_a.shape[0] > depth:
        windows_a[depth:, :] = jnp.zeros((windows_a.shape[0] - depth, length), windows_a.dtype)
    offsets = lax.broadcasted_iota(jnp.int32, (stations, LANES), 1)
    which = lax.broadcasted_iota(jnp.int32, (stations, LANES), 0)
    mirror = LANES - 1 - lax.broadcasted_iota(jnp.int32, (up(stations, 8), LANES), 1)

    def mask_tile(i, carry):
        at = pl.multiple_of(i * LANES, LANES)
        to = pl.multiple_of(lead + length - LANES - at, LANES)
        block = at // block_len
        limit = jnp.zeros((stations, LANES), jnp.int32)
        for s in range(stations):
            limit = jnp.where(which == s, uptime_ref[block, s], limit)
        live = offsets + (at - block * block_len) < limit
        for j in range(components):
            values = records_ref[j, :, pl.ds(at, LANES)].astype(jnp.float32)
            values = jnp.where(live, values, 0.0)
            if stations % 8:
                rest = jnp.zeros((up(stations, 8) - stations, LANES), jnp.float32)
                values = jnp.concatenate([values, rest], axis=0)
            values = jnp.take_along_axis(values, mirror, axis=1)
            masked[j * stations:(j + 1) * stations, pl.ds(to, LANES)] = values[:stations]
        return carry

    lax.fori_loop(0, length // LANES, mask_tile, 0, unroll=length // LANES <= 8)
    burst = stations

    def shift_some(i, carry):
        shifts = []
        for u in range(burst):
            for j in range(components):
                c = j * stations + i * burst + u
                moveout = moveouts_ref[j, i * burst + u]
                whole = moveout // LANES * LANES
                base = pl.multiple_of(lead - margin - LANES - whole, LANES)
                row = masked[pl.ds(c, 1), pl.ds(base, span + LANES)]
                shifts.append((c, pltpu.roll(row, moveout - whole, 1)))
        for c, row in shifts:
            shifted[pl.ds(c, 1), :] = row[:, LANES:]
        return carry

    lax.fori_loop(0, stations // burst, shift_some, 0)
    chunk = rows

    def energy_some(i, carry):
        at = pl.ds(pl.multiple_of(i * chunk, 8), chunk)
        values = shifted[at, :]
        energy = window_sum(values * values, window)[:, margin:]
        factor[at, :] = lax.rsqrt(jnp.maximum(energy, 1.0))
        return carry

    lax.fori_loop(0, rows // chunk, energy_some, 0)
    width = min(2 * LANES, length)

    def multiply(n, windows, turned):
        total[:, n:n + width] += jnp.dot(
            turned[...], windows[:, n:n + width], preferred_element_type=jnp.float32)

    def build(i, windows, turned, pending):
        strips, scales = [], []
        for j in range(components):
            c = j * stations + i
            half = jnp.broadcast_to(shifted[pl.ds(c, 1), :], (8, span))
            strips.append(jnp.concatenate(
                [pltpu.roll(half, b, 1, stride=1, stride_axis=0) for b in (0, 8)], axis=0
            ).astype(jnp.bfloat16))
            scale = jnp.broadcast_to(factor[pl.ds(c, 1), :], (GROUP, length))
            scales.append(scale.astype(jnp.bfloat16))
        for j in range(components):
            values = loaded[i, j].astype(jnp.float32)
            squares = jnp.sum(values * values, axis=0, keepdims=True)
            unit = (values * lax.rsqrt(squares + 1e-06)).astype(jnp.bfloat16)
            at = j * groups * GROUP
            bank[at:at + window, :] = unit
        turned[...] = lax.dot_general(
            unit_matrix[...], bank[...], (((1,), (1,)), ((), ())),
            preferred_element_type=jnp.float32).astype(turned.dtype)
        left = list(range(0, length, width))
        share = up(len(left), components) // components
        for j in range(components):
            for a in range(min(groups, LANES // GROUP)):
                rolled = strips[j] if a == 0 else pltpu.roll(strips[j], a * GROUP, 1)
                for g in range(a, groups, LANES // GROUP):
                    begin = margin - (g - a) * GROUP
                    at = (j * groups + g) * GROUP
                    windows[at:at + GROUP, :] = rolled[:, begin:begin + length] * scales[j]
            for n in left[:share]:
                multiply(n, *pending)
            left = left[share:]

    def two_stations(i, carry):
        station = jnp.minimum(2 * i, stations - 1)

        @pl.when(2 * i < stations)
        def _():
            fetch(2 * i).wait()

        build(station, windows_a, bank_a, (windows_b, bank_b))

        @pl.when(2 * i < stations)
        def _():
            later = jnp.minimum(2 * i + 1, stations - 1)

            @pl.when(2 * i + 1 < stations)
            def _():
                fetch(2 * i + 1).wait()

            build(later, windows_b, bank_b, (windows_a, bank_a))

        return carry

    lax.fori_loop(0, stations // 2 + 1, two_stations, 0)

    send_far, send_near, keep_far, keep_near = out_refs
    size = send_near.shape[1]
    hops = length // (2 * size)
    core, x = place_ref[0] % 2, place_ref[0] // 2
    flip = LANES - 1 - lax.broadcasted_iota(jnp.int32, (LANES, LANES), 1)

    def write(region, out_ref, n):
        for r in range(0, size, LANES):
            at = pl.multiple_of(length - LANES - region * size - r, LANES)
            for h in range(0, total.shape[0], LANES):
                block = total[h:h + LANES, pl.ds(at, LANES)]
                block = jnp.take_along_axis(block, flip, axis=1).T
                out_ref[n, r:r + LANES, h:h + LANES] = block.astype(out_ref.dtype)

    for n in range(hops):
        chip = 2 * ((x + n) % hops)
        send_ref, keep_ref = (send_far, keep_far) if n else (send_near, keep_near)
        write(chip + 1 - core, send_ref, max(n - 1, 0))
        write(chip + core, keep_ref, max(n - 1, 0))


def correlate(place, records, templates, moveouts, uptime, hops):
    components, stations, length = records.shape
    window, bank_size = templates.shape[2:]
    margin = up(window, LANES)
    rows = up(stations * components, 8)
    region = length // (2 * hops)
    depth = up(components * up(window, GROUP), LANES)
    scalars = pl.BlockSpec(memory_space=pltpu.SMEM)
    vectors = pl.BlockSpec(memory_space=pltpu.VMEM)
    return pl.pallas_call(
        functools.partial(correlate_kernel, window=window),
        in_specs=[scalars, scalars, scalars, vectors, pl.BlockSpec(memory_space=pl.ANY)],
        out_specs=[vectors] * 4,
        scratch_shapes=[
            pltpu.VMEM((rows, length + margin + LANES + up(MAXMO, LANES)), jnp.float32),
            pltpu.VMEM((rows, length + margin), jnp.float32),
            pltpu.VMEM((rows, length), jnp.float32),
            pltpu.VMEM(templates.shape, templates.dtype),
            pltpu.VMEM((bank_size, bank_size), jnp.bfloat16),
            pltpu.VMEM((depth, bank_size), jnp.bfloat16),
            pltpu.VMEM((depth, length), jnp.bfloat16),
            pltpu.VMEM((depth, length), jnp.bfloat16),
            pltpu.VMEM((bank_size, depth), jnp.bfloat16),
            pltpu.VMEM((bank_size, depth), jnp.bfloat16),
            pltpu.VMEM((bank_size, length), jnp.float32),
            pltpu.SemaphoreType.DMA((stations,)),
        ],
        out_shape=[
            jax.ShapeDtypeStruct((count, region, bank_size), kind)
            for kind in (jnp.bfloat16, jnp.float32) for count in (hops - 1, 1)
        ],
        compiler_params=pltpu.CompilerParams(vmem_limit_bytes=58 * 2**20),
        name="correlate",
    )(place, moveouts, uptime, records, templates)


def body(records, templates, moveouts, uptime):
    tm, chan = lax.axis_size("tm"), lax.axis_size("chan")
    hops = tm // 2
    t, z = lax.axis_index("tm"), lax.axis_index("chan")
    send_far, send_near, keep_far, keep_near = correlate(
        t.reshape(1), records.transpose(1, 0, 2), templates, moveouts.T, uptime.T, hops
    )
    cores = [(i, i ^ 1) for i in range(tm)]
    far = lax.ppermute(send_far, "tm", cores)
    near = lax.ppermute(send_near, "tm", cores)
    far = (keep_far + far.astype(jnp.float32)).astype(jnp.bfloat16)
    result = keep_near[0] + near[0].astype(jnp.float32)
    for step in range(1, hops):
        perm = [(i, ((i // 2 + step) % hops) * 2 + i % 2) for i in range(tm)]
        result = result + lax.ppermute(far[step - 1], "tm", perm).astype(jnp.float32)
    mine = result.reshape(chan, result.shape[0] // chan, result.shape[1])
    result = lax.dynamic_index_in_dim(mine, z, 0, keepdims=False)
    for step in range(1, chan):
        block = lax.dynamic_index_in_dim(mine, (z + step) % chan, 0, keepdims=False)
        perm = [(i, (i + step) % chan) for i in range(chan)]
        result = result + lax.ppermute(block.astype(jnp.bfloat16), "chan", perm).astype(jnp.float32)
    return result.T


def solution(mesh):
    placed = (
        P(("grp", "tm", "chan"), None, None),
        P(("tm", "chan"), None, None, None),
        P(("tm", "chan"), None),
        P(("grp", "tm", "chan"), None),
    )
    return jax.shard_map(
        body, mesh=mesh, in_specs=placed, out_specs=P(None, ("grp", "tm", "chan")), check_vma=False
    )
```

```python
import functools

import jax
import jax.numpy as jnp
from jax import lax
from jax.experimental import pallas as pl
from jax.experimental.pallas import tpu as pltpu
from jax.sharding import PartitionSpec as P

MAXMO = 1000
LANES = 128
GROUP = 16


def up(value, unit):
    return -(-value // unit) * unit


def window_sum(values, window):
    def behind(array, by):
        return array if by == 0 else pltpu.roll(array, by, 1)

    total, offset, size, run = None, 0, 1, values
    while size <= window:
        if window & size:
            piece = behind(run, offset)
            total = piece if total is None else total + piece
            offset += size
        size *= 2
        if size <= window:
            run = run + behind(run, size // 2)
    return total


def correlate_kernel(
    place_ref, moveouts_ref, uptime_ref, records_ref, templates_ref, send_ref, keep_ref,
    masked, shifted, factor, loaded, bank, windows_a, windows_b, bank_a, bank_b, total, arrived,
    *, window, batch,
):
    components, stations, length = records_ref.shape
    block_count = uptime_ref.shape[0]
    rows = masked.shape[0]
    groups = up(window, GROUP) // GROUP
    margin = up(window, LANES)
    block_len = length // block_count
    span = shifted.shape[1]
    lead = masked.shape[1] - length

    def fetch(i):
        at = pl.ds(i * batch, batch)
        return pltpu.make_async_copy(templates_ref.at[at], loaded.at[at], arrived.at[i])

    def start(i, carry):
        fetch(i).start()
        return carry

    batches = stations // batch
    lax.fori_loop(0, batches, start, 0)

    masked[:, :lead] = jnp.zeros((rows, lead), jnp.float32)
    shifted[...] = jnp.zeros(shifted.shape, jnp.float32)
    total[...] = jnp.zeros(total.shape, total.dtype)
    for ref in (bank, bank_a, bank_b, windows_b):
        ref[...] = jnp.zeros(ref.shape, ref.dtype)
    depth = batch * components * groups * GROUP
    if windows_a.shape[0] > depth:
        windows_a[depth:, :] = jnp.zeros((windows_a.shape[0] - depth, length), windows_a.dtype)
    offsets = lax.broadcasted_iota(jnp.int32, (stations, LANES), 1)
    which = lax.broadcasted_iota(jnp.int32, (stations, LANES), 0)
    mirror = LANES - 1 - lax.broadcasted_iota(jnp.int32, (up(stations, 8), LANES), 1)

    def mask_tile(i, carry):
        at = pl.multiple_of(i * LANES, LANES)
        to = pl.multiple_of(lead + length - LANES - at, LANES)
        block = at // block_len
        limit = jnp.zeros((stations, LANES), jnp.int32)
        for s in range(stations):
            limit = jnp.where(which == s, uptime_ref[block, s], limit)
        live = offsets + (at - block * block_len) < limit
        for j in range(components):
            values = records_ref[j, :, pl.ds(at, LANES)].astype(jnp.float32)
            values = jnp.where(live, values, 0.0)
            if stations % 8:
                rest = jnp.zeros((up(stations, 8) - stations, LANES), jnp.float32)
                values = jnp.concatenate([values, rest], axis=0)
            values = jnp.take_along_axis(values, mirror, axis=1)
            masked[j * stations:(j + 1) * stations, pl.ds(to, LANES)] = values[:stations]
        return carry

    lax.fori_loop(0, length // LANES, mask_tile, 0, unroll=length // LANES <= 8)
    burst = stations

    def shift_some(i, carry):
        shifts = []
        for u in range(burst):
            for j in range(components):
                c = j * stations + i * burst + u
                moveout = moveouts_ref[j, i * burst + u]
                whole = moveout // LANES * LANES
                base = pl.multiple_of(lead - margin - LANES - whole, LANES)
                row = masked[pl.ds(c, 1), pl.ds(base, span + LANES)]
                shifts.append((c, pltpu.roll(row, moveout - whole, 1)))
        for c, row in shifts:
            shifted[pl.ds(c, 1), :] = row[:, LANES:]
        return carry

    lax.fori_loop(0, stations // burst, shift_some, 0)
    chunk = rows

    def energy_some(i, carry):
        at = pl.ds(pl.multiple_of(i * chunk, 8), chunk)
        values = shifted[at, :]
        energy = window_sum(values * values, window)[:, margin:]
        factor[at, :] = lax.rsqrt(jnp.maximum(energy, 1.0))
        return carry

    lax.fori_loop(0, rows // chunk, energy_some, 0)
    width = min(2 * LANES, length)

    def multiply(n, windows, turned):
        total[:, n:n + width] += jnp.dot(
            turned[...], windows[:, n:n + width], preferred_element_type=jnp.float32)

    def build(i, windows, turned, pending):
        places = [(u, j) for u in range(batch) for j in range(components)]
        strips, scales = [], []
        for u, j in places:
            c = j * stations + i * batch + u
            half = jnp.broadcast_to(shifted[pl.ds(c, 1), :], (8, span))
            strips.append(jnp.concatenate(
                [pltpu.roll(half, b, 1, stride=1, stride_axis=0) for b in (0, 8)], axis=0
            ).astype(jnp.bfloat16))
            scale = jnp.broadcast_to(factor[pl.ds(c, 1), :], (GROUP, length))
            scales.append(scale.astype(jnp.bfloat16))
        for m, (u, j) in enumerate(places):
            values = loaded[i * batch + u, j].astype(jnp.float32)
            squares = jnp.sum(values * values, axis=0, keepdims=True)
            unit = (values * lax.rsqrt(squares + 1e-06)).astype(jnp.bfloat16)
            bank[m * groups * GROUP:m * groups * GROUP + window, :] = unit
        turned[...] = bank[...].T
        left = list(range(0, length, width))
        share = up(len(left), len(places)) // len(places)
        for m in range(len(places)):
            for a in range(min(groups, LANES // GROUP)):
                rolled = strips[m] if a == 0 else pltpu.roll(strips[m], a * GROUP, 1)
                for g in range(a, groups, LANES // GROUP):
                    begin = margin - (g - a) * GROUP
                    at = (m * groups + g) * GROUP
                    windows[at:at + GROUP, :] = rolled[:, begin:begin + length] * scales[m]
            for n in left[:share]:
                multiply(n, *pending)
            left = left[share:]

    def two_batches(i, carry):
        @pl.when(2 * i < batches)
        def _():
            fetch(2 * i).wait()

        build(jnp.minimum(2 * i, batches - 1), windows_a, bank_a, (windows_b, bank_b))

        @pl.when(2 * i < batches)
        def _():
            @pl.when(2 * i + 1 < batches)
            def _():
                fetch(2 * i + 1).wait()

            build(jnp.minimum(2 * i + 1, batches - 1), windows_b, bank_b, (windows_a, bank_a))

        return carry

    lax.fori_loop(0, batches // 2 + 1, two_batches, 0)
    core = place_ref[0] % 2
    hops, region = keep_ref.shape[0], keep_ref.shape[1]
    flip = LANES - 1 - lax.broadcasted_iota(jnp.int32, (LANES, LANES), 1)

    def ordered(begin, h):
        at = pl.multiple_of(length - LANES - begin, LANES)
        block = total[h:h + LANES, pl.ds(at, LANES)]
        return jnp.take_along_axis(block, flip, axis=1).T

    for x in range(hops):
        for r in range(0, region, LANES):
            for h in range(0, total.shape[0], LANES):
                own = (2 * x + core) * region + r
                other = (2 * x + 1 - core) * region + r
                keep_ref[x, r:r + LANES, h:h + LANES] = ordered(own, h)
                send_ref[x, r:r + LANES, h:h + LANES] = ordered(other, h).astype(send_ref.dtype)


def correlate(place, records, templates, moveouts, uptime, hops):
    components, stations, length = records.shape
    window, bank_size = templates.shape[2:]
    margin = up(window, LANES)
    rows = up(stations * components, 8)
    region = length // (2 * hops)
    batch = 2 if stations % 2 == 0 else 1
    depth = up(batch * components * up(window, GROUP), LANES)
    scalars = pl.BlockSpec(memory_space=pltpu.SMEM)
    vectors = pl.BlockSpec(memory_space=pltpu.VMEM)
    return pl.pallas_call(
        functools.partial(correlate_kernel, window=window, batch=batch),
        in_specs=[scalars, scalars, scalars, vectors, pl.BlockSpec(memory_space=pl.ANY)],
        out_specs=[vectors] * 2,
        scratch_shapes=[
            pltpu.VMEM((rows, length + margin + LANES + up(MAXMO, LANES)), jnp.float32),
            pltpu.VMEM((rows, length + margin), jnp.float32),
            pltpu.VMEM((rows, length), jnp.float32),
            pltpu.VMEM(templates.shape, templates.dtype),
            pltpu.VMEM((depth, bank_size), jnp.bfloat16),
            pltpu.VMEM((depth, length), jnp.bfloat16),
            pltpu.VMEM((depth, length), jnp.bfloat16),
            pltpu.VMEM((bank_size, depth), jnp.bfloat16),
            pltpu.VMEM((bank_size, depth), jnp.bfloat16),
            pltpu.VMEM((bank_size, length), jnp.float32),
            pltpu.SemaphoreType.DMA((stations // batch,)),
        ],
        out_shape=[
            jax.ShapeDtypeStruct((hops, region, bank_size), kind)
            for kind in (jnp.bfloat16, jnp.float32)
        ],
        compiler_params=pltpu.CompilerParams(vmem_limit_bytes=58 * 2**20),
        name="correlate",
    )(place, moveouts, uptime, records, templates)


def body(records, templates, moveouts, uptime):
    tm, chan = lax.axis_size("tm"), lax.axis_size("chan")
    hops = tm // 2
    t, z = lax.axis_index("tm"), lax.axis_index("chan")
    x = t // 2
    send, keep = correlate(
        t.reshape(1), records.transpose(1, 0, 2), templates, moveouts.T, uptime.T, hops
    )
    got = lax.ppermute(send, "tm", [(i, i ^ 1) for i in range(tm)])
    mine = keep + got.astype(jnp.float32)
    result = lax.dynamic_index_in_dim(mine, x, 0, keepdims=False)
    for step in range(1, hops):
        block = lax.dynamic_index_in_dim(mine, (x + step) % hops, 0, keepdims=False)
        perm = [(i, ((i // 2 + step) % hops) * 2 + i % 2) for i in range(tm)]
        result = result + lax.ppermute(block.astype(jnp.bfloat16), "tm", perm).astype(jnp.float32)
    mine = result.reshape(chan, result.shape[0] // chan, result.shape[1])
    result = lax.dynamic_index_in_dim(mine, z, 0, keepdims=False)
    for step in range(1, chan):
        block = lax.dynamic_index_in_dim(mine, (z + step) % chan, 0, keepdims=False)
        perm = [(i, (i + step) % chan) for i in range(chan)]
        result = result + lax.ppermute(block.astype(jnp.bfloat16), "chan", perm).astype(jnp.float32)
    return result.T


def solution(mesh):
    placed = (
        P(("grp", "tm", "chan"), None, None),
        P(("tm", "chan"), None, None, None),
        P(("tm", "chan"), None),
        P(("grp", "tm", "chan"), None),
    )
    return jax.shard_map(
        body, mesh=mesh, in_specs=placed, out_specs=P(None, ("grp", "tm", "chan")), check_vma=False
    )
```

```python
import functools

import jax
import jax.numpy as jnp
from jax import lax
from jax.experimental import pallas as pl
from jax.experimental.pallas import tpu as pltpu
from jax.sharding import PartitionSpec as P

MAXMO = 1000
LANES = 128
GROUP = 16


def up(value, unit):
    return -(-value // unit) * unit


def window_sum(values, window):
    def behind(array, by):
        return array if by == 0 else pltpu.roll(array, by, 1)

    total, offset, size, run = None, 0, 1, values
    while size <= window:
        if window & size:
            piece = behind(run, offset)
            total = piece if total is None else total + piece
            offset += size
        size *= 2
        if size <= window:
            run = run + behind(run, size // 2)
    return total


def correlate_kernel(
    place_ref, moveouts_ref, uptime_ref, records_ref, templates_ref, send_ref, keep_ref,
    masked, shifted, factor, loaded, bank, windows_a, windows_b, bank_a, bank_b, total, arrived,
    *, window, batch,
):
    components, stations, length = records_ref.shape
    block_count = uptime_ref.shape[0]
    rows = masked.shape[0]
    groups = up(window, GROUP) // GROUP
    margin = up(window, LANES)
    block_len = length // block_count
    span = shifted.shape[1]
    lead = masked.shape[1] - length

    def fetch(i):
        at = pl.ds(i * batch, batch)
        return pltpu.make_async_copy(templates_ref.at[at], loaded.at[at], arrived.at[i])

    def start(i, carry):
        fetch(i).start()
        return carry

    batches = stations // batch
    lax.fori_loop(0, batches, start, 0)

    masked[:, :lead] = jnp.zeros((rows, lead), jnp.float32)
    shifted[...] = jnp.zeros(shifted.shape, jnp.float32)
    total[...] = jnp.zeros(total.shape, total.dtype)
    for ref in (bank, bank_a, bank_b, windows_b):
        ref[...] = jnp.zeros(ref.shape, ref.dtype)
    depth = batch * components * groups * GROUP
    if windows_a.shape[0] > depth:
        windows_a[depth:, :] = jnp.zeros((windows_a.shape[0] - depth, length), windows_a.dtype)
    offsets = lax.broadcasted_iota(jnp.int32, (stations, LANES), 1)
    which = lax.broadcasted_iota(jnp.int32, (stations, LANES), 0)
    mirror = LANES - 1 - lax.broadcasted_iota(jnp.int32, (up(stations, 8), LANES), 1)

    def mask_tile(i, carry):
        at = pl.multiple_of(i * LANES, LANES)
        to = pl.multiple_of(lead + length - LANES - at, LANES)
        block = at // block_len
        limit = jnp.zeros((stations, LANES), jnp.int32)
        for s in range(stations):
            limit = jnp.where(which == s, uptime_ref[block, s], limit)
        live = offsets + (at - block * block_len) < limit
        for j in range(components):
            values = records_ref[j, :, pl.ds(at, LANES)].astype(jnp.float32)
            values = jnp.where(live, values, 0.0)
            if stations % 8:
                rest = jnp.zeros((up(stations, 8) - stations, LANES), jnp.float32)
                values = jnp.concatenate([values, rest], axis=0)
            values = jnp.take_along_axis(values, mirror, axis=1)
            masked[j * stations:(j + 1) * stations, pl.ds(to, LANES)] = values[:stations]
        return carry

    lax.fori_loop(0, length // LANES, mask_tile, 0, unroll=length // LANES <= 8)
    burst = stations

    def shift_some(i, carry):
        shifts = []
        for u in range(burst):
            for j in range(components):
                c = j * stations + i * burst + u
                moveout = moveouts_ref[j, i * burst + u]
                whole = moveout // LANES * LANES
                base = pl.multiple_of(lead - margin - LANES - whole, LANES)
                row = masked[pl.ds(c, 1), pl.ds(base, span + LANES)]
                shifts.append((c, pltpu.roll(row, moveout - whole, 1)))
        for c, row in shifts:
            shifted[pl.ds(c, 1), :] = row[:, LANES:]
        return carry

    lax.fori_loop(0, stations // burst, shift_some, 0)
    chunk = rows

    def energy_some(i, carry):
        at = pl.ds(pl.multiple_of(i * chunk, 8), chunk)
        values = shifted[at, :]
        energy = window_sum(values * values, window)[:, margin:]
        factor[at, :] = lax.rsqrt(jnp.maximum(energy, 1.0))
        return carry

    lax.fori_loop(0, rows // chunk, energy_some, 0)
    width = min(2 * LANES, length)

    def multiply(n, windows, turned):
        total[:, n:n + width] += jnp.dot(
            turned[...], windows[:, n:n + width], preferred_element_type=jnp.float32)

    def build(i, windows, turned, pending):
        places = [(u, j) for u in range(batch) for j in range(components)]
        strips, scales = [], []
        for u, j in places:
            c = j * stations + i * batch + u
            half = jnp.broadcast_to(shifted[pl.ds(c, 1), :], (8, span))
            strips.append(jnp.concatenate(
                [pltpu.roll(half, b, 1, stride=1, stride_axis=0) for b in (0, 8)], axis=0
            ).astype(jnp.bfloat16))
            scale = jnp.broadcast_to(factor[pl.ds(c, 1), :], (GROUP, length))
            scales.append(scale.astype(jnp.bfloat16))
        for m, (u, j) in enumerate(places):
            values = loaded[i * batch + u, j].astype(jnp.float32)
            squares = jnp.sum(values * values, axis=0, keepdims=True)
            unit = (values * lax.rsqrt(squares + 1e-06)).astype(jnp.bfloat16)
            bank[m * groups * GROUP:m * groups * GROUP + window, :] = unit
        turned[...] = bank[...].T
        left = list(range(0, length, width))
        share = up(len(left), len(places)) // len(places)
        for m in range(len(places)):
            for a in range(min(groups, LANES // GROUP)):
                rolled = strips[m] if a == 0 else pltpu.roll(strips[m], a * GROUP, 1)
                for g in range(a, groups, LANES // GROUP):
                    begin = margin - (g - a) * GROUP
                    at = (m * groups + g) * GROUP
                    windows[at:at + GROUP, :] = rolled[:, begin:begin + length] * scales[m]
            for n in left[:share]:
                multiply(n, *pending)
            left = left[share:]

    def two_batches(i, carry):
        @pl.when(2 * i < batches)
        def _():
            fetch(2 * i).wait()

        build(jnp.minimum(2 * i, batches - 1), windows_a, bank_a, (windows_b, bank_b))

        @pl.when(2 * i < batches)
        def _():
            @pl.when(2 * i + 1 < batches)
            def _():
                fetch(2 * i + 1).wait()

            build(jnp.minimum(2 * i + 1, batches - 1), windows_b, bank_b, (windows_a, bank_a))

        return carry

    lax.fori_loop(0, batches // 2 + 1, two_batches, 0)
    core = place_ref[0] % 2
    hops, region = keep_ref.shape[0], keep_ref.shape[1]
    flip = LANES - 1 - lax.broadcasted_iota(jnp.int32, (LANES, LANES), 1)

    def ordered(begin, h):
        at = pl.multiple_of(length - LANES - begin, LANES)
        block = total[h:h + LANES, pl.ds(at, LANES)]
        return jnp.take_along_axis(block, flip, axis=1).T

    for x in range(hops):
        for r in range(0, region, LANES):
            for h in range(0, total.shape[0], LANES):
                own = (2 * x + core) * region + r
                other = (2 * x + 1 - core) * region + r
                keep_ref[x, r:r + LANES, h:h + LANES] = ordered(own, h)
                send_ref[x, r:r + LANES, h:h + LANES] = ordered(other, h).astype(send_ref.dtype)


def correlate(place, records, templates, moveouts, uptime, hops):
    components, stations, length = records.shape
    window, bank_size = templates.shape[2:]
    margin = up(window, LANES)
    rows = up(stations * components, 8)
    region = length // (2 * hops)
    batch = 2 if stations % 2 == 0 else 1
    depth = up(batch * components * up(window, GROUP), LANES)
    scalars = pl.BlockSpec(memory_space=pltpu.SMEM)
    vectors = pl.BlockSpec(memory_space=pltpu.VMEM)
    return pl.pallas_call(
        functools.partial(correlate_kernel, window=window, batch=batch),
        in_specs=[scalars, scalars, scalars, vectors, pl.BlockSpec(memory_space=pl.ANY)],
        out_specs=[vectors] * 2,
        scratch_shapes=[
            pltpu.VMEM((rows, length + margin + LANES + up(MAXMO, LANES)), jnp.float32),
            pltpu.VMEM((rows, length + margin), jnp.float32),
            pltpu.VMEM((rows, length), jnp.float32),
            pltpu.VMEM(templates.shape, templates.dtype),
            pltpu.VMEM((depth, bank_size), jnp.bfloat16),
            pltpu.VMEM((depth, length), jnp.bfloat16),
            pltpu.VMEM((depth, length), jnp.bfloat16),
            pltpu.VMEM((bank_size, depth), jnp.bfloat16),
            pltpu.VMEM((bank_size, depth), jnp.bfloat16),
            pltpu.VMEM((bank_size, length), jnp.float32),
            pltpu.SemaphoreType.DMA((stations // batch,)),
        ],
        out_shape=[
            jax.ShapeDtypeStruct((hops, region, bank_size), kind)
            for kind in (jnp.bfloat16, jnp.float32)
        ],
        compiler_params=pltpu.CompilerParams(vmem_limit_bytes=58 * 2**20),
        name="correlate",
    )(place, moveouts, uptime, records, templates)


def body(records, templates, moveouts, uptime):
    tm, chan = lax.axis_size("tm"), lax.axis_size("chan")
    hops = tm // 2
    t, z = lax.axis_index("tm"), lax.axis_index("chan")
    x = t // 2
    send, keep = correlate(
        t.reshape(1), records.transpose(1, 0, 2), templates, moveouts.T, uptime.T, hops
    )
    got = lax.ppermute(send, "tm", [(i, i ^ 1) for i in range(tm)])
    mine = keep + got.astype(jnp.float32)
    x_bits = [("tm", 2 << b, (x >> b) & 1) for b in range((hops - 1).bit_length())]
    z_bits = [("chan", 1 << b, (z >> b) & 1) for b in range((chan - 1).bit_length())]
    names = x_bits[::-1] + z_bits[::-1]
    orders = (x_bits + z_bits, z_bits[:1] + x_bits + z_bits[1:])
    samples, bank_size = mine.shape[1] // chan, mine.shape[2]
    mine = mine.reshape((2,) * len(names) + (samples, bank_size))
    width = bank_size // len(orders)
    halves = [mine[..., h * width:(h + 1) * width] for h in range(len(orders))]
    left = [list(names) for _ in orders]

    def give(part, axis, bit):
        send = lax.dynamic_index_in_dim(part, 1 - bit, axis, keepdims=False)
        return send.astype(jnp.bfloat16)

    def swap(array, axis_name, distance):
        count = lax.axis_size(axis_name)
        return lax.ppermute(array, axis_name, [(i, i ^ distance) for i in range(count)])

    joined = None
    for steps in zip(*orders):
        if all(step is steps[0] for step in steps) and len(left[0]) == 1:
            joined = jnp.concatenate(halves, axis=-1)
            name, distance, bit = steps[0]
            came = swap(give(joined, 0, bit), name, distance)
            joined = lax.dynamic_index_in_dim(joined, bit, 0, keepdims=False)
            joined = joined + came.astype(jnp.float32)
            break
        axes = [left[h].index(step) for h, step in enumerate(steps)]
        came = [
            swap(give(halves[h], axes[h], step[2]), step[0], step[1])
            for h, step in enumerate(steps)
        ]
        for h, step in enumerate(steps):
            kept = lax.dynamic_index_in_dim(halves[h], step[2], axes[h], keepdims=False)
            halves[h] = kept + came[h].astype(jnp.float32)
            left[h].pop(axes[h])
    if joined is None:
        joined = jnp.concatenate(halves, axis=-1)
    return joined.T


def solution(mesh):
    placed = (
        P(("grp", "tm", "chan"), None, None),
        P(("tm", "chan"), None, None, None),
        P(("tm", "chan"), None),
        P(("grp", "tm", "chan"), None),
    )
    return jax.shard_map(
        body, mesh=mesh, in_specs=placed, out_specs=P(None, ("grp", "tm", "chan")), check_vma=False
    )
```

```python
import functools

import jax
import jax.numpy as jnp
from jax import lax
from jax.experimental import pallas as pl
from jax.experimental.pallas import tpu as pltpu
from jax.sharding import PartitionSpec as P

MAXMO = 1000
LANES = 128
GROUP = 16


def up(value, unit):
    return -(-value // unit) * unit


def window_sum(values, window):
    def behind(array, by):
        return array if by == 0 else pltpu.roll(array, by, 1)

    total, offset, size, run = None, 0, 1, values
    while size <= window:
        if window & size:
            piece = behind(run, offset)
            total = piece if total is None else total + piece
            offset += size
        size *= 2
        if size <= window:
            run = run + behind(run, size // 2)
    return total


def correlate_kernel(
    place_ref, numbers_ref, records_ref, templates_ref, send_ref, keep_ref,
    masked, shifted, factor, loaded, bank, windows_a, windows_b, bank_a, bank_b, total, arrived,
    *, window, batch,
):
    components, stations, length = records_ref.shape
    block_count = numbers_ref.shape[0] - components
    rows = masked.shape[0]
    groups = up(window, GROUP) // GROUP
    margin = up(window, LANES)
    block_len = length // block_count
    span = shifted.shape[1]
    lead = masked.shape[1] - length

    def fetch(i):
        at = pl.ds(i * batch, batch)
        return pltpu.make_async_copy(templates_ref.at[at], loaded.at[at], arrived.at[i])

    def start(i, carry):
        fetch(i).start()
        return carry

    batches = stations // batch
    lax.fori_loop(0, batches, start, 0)

    masked[:, :lead] = jnp.zeros((rows, lead), jnp.float32)
    shifted[...] = jnp.zeros(shifted.shape, jnp.float32)
    total[...] = jnp.zeros(total.shape, total.dtype)
    for ref in (bank, bank_a, bank_b, windows_b):
        ref[...] = jnp.zeros(ref.shape, ref.dtype)
    depth = batch * components * groups * GROUP
    if windows_a.shape[0] > depth:
        windows_a[depth:, :] = jnp.zeros((windows_a.shape[0] - depth, length), windows_a.dtype)
    offsets = lax.broadcasted_iota(jnp.int32, (stations, LANES), 1)
    which = lax.broadcasted_iota(jnp.int32, (stations, LANES), 0)
    mirror = LANES - 1 - lax.broadcasted_iota(jnp.int32, (up(stations, 8), LANES), 1)

    def mask_tile(i, carry):
        at = pl.multiple_of(i * LANES, LANES)
        to = pl.multiple_of(lead + length - LANES - at, LANES)
        block = at // block_len
        limit = jnp.zeros((stations, LANES), jnp.int32)
        for s in range(stations):
            limit = jnp.where(which == s, numbers_ref[components + block, s], limit)
        live = offsets + (at - block * block_len) < limit
        for j in range(components):
            values = records_ref[j, :, pl.ds(at, LANES)].astype(jnp.float32)
            values = jnp.where(live, values, 0.0)
            if stations % 8:
                rest = jnp.zeros((up(stations, 8) - stations, LANES), jnp.float32)
                values = jnp.concatenate([values, rest], axis=0)
            values = jnp.take_along_axis(values, mirror, axis=1)
            masked[j * stations:(j + 1) * stations, pl.ds(to, LANES)] = values[:stations]
        return carry

    lax.fori_loop(0, length // LANES, mask_tile, 0, unroll=length // LANES <= 8)
    burst = stations

    def shift_some(i, carry):
        shifts = []
        for u in range(burst):
            for j in range(components):
                c = j * stations + i * burst + u
                moveout = numbers_ref[j, i * burst + u]
                whole = moveout // LANES * LANES
                base = pl.multiple_of(lead - margin - LANES - whole, LANES)
                row = masked[pl.ds(c, 1), pl.ds(base, span + LANES)]
                shifts.append((c, pltpu.roll(row, moveout - whole, 1)))
        for c, row in shifts:
            shifted[pl.ds(c, 1), :] = row[:, LANES:]
        return carry

    lax.fori_loop(0, stations // burst, shift_some, 0)
    chunk = rows

    def energy_some(i, carry):
        at = pl.ds(pl.multiple_of(i * chunk, 8), chunk)
        values = shifted[at, :]
        energy = window_sum(values * values, window)[:, margin:]
        factor[at, :] = lax.rsqrt(jnp.maximum(energy, 1.0))
        return carry

    lax.fori_loop(0, rows // chunk, energy_some, 0)
    width = min(2 * LANES, length)

    def multiply(n, windows, turned):
        total[:, n:n + width] += jnp.dot(
            turned[...], windows[:, n:n + width], preferred_element_type=jnp.float32)

    def build(i, windows, turned, pending):
        places = [(u, j) for u in range(batch) for j in range(components)]
        strips, scales = [], []
        for u, j in places:
            c = j * stations + i * batch + u
            half = jnp.broadcast_to(shifted[pl.ds(c, 1), :], (8, span))
            strips.append(jnp.concatenate(
                [pltpu.roll(half, b, 1, stride=1, stride_axis=0) for b in (0, 8)], axis=0
            ).astype(jnp.bfloat16))
            scale = jnp.broadcast_to(factor[pl.ds(c, 1), :], (GROUP, length))
            scales.append(scale.astype(jnp.bfloat16))
        for m, (u, j) in enumerate(places):
            values = loaded[i * batch + u, j].astype(jnp.float32)
            squares = jnp.sum(values * values, axis=0, keepdims=True)
            unit = (values * lax.rsqrt(squares + 1e-06)).astype(jnp.bfloat16)
            bank[m * groups * GROUP:m * groups * GROUP + window, :] = unit
        turned[...] = bank[...].T
        left = list(range(0, length, width))
        share = up(len(left), len(places)) // len(places)
        for m in range(len(places)):
            for a in range(min(groups, LANES // GROUP)):
                rolled = strips[m] if a == 0 else pltpu.roll(strips[m], a * GROUP, 1)
                for g in range(a, groups, LANES // GROUP):
                    begin = margin - (g - a) * GROUP
                    at = (m * groups + g) * GROUP
                    windows[at:at + GROUP, :] = rolled[:, begin:begin + length] * scales[m]
            for n in left[:share]:
                multiply(n, *pending)
            left = left[share:]

    def two_batches(i, carry):
        @pl.when(2 * i < batches)
        def _():
            fetch(2 * i).wait()

        build(jnp.minimum(2 * i, batches - 1), windows_a, bank_a, (windows_b, bank_b))

        @pl.when(2 * i < batches)
        def _():
            @pl.when(2 * i + 1 < batches)
            def _():
                fetch(2 * i + 1).wait()

            build(jnp.minimum(2 * i + 1, batches - 1), windows_b, bank_b, (windows_a, bank_a))

        return carry

    lax.fori_loop(0, batches // 2 + 1, two_batches, 0)
    core = place_ref[0] % 2
    hops, region = keep_ref.shape[0], keep_ref.shape[1]
    flip = LANES - 1 - lax.broadcasted_iota(jnp.int32, (LANES, LANES), 1)

    def ordered(begin, h):
        at = pl.multiple_of(length - LANES - begin, LANES)
        block = total[h:h + LANES, pl.ds(at, LANES)]
        return jnp.take_along_axis(block, flip, axis=1).T

    for x in range(hops):
        for r in range(0, region, LANES):
            for h in range(0, total.shape[0], LANES):
                own = (2 * x + core) * region + r
                other = (2 * x + 1 - core) * region + r
                keep_ref[x, r:r + LANES, h:h + LANES] = ordered(own, h)
                send_ref[x, r:r + LANES, h:h + LANES] = ordered(other, h).astype(send_ref.dtype)


def correlate(place, numbers, records, templates, hops):
    components, stations, length = records.shape
    window, bank_size = templates.shape[2:]
    margin = up(window, LANES)
    rows = up(stations * components, 8)
    region = length // (2 * hops)
    batch = 2 if stations % 2 == 0 else 1
    depth = up(batch * components * up(window, GROUP), LANES)
    scalars = pl.BlockSpec(memory_space=pltpu.SMEM)
    vectors = pl.BlockSpec(memory_space=pltpu.VMEM)
    return pl.pallas_call(
        functools.partial(correlate_kernel, window=window, batch=batch),
        in_specs=[scalars, scalars, vectors, pl.BlockSpec(memory_space=pl.ANY)],
        out_specs=[vectors] * 2,
        scratch_shapes=[
            pltpu.VMEM((rows, length + margin + LANES + up(MAXMO, LANES)), jnp.float32),
            pltpu.VMEM((rows, length + margin), jnp.float32),
            pltpu.VMEM((rows, length), jnp.float32),
            pltpu.VMEM(templates.shape, templates.dtype),
            pltpu.VMEM((depth, bank_size), jnp.bfloat16),
            pltpu.VMEM((depth, length), jnp.bfloat16),
            pltpu.VMEM((depth, length), jnp.bfloat16),
            pltpu.VMEM((bank_size, depth), jnp.bfloat16),
            pltpu.VMEM((bank_size, depth), jnp.bfloat16),
            pltpu.VMEM((bank_size, length), jnp.float32),
            pltpu.SemaphoreType.DMA((stations // batch,)),
        ],
        out_shape=[
            jax.ShapeDtypeStruct((hops, region, bank_size), kind)
            for kind in (jnp.bfloat16, jnp.float32)
        ],
        compiler_params=pltpu.CompilerParams(vmem_limit_bytes=52 * 2**20),
        name="correlate",
    )(place, numbers, records, templates)


def body(records, templates, moveouts, uptime):
    tm, chan = lax.axis_size("tm"), lax.axis_size("chan")
    hops = tm // 2
    t, z = lax.axis_index("tm"), lax.axis_index("chan")
    x = t // 2
    send, keep = correlate(
        t.reshape(1), jnp.concatenate([moveouts.T, uptime.T]), records.transpose(1, 0, 2), templates, hops
    )
    got = lax.ppermute(send, "tm", [(i, i ^ 1) for i in range(tm)])
    mine = keep + got.astype(jnp.float32)
    result = lax.dynamic_index_in_dim(mine, x, 0, keepdims=False)
    for step in range(1, hops):
        block = lax.dynamic_index_in_dim(mine, (x + step) % hops, 0, keepdims=False)
        perm = [(i, ((i // 2 + step) % hops) * 2 + i % 2) for i in range(tm)]
        result = result + lax.ppermute(block.astype(jnp.bfloat16), "tm", perm).astype(jnp.float32)
    mine = result.reshape(chan, result.shape[0] // chan, result.shape[1])
    result = lax.dynamic_index_in_dim(mine, z, 0, keepdims=False)
    for step in range(1, chan):
        block = lax.dynamic_index_in_dim(mine, (z + step) % chan, 0, keepdims=False)
        perm = [(i, (i + step) % chan) for i in range(chan)]
        result = result + lax.ppermute(block.astype(jnp.bfloat16), "chan", perm).astype(jnp.float32)
    return result.T


def solution(mesh):
    placed = (
        P(("grp", "tm", "chan"), None, None),
        P(("tm", "chan"), None, None, None),
        P(("tm", "chan"), None),
        P(("grp", "tm", "chan"), None),
    )
    return jax.shard_map(
        body, mesh=mesh, in_specs=placed, out_specs=P(None, ("grp", "tm", "chan")), check_vma=False
    )
```

```python
import functools

import jax
import jax.numpy as jnp
from jax import lax
from jax.experimental import pallas as pl
from jax.experimental.pallas import tpu as pltpu
from jax.sharding import PartitionSpec as P

MAXMO = 1000
LANES = 128
GROUP = 16


def up(value, unit):
    return -(-value // unit) * unit


def window_sum(values, window):
    def behind(array, by):
        return array if by == 0 else pltpu.roll(array, by, 1)

    total, offset, size, run = None, 0, 1, values
    while size <= window:
        if window & size:
            piece = behind(run, offset)
            total = piece if total is None else total + piece
            offset += size
        size *= 2
        if size <= window:
            run = run + behind(run, size // 2)
    return total


def correlate_kernel(
    place_ref, numbers_ref, records_ref, templates_ref, send_ref, keep_ref,
    masked, shifted, factor, loaded, bank, windows_a, windows_b, bank_a, bank_b, total, arrived,
    *, window, batch,
):
    components, stations, length = records_ref.shape
    block_count = numbers_ref.shape[0] - components
    rows = masked.shape[0]
    groups = up(window, GROUP) // GROUP
    margin = up(window, LANES)
    block_len = length // block_count
    span = shifted.shape[1]
    lead = masked.shape[1] - length

    def fetch(i):
        at = pl.ds(i * batch, batch)
        return pltpu.make_async_copy(templates_ref.at[at], loaded.at[at], arrived.at[i])

    def start(i, carry):
        fetch(i).start()
        return carry

    batches = stations // batch
    lax.fori_loop(0, batches, start, 0)

    masked[:, :lead] = jnp.zeros((rows, lead), jnp.float32)
    shifted[...] = jnp.zeros(shifted.shape, jnp.float32)
    total[...] = jnp.zeros(total.shape, total.dtype)
    for ref in (bank, bank_a, bank_b, windows_b):
        ref[...] = jnp.zeros(ref.shape, ref.dtype)
    depth = batch * components * groups * GROUP
    if windows_a.shape[0] > depth:
        windows_a[depth:, :] = jnp.zeros((windows_a.shape[0] - depth, length), windows_a.dtype)
    offsets = lax.broadcasted_iota(jnp.int32, (stations, LANES), 1)
    which = lax.broadcasted_iota(jnp.int32, (stations, LANES), 0)
    mirror = LANES - 1 - lax.broadcasted_iota(jnp.int32, (up(stations, 8), LANES), 1)

    def mask_tile(i, carry):
        at = pl.multiple_of(i * LANES, LANES)
        to = pl.multiple_of(lead + length - LANES - at, LANES)
        block = at // block_len
        limit = jnp.zeros((stations, LANES), jnp.int32)
        for s in range(stations):
            limit = jnp.where(which == s, numbers_ref[components + block, s], limit)
        live = offsets + (at - block * block_len) < limit
        for j in range(components):
            values = records_ref[j, :, pl.ds(at, LANES)].astype(jnp.float32)
            values = jnp.where(live, values, 0.0)
            if stations % 8:
                rest = jnp.zeros((up(stations, 8) - stations, LANES), jnp.float32)
                values = jnp.concatenate([values, rest], axis=0)
            values = jnp.take_along_axis(values, mirror, axis=1)
            masked[j * stations:(j + 1) * stations, pl.ds(to, LANES)] = values[:stations]
        return carry

    lax.fori_loop(0, length // LANES, mask_tile, 0, unroll=length // LANES <= 8)
    burst = stations

    def shift_some(i, carry):
        shifts = []
        for u in range(burst):
            for j in range(components):
                c = j * stations + i * burst + u
                moveout = numbers_ref[j, i * burst + u]
                whole = moveout // LANES * LANES
                base = pl.multiple_of(lead - margin - LANES - whole, LANES)
                row = masked[pl.ds(c, 1), pl.ds(base, span + LANES)]
                shifts.append((c, pltpu.roll(row, moveout - whole, 1)))
        for c, row in shifts:
            shifted[pl.ds(c, 1), :] = row[:, LANES:]
        return carry

    lax.fori_loop(0, stations // burst, shift_some, 0)
    chunk = rows

    def energy_some(i, carry):
        at = pl.ds(pl.multiple_of(i * chunk, 8), chunk)
        values = shifted[at, :]
        energy = window_sum(values * values, window)[:, margin:]
        factor[at, :] = lax.rsqrt(jnp.maximum(energy, 1.0))
        return carry

    lax.fori_loop(0, rows // chunk, energy_some, 0)
    width = min(2 * LANES, length)

    def multiply(n, windows, turned):
        total[:, n:n + width] += jnp.dot(
            turned[...], windows[:, n:n + width], preferred_element_type=jnp.float32)

    def build(i, windows, turned, pending):
        places = [(u, j) for u in range(batch) for j in range(components)]
        strips, scales = [], []
        for u, j in places:
            c = j * stations + i * batch + u
            half = jnp.broadcast_to(shifted[pl.ds(c, 1), :], (8, span))
            strips.append(jnp.concatenate(
                [pltpu.roll(half, b, 1, stride=1, stride_axis=0) for b in (0, 8)], axis=0
            ).astype(jnp.bfloat16))
            scale = jnp.broadcast_to(factor[pl.ds(c, 1), :], (GROUP, length))
            scales.append(scale.astype(jnp.bfloat16))
        for m, (u, j) in enumerate(places):
            values = loaded[i * batch + u, j].astype(jnp.float32)
            squares = jnp.sum(values * values, axis=0, keepdims=True)
            unit = (values * lax.rsqrt(squares + 1e-06)).astype(jnp.bfloat16)
            bank[m * groups * GROUP:m * groups * GROUP + window, :] = unit
        turned[...] = bank[...].T
        left = list(range(0, length, width))
        share = up(len(left), len(places)) // len(places)
        for m in range(len(places)):
            for a in range(min(groups, LANES // GROUP)):
                rolled = strips[m] if a == 0 else pltpu.roll(strips[m], a * GROUP, 1)
                for g in range(a, groups, LANES // GROUP):
                    begin = margin - (g - a) * GROUP
                    at = (m * groups + g) * GROUP
                    windows[at:at + GROUP, :] = rolled[:, begin:begin + length] * scales[m]
            for n in left[:share]:
                multiply(n, *pending)
            left = left[share:]

    def two_batches(i, carry):
        @pl.when(2 * i < batches)
        def _():
            fetch(2 * i).wait()

        build(jnp.minimum(2 * i, batches - 1), windows_a, bank_a, (windows_b, bank_b))

        @pl.when(2 * i < batches)
        def _():
            @pl.when(2 * i + 1 < batches)
            def _():
                fetch(2 * i + 1).wait()

            build(jnp.minimum(2 * i + 1, batches - 1), windows_b, bank_b, (windows_a, bank_a))

        return carry

    lax.fori_loop(0, batches // 2 + 1, two_batches, 0)
    core = place_ref[0] % 2
    hops, region = keep_ref.shape[0], keep_ref.shape[1]
    flip = LANES - 1 - lax.broadcasted_iota(jnp.int32, (LANES, LANES), 1)

    def ordered(begin, h):
        at = pl.multiple_of(length - LANES - begin, LANES)
        block = total[h:h + LANES, pl.ds(at, LANES)]
        return jnp.take_along_axis(block, flip, axis=1).T

    for x in range(hops):
        for r in range(0, region, LANES):
            for h in range(0, total.shape[0], LANES):
                own = (2 * x + core) * region + r
                other = (2 * x + 1 - core) * region + r
                keep_ref[x, r:r + LANES, h:h + LANES] = ordered(own, h)
                send_ref[x, r:r + LANES, h:h + LANES] = ordered(other, h).astype(send_ref.dtype)


def correlate(place, numbers, records, templates, hops):
    components, stations, length = records.shape
    window, bank_size = templates.shape[2:]
    margin = up(window, LANES)
    rows = up(stations * components, 8)
    region = length // (2 * hops)
    batch = 2 if stations % 2 == 0 else 1
    depth = up(batch * components * up(window, GROUP), LANES)
    scalars = pl.BlockSpec(memory_space=pltpu.SMEM)
    vectors = pl.BlockSpec(memory_space=pltpu.VMEM)
    return pl.pallas_call(
        functools.partial(correlate_kernel, window=window, batch=batch),
        in_specs=[scalars, scalars, vectors, pl.BlockSpec(memory_space=pl.ANY)],
        out_specs=[vectors] * 2,
        scratch_shapes=[
            pltpu.VMEM((rows, length + margin + LANES + up(MAXMO, LANES)), jnp.float32),
            pltpu.VMEM((rows, length + margin), jnp.float32),
            pltpu.VMEM((rows, length), jnp.float32),
            pltpu.VMEM(templates.shape, templates.dtype),
            pltpu.VMEM((depth, bank_size), jnp.bfloat16),
            pltpu.VMEM((depth, length), jnp.bfloat16),
            pltpu.VMEM((depth, length), jnp.bfloat16),
            pltpu.VMEM((bank_size, depth), jnp.bfloat16),
            pltpu.VMEM((bank_size, depth), jnp.bfloat16),
            pltpu.VMEM((bank_size, length), jnp.float32),
            pltpu.SemaphoreType.DMA((stations // batch,)),
        ],
        out_shape=[
            jax.ShapeDtypeStruct((hops, region, bank_size), kind)
            for kind in (jnp.bfloat16, jnp.float32)
        ],
        compiler_params=pltpu.CompilerParams(vmem_limit_bytes=52 * 2**20),
        name="correlate",
    )(place, numbers, records, templates)


def body(records, templates, moveouts, uptime):
    tm, chan = lax.axis_size("tm"), lax.axis_size("chan")
    hops = tm // 2
    t, z = lax.axis_index("tm"), lax.axis_index("chan")
    x = t // 2
    send, keep = correlate(
        t.reshape(1), jnp.concatenate([moveouts.T, uptime.T]), records.transpose(1, 0, 2), templates, hops
    )
    got = lax.ppermute(send, "tm", [(i, i ^ 1) for i in range(tm)])
    mine = keep + got.astype(jnp.float32)
    result = lax.dynamic_index_in_dim(mine, x, 0, keepdims=False)
    for step in range(1, hops):
        block = lax.dynamic_index_in_dim(mine, (x + step) % hops, 0, keepdims=False)
        perm = [(i, ((i // 2 + step) % hops) * 2 + i % 2) for i in range(tm)]
        result = result + lax.ppermute(block.astype(jnp.bfloat16), "tm", perm).astype(jnp.float32)
    mine = result.reshape(chan, result.shape[0] // chan, result.shape[1])
    result = lax.dynamic_index_in_dim(mine, z, 0, keepdims=False)
    paired = chan & (chan - 1) == 0

    def partner(place, step):
        return place ^ step if paired else (place + step) % chan

    for step in range(1, chan):
        block = lax.dynamic_index_in_dim(mine, partner(z, step), 0, keepdims=False)
        perm = [(i, partner(i, step)) for i in range(chan)]
        result = result + lax.ppermute(block.astype(jnp.bfloat16), "chan", perm).astype(jnp.float32)
    return result.T


def solution(mesh):
    placed = (
        P(("grp", "tm", "chan"), None, None),
        P(("tm", "chan"), None, None, None),
        P(("tm", "chan"), None),
        P(("grp", "tm", "chan"), None),
    )
    return jax.shard_map(
        body, mesh=mesh, in_specs=placed, out_specs=P(None, ("grp", "tm", "chan")), check_vma=False
    )
```

```python
import functools

import jax
import jax.numpy as jnp
from jax import lax
from jax.experimental import pallas as pl
from jax.experimental.pallas import tpu as pltpu
from jax.sharding import PartitionSpec as P

MAXMO = 1000
LANES = 128
GROUP = 16


def up(value, unit):
    return -(-value // unit) * unit


def window_sum(values, window):
    def behind(array, by):
        return array if by == 0 else pltpu.roll(array, by, 1)

    total, offset, size, run = None, 0, 1, values
    while size <= window:
        if window & size:
            piece = behind(run, offset)
            total = piece if total is None else total + piece
            offset += size
        size *= 2
        if size <= window:
            run = run + behind(run, size // 2)
    return total


def correlate_kernel(
    place_ref, numbers_ref, records_ref, templates_ref, send_ref, keep_ref,
    masked, shifted, factor, loaded, bank, windows_a, windows_b, bank_a, bank_b, total, arrived,
    *, window, batch,
):
    components, stations, length = records_ref.shape
    block_count = numbers_ref.shape[0] - components
    rows = masked.shape[0]
    groups = up(window, GROUP) // GROUP
    margin = up(window, LANES)
    block_len = length // block_count
    span = shifted.shape[1]
    lead = masked.shape[1] - length

    def fetch(i):
        at = pl.ds(i * batch, batch)
        return pltpu.make_async_copy(templates_ref.at[at], loaded.at[at], arrived.at[i])

    def start(i, carry):
        fetch(i).start()
        return carry

    batches = stations // batch
    lax.fori_loop(0, batches, start, 0)

    masked[:, :lead] = jnp.zeros((rows, lead), jnp.float32)
    shifted[...] = jnp.zeros(shifted.shape, jnp.float32)
    total[...] = jnp.zeros(total.shape, total.dtype)
    bank[...] = jnp.zeros(bank.shape, bank.dtype)
    depth = batch * components * groups * GROUP
    if windows_a.shape[0] > depth:
        for windows in (windows_a, windows_b):
            rest = (windows.shape[0] - depth, length)
            windows[depth:, :] = jnp.zeros(rest, windows.dtype)
    offsets = lax.broadcasted_iota(jnp.int32, (stations, LANES), 1)
    which = lax.broadcasted_iota(jnp.int32, (stations, LANES), 0)
    mirror = LANES - 1 - lax.broadcasted_iota(jnp.int32, (up(stations, 8), LANES), 1)

    def mask_tile(i, carry):
        at = pl.multiple_of(i * LANES, LANES)
        to = pl.multiple_of(lead + length - LANES - at, LANES)
        block = at // block_len
        limit = jnp.zeros((stations, LANES), jnp.int32)
        for s in range(stations):
            limit = jnp.where(which == s, numbers_ref[components + block, s], limit)
        live = offsets + (at - block * block_len) < limit
        for j in range(components):
            values = records_ref[j, :, pl.ds(at, LANES)].astype(jnp.float32)
            values = jnp.where(live, values, 0.0)
            if stations % 8:
                rest = jnp.zeros((up(stations, 8) - stations, LANES), jnp.float32)
                values = jnp.concatenate([values, rest], axis=0)
            values = jnp.take_along_axis(values, mirror, axis=1)
            masked[j * stations:(j + 1) * stations, pl.ds(to, LANES)] = values[:stations]
        return carry

    lax.fori_loop(0, length // LANES, mask_tile, 0, unroll=length // LANES <= 8)
    burst = stations

    def shift_some(i, carry):
        shifts = []
        for u in range(burst):
            for j in range(components):
                c = j * stations + i * burst + u
                moveout = numbers_ref[j, i * burst + u]
                whole = moveout // LANES * LANES
                base = pl.multiple_of(lead - margin - LANES - whole, LANES)
                row = masked[pl.ds(c, 1), pl.ds(base, span + LANES)]
                shifts.append((c, pltpu.roll(row, moveout - whole, 1)))
        for c, row in shifts:
            shifted[pl.ds(c, 1), :] = row[:, LANES:]
        return carry

    lax.fori_loop(0, stations // burst, shift_some, 0)
    chunk = rows

    def energy_some(i, carry):
        at = pl.ds(pl.multiple_of(i * chunk, 8), chunk)
        values = shifted[at, :]
        energy = window_sum(values * values, window)[:, margin:]
        factor[at, :] = lax.rsqrt(jnp.maximum(energy, 1.0))
        return carry

    lax.fori_loop(0, rows // chunk, energy_some, 0)
    width = min(2 * LANES, length)

    def multiply(n, windows, turned):
        total[:, n:n + width] += jnp.dot(
            turned[...], windows[:, n:n + width], preferred_element_type=jnp.float32)

    def build(i, windows, turned, pending):
        places = [(u, j) for u in range(batch) for j in range(components)]
        strips, scales = [], []
        for u, j in places:
            c = j * stations + i * batch + u
            half = jnp.broadcast_to(shifted[pl.ds(c, 1), :], (8, span))
            strips.append(jnp.concatenate(
                [pltpu.roll(half, b, 1, stride=1, stride_axis=0) for b in (0, 8)], axis=0
            ).astype(jnp.bfloat16))
            scale = jnp.broadcast_to(factor[pl.ds(c, 1), :], (GROUP, length))
            scales.append(scale.astype(jnp.bfloat16))
        for m, (u, j) in enumerate(places):
            values = loaded[i * batch + u, j].astype(jnp.float32)
            squares = jnp.sum(values * values, axis=0, keepdims=True)
            unit = (values * lax.rsqrt(squares + 1e-06)).astype(jnp.bfloat16)
            bank[m * groups * GROUP:m * groups * GROUP + window, :] = unit
        turned[...] = bank[...].T
        left = list(range(0, length, width)) if pending else []
        share = up(len(left), len(places)) // len(places)
        for m in range(len(places)):
            for a in range(min(groups, LANES // GROUP)):
                rolled = strips[m] if a == 0 else pltpu.roll(strips[m], a * GROUP, 1)
                for g in range(a, groups, LANES // GROUP):
                    begin = margin - (g - a) * GROUP
                    at = (m * groups + g) * GROUP
                    windows[at:at + GROUP, :] = rolled[:, begin:begin + length] * scales[m]
            for n in left[:share]:
                multiply(n, *pending)
            left = left[share:]

    a, b = (windows_a, bank_a), (windows_b, bank_b)
    fetch(0).wait()
    build(0, *a, None)

    def two_batches(i, carry):
        fetch(2 * i + 1).wait()
        build(2 * i + 1, *b, a)

        @pl.when(2 * i + 2 < batches)
        def _():
            fetch(2 * i + 2).wait()

        build(jnp.minimum(2 * i + 2, batches - 1), *a, b)
        return carry

    if batches > 1:
        lax.fori_loop(0, batches // 2, two_batches, 0)
    if batches % 2:
        for n in range(0, length, width):
            multiply(n, *a)

    core = place_ref[0] % 2
    hops, region = keep_ref.shape[0], keep_ref.shape[1]
    flip = LANES - 1 - lax.broadcasted_iota(jnp.int32, (LANES, LANES), 1)

    def ordered(begin, h):
        at = pl.multiple_of(length - LANES - begin, LANES)
        block = total[h:h + LANES, pl.ds(at, LANES)]
        return jnp.take_along_axis(block, flip, axis=1).T

    for x in range(hops):
        for r in range(0, region, LANES):
            for h in range(0, total.shape[0], LANES):
                own = (2 * x + core) * region + r
                other = (2 * x + 1 - core) * region + r
                keep_ref[x, r:r + LANES, h:h + LANES] = ordered(own, h)
                send_ref[x, r:r + LANES, h:h + LANES] = ordered(other, h).astype(send_ref.dtype)


def correlate(place, numbers, records, templates, hops):
    components, stations, length = records.shape
    window, bank_size = templates.shape[2:]
    margin = up(window, LANES)
    rows = up(stations * components, 8)
    region = length // (2 * hops)
    batch = 2 if stations % 2 == 0 else 1
    depth = up(batch * components * up(window, GROUP), LANES)
    scalars = pl.BlockSpec(memory_space=pltpu.SMEM)
    vectors = pl.BlockSpec(memory_space=pltpu.VMEM)
    return pl.pallas_call(
        functools.partial(correlate_kernel, window=window, batch=batch),
        in_specs=[scalars, scalars, vectors, pl.BlockSpec(memory_space=pl.ANY)],
        out_specs=[vectors] * 2,
        scratch_shapes=[
            pltpu.VMEM((rows, length + margin + LANES + up(MAXMO, LANES)), jnp.float32),
            pltpu.VMEM((rows, length + margin), jnp.float32),
            pltpu.VMEM((rows, length), jnp.float32),
            pltpu.VMEM(templates.shape, templates.dtype),
            pltpu.VMEM((depth, bank_size), jnp.bfloat16),
            pltpu.VMEM((depth, length), jnp.bfloat16),
            pltpu.VMEM((depth, length), jnp.bfloat16),
            pltpu.VMEM((bank_size, depth), jnp.bfloat16),
            pltpu.VMEM((bank_size, depth), jnp.bfloat16),
            pltpu.VMEM((bank_size, length), jnp.float32),
            pltpu.SemaphoreType.DMA((stations // batch,)),
        ],
        out_shape=[
            jax.ShapeDtypeStruct((hops, region, bank_size), kind)
            for kind in (jnp.bfloat16, jnp.float32)
        ],
        compiler_params=pltpu.CompilerParams(vmem_limit_bytes=52 * 2**20),
        name="correlate",
    )(place, numbers, records, templates)


def body(records, templates, moveouts, uptime):
    tm, chan = lax.axis_size("tm"), lax.axis_size("chan")
    hops = tm // 2
    t, z = lax.axis_index("tm"), lax.axis_index("chan")
    x = t // 2
    send, keep = correlate(
        t.reshape(1), jnp.concatenate([moveouts.T, uptime.T]), records.transpose(1, 0, 2), templates, hops
    )
    got = lax.ppermute(send, "tm", [(i, i ^ 1) for i in range(tm)])
    mine = keep + got.astype(jnp.float32)
    result = lax.dynamic_index_in_dim(mine, x, 0, keepdims=False)
    for step in range(1, hops):
        block = lax.dynamic_index_in_dim(mine, (x + step) % hops, 0, keepdims=False)
        perm = [(i, ((i // 2 + step) % hops) * 2 + i % 2) for i in range(tm)]
        result = result + lax.ppermute(block.astype(jnp.bfloat16), "tm", perm).astype(jnp.float32)
    mine = result.reshape(chan, result.shape[0] // chan, result.shape[1])
    result = lax.dynamic_index_in_dim(mine, z, 0, keepdims=False)
    paired = chan & (chan - 1) == 0

    def partner(place, step):
        return place ^ step if paired else (place + step) % chan

    for step in range(1, chan):
        block = lax.dynamic_index_in_dim(mine, partner(z, step), 0, keepdims=False)
        perm = [(i, partner(i, step)) for i in range(chan)]
        result = result + lax.ppermute(block.astype(jnp.bfloat16), "chan", perm).astype(jnp.float32)
    return result.T


def solution(mesh):
    placed = (
        P(("grp", "tm", "chan"), None, None),
        P(("tm", "chan"), None, None, None),
        P(("tm", "chan"), None),
        P(("grp", "tm", "chan"), None),
    )
    return jax.shard_map(
        body, mesh=mesh, in_specs=placed, out_specs=P(None, ("grp", "tm", "chan")), check_vma=False
    )
```

```python
import functools

import jax
import jax.numpy as jnp
from jax import lax
from jax.experimental import pallas as pl
from jax.experimental.pallas import tpu as pltpu
from jax.sharding import PartitionSpec as P

MAXMO = 1000
LANES = 128
GROUP = 16


def up(value, unit):
    return -(-value // unit) * unit


def window_sum(values, window):
    def behind(array, by):
        return array if by == 0 else pltpu.roll(array, by, 1)

    total, offset, size, run = None, 0, 1, values
    while size <= window:
        if window & size:
            piece = behind(run, offset)
            total = piece if total is None else total + piece
            offset += size
        size *= 2
        if size <= window:
            run = run + behind(run, size // 2)
    return total


def correlate_kernel(
    place_ref, numbers_ref, records_ref, templates_ref, send_ref, keep_ref,
    masked, shifted, factor, loaded, bank, windows_a, windows_b, bank_a, bank_b, total, arrived,
    *, window, batch,
):
    components, stations, length = records_ref.shape
    block_count = numbers_ref.shape[0] - components
    rows = masked.shape[0]
    groups = up(window, GROUP) // GROUP
    margin = up(window, LANES)
    block_len = length // block_count
    span = shifted.shape[1]
    lead = masked.shape[1] - length

    def fetch(i):
        at = pl.ds(i * batch, batch)
        return pltpu.make_async_copy(templates_ref.at[at], loaded.at[at], arrived.at[i])

    def start(i, carry):
        fetch(i).start()
        return carry

    batches = stations // batch
    lax.fori_loop(0, batches, start, 0)

    masked[:, :lead] = jnp.zeros((rows, lead), jnp.float32)
    shifted[...] = jnp.zeros(shifted.shape, jnp.float32)
    total[...] = jnp.zeros(total.shape, total.dtype)
    bank[...] = jnp.zeros(bank.shape, bank.dtype)
    depth = batch * components * groups * GROUP
    if windows_a.shape[0] > depth:
        for windows in (windows_a, windows_b):
            rest = (windows.shape[0] - depth, length)
            windows[depth:, :] = jnp.zeros(rest, windows.dtype)
    offsets = lax.broadcasted_iota(jnp.int32, (stations, LANES), 1)
    which = lax.broadcasted_iota(jnp.int32, (stations, LANES), 0)
    mirror = LANES - 1 - lax.broadcasted_iota(jnp.int32, (up(stations, 8), LANES), 1)

    def mask_tile(i, carry):
        at = pl.multiple_of(i * LANES, LANES)
        to = pl.multiple_of(lead + length - LANES - at, LANES)
        block = at // block_len
        limit = jnp.zeros((stations, LANES), jnp.int32)
        for s in range(stations):
            limit = jnp.where(which == s, numbers_ref[components + block, s], limit)
        live = offsets + (at - block * block_len) < limit
        for j in range(components):
            values = records_ref[j, :, pl.ds(at, LANES)].astype(jnp.float32)
            values = jnp.where(live, values, 0.0)
            if stations % 8:
                rest = jnp.zeros((up(stations, 8) - stations, LANES), jnp.float32)
                values = jnp.concatenate([values, rest], axis=0)
            values = jnp.take_along_axis(values, mirror, axis=1)
            masked[j * stations:(j + 1) * stations, pl.ds(to, LANES)] = values[:stations]
        return carry

    lax.fori_loop(0, length // LANES, mask_tile, 0, unroll=length // LANES <= 8)
    burst = stations

    def shift_some(i, carry):
        shifts = []
        for u in range(burst):
            for j in range(components):
                c = j * stations + i * burst + u
                moveout = numbers_ref[j, i * burst + u]
                whole = moveout // LANES * LANES
                base = pl.multiple_of(lead - margin - LANES - whole, LANES)
                row = masked[pl.ds(c, 1), pl.ds(base, span + LANES)]
                shifts.append((c, pltpu.roll(row, moveout - whole, 1)))
        for c, row in shifts:
            shifted[pl.ds(c, 1), :] = row[:, LANES:]
        return carry

    fetch(0).wait()
    shift_some(0, 0)
    chunk = rows

    def energy_some(i, carry):
        at = pl.ds(pl.multiple_of(i * chunk, 8), chunk)
        values = shifted[at, :]
        energy = window_sum(values * values, window)[:, margin:]
        factor[at, :] = lax.rsqrt(jnp.maximum(energy, 1.0))
        return carry

    energy_some(0, 0)
    width = min(2 * LANES, length)

    def multiply(n, windows, turned):
        total[:, n:n + width] += jnp.dot(
            turned[...], windows[:, n:n + width], preferred_element_type=jnp.float32)

    def build(i, windows, turned, pending):
        places = [(u, j) for u in range(batch) for j in range(components)]
        strips, scales = [], []
        for u, j in places:
            c = j * stations + i * batch + u
            half = jnp.broadcast_to(shifted[pl.ds(c, 1), :], (8, span))
            strips.append(jnp.concatenate(
                [pltpu.roll(half, b, 1, stride=1, stride_axis=0) for b in (0, 8)], axis=0
            ).astype(jnp.bfloat16))
            scale = jnp.broadcast_to(factor[pl.ds(c, 1), :], (GROUP, length))
            scales.append(scale.astype(jnp.bfloat16))
        for m, (u, j) in enumerate(places):
            values = loaded[i * batch + u, j].astype(jnp.float32)
            squares = jnp.sum(values * values, axis=0, keepdims=True)
            unit = (values * lax.rsqrt(squares + 1e-06)).astype(jnp.bfloat16)
            bank[m * groups * GROUP:m * groups * GROUP + window, :] = unit
        turned[...] = bank[...].T
        left = list(range(0, length, width)) if pending else []
        share = up(len(left), len(places)) // len(places)
        for m in range(len(places)):
            for a in range(min(groups, LANES // GROUP)):
                rolled = strips[m] if a == 0 else pltpu.roll(strips[m], a * GROUP, 1)
                for g in range(a, groups, LANES // GROUP):
                    begin = margin - (g - a) * GROUP
                    at = (m * groups + g) * GROUP
                    windows[at:at + GROUP, :] = rolled[:, begin:begin + length] * scales[m]
            for n in left[:share]:
                multiply(n, *pending)
            left = left[share:]

    a, b = (windows_a, bank_a), (windows_b, bank_b)
    build(0, *a, None)

    def two_batches(i, carry):
        fetch(2 * i + 1).wait()
        build(2 * i + 1, *b, a)

        @pl.when(2 * i + 2 < batches)
        def _():
            fetch(2 * i + 2).wait()

        build(jnp.minimum(2 * i + 2, batches - 1), *a, b)
        return carry

    if batches > 1:
        lax.fori_loop(0, batches // 2, two_batches, 0)
    if batches % 2:
        for n in range(0, length, width):
            multiply(n, *a)

    core = place_ref[0] % 2
    hops, region = keep_ref.shape[0], keep_ref.shape[1]
    flip = LANES - 1 - lax.broadcasted_iota(jnp.int32, (LANES, LANES), 1)

    def ordered(begin, h):
        at = pl.multiple_of(length - LANES - begin, LANES)
        block = total[h:h + LANES, pl.ds(at, LANES)]
        return jnp.take_along_axis(block, flip, axis=1).T

    for x in range(hops):
        for r in range(0, region, LANES):
            for h in range(0, total.shape[0], LANES):
                own = (2 * x + core) * region + r
                other = (2 * x + 1 - core) * region + r
                keep_ref[x, r:r + LANES, h:h + LANES] = ordered(own, h)
                send_ref[x, r:r + LANES, h:h + LANES] = ordered(other, h).astype(send_ref.dtype)


def correlate(place, numbers, records, templates, hops):
    components, stations, length = records.shape
    window, bank_size = templates.shape[2:]
    margin = up(window, LANES)
    rows = up(stations * components, 8)
    region = length // (2 * hops)
    batch = 2 if stations % 2 == 0 else 1
    depth = up(batch * components * up(window, GROUP), LANES)
    scalars = pl.BlockSpec(memory_space=pltpu.SMEM)
    vectors = pl.BlockSpec(memory_space=pltpu.VMEM)
    return pl.pallas_call(
        functools.partial(correlate_kernel, window=window, batch=batch),
        in_specs=[scalars, scalars, vectors, pl.BlockSpec(memory_space=pl.ANY)],
        out_specs=[vectors] * 2,
        scratch_shapes=[
            pltpu.VMEM((rows, length + margin + LANES + up(MAXMO, LANES)), jnp.float32),
            pltpu.VMEM((rows, length + margin), jnp.float32),
            pltpu.VMEM((rows, length), jnp.float32),
            pltpu.VMEM(templates.shape, templates.dtype),
            pltpu.VMEM((depth, bank_size), jnp.bfloat16),
            pltpu.VMEM((depth, length), jnp.bfloat16),
            pltpu.VMEM((depth, length), jnp.bfloat16),
            pltpu.VMEM((bank_size, depth), jnp.bfloat16),
            pltpu.VMEM((bank_size, depth), jnp.bfloat16),
            pltpu.VMEM((bank_size, length), jnp.float32),
            pltpu.SemaphoreType.DMA((stations // batch,)),
        ],
        out_shape=[
            jax.ShapeDtypeStruct((hops, region, bank_size), kind)
            for kind in (jnp.bfloat16, jnp.float32)
        ],
        compiler_params=pltpu.CompilerParams(vmem_limit_bytes=52 * 2**20),
        name="correlate",
    )(place, numbers, records, templates)


def body(records, templates, moveouts, uptime):
    tm, chan = lax.axis_size("tm"), lax.axis_size("chan")
    hops = tm // 2
    t, z = lax.axis_index("tm"), lax.axis_index("chan")
    x = t // 2
    send, keep = correlate(
        t.reshape(1), jnp.concatenate([moveouts.T, uptime.T]), records.transpose(1, 0, 2), templates, hops
    )
    got = lax.ppermute(send, "tm", [(i, i ^ 1) for i in range(tm)])
    mine = keep + got.astype(jnp.float32)
    result = lax.dynamic_index_in_dim(mine, x, 0, keepdims=False)
    for step in range(1, hops):
        block = lax.dynamic_index_in_dim(mine, (x + step) % hops, 0, keepdims=False)
        perm = [(i, ((i // 2 + step) % hops) * 2 + i % 2) for i in range(tm)]
        result = result + lax.ppermute(block.astype(jnp.bfloat16), "tm", perm).astype(jnp.float32)
    mine = result.reshape(chan, result.shape[0] // chan, result.shape[1])
    result = lax.dynamic_index_in_dim(mine, z, 0, keepdims=False)
    paired = chan & (chan - 1) == 0

    def partner(place, step):
        return place ^ step if paired else (place + step) % chan

    for step in range(1, chan):
        block = lax.dynamic_index_in_dim(mine, partner(z, step), 0, keepdims=False)
        perm = [(i, partner(i, step)) for i in range(chan)]
        result = result + lax.ppermute(block.astype(jnp.bfloat16), "chan", perm).astype(jnp.float32)
    return result.T


def solution(mesh):
    placed = (
        P(("grp", "tm", "chan"), None, None),
        P(("tm", "chan"), None, None, None),
        P(("tm", "chan"), None),
        P(("grp", "tm", "chan"), None),
    )
    return jax.shard_map(
        body, mesh=mesh, in_specs=placed, out_specs=P(None, ("grp", "tm", "chan")), check_vma=False
    )
```

```python
import functools

import jax
import jax.numpy as jnp
from jax import lax
from jax.experimental import pallas as pl
from jax.experimental.pallas import tpu as pltpu
from jax.sharding import PartitionSpec as P

MAXMO = 1000
LANES = 128
GROUP = 16


def up(value, unit):
    return -(-value // unit) * unit


def window_sum(values, window):
    def behind(array, by):
        return array if by == 0 else pltpu.roll(array, by, 1)

    total, offset, size, run = None, 0, 1, values
    while size <= window:
        if window & size:
            piece = behind(run, offset)
            total = piece if total is None else total + piece
            offset += size
        size *= 2
        if size <= window:
            run = run + behind(run, size // 2)
    return total


def correlate_kernel(
    place_ref, numbers_ref, records_ref, templates_ref, send_ref, keep_ref,
    masked, shifted, factor, loaded, bank, windows_a, windows_b, bank_a, bank_b, total, arrived,
    *, window, batch,
):
    components, stations, length = records_ref.shape
    block_count = numbers_ref.shape[0] - components
    rows = masked.shape[0]
    groups = up(window, GROUP) // GROUP
    margin = up(window, LANES)
    block_len = length // block_count
    span = shifted.shape[1]
    lead = masked.shape[1] - length

    def fetch(i):
        at = pl.ds(i * batch, batch)
        return pltpu.make_async_copy(templates_ref.at[at], loaded.at[at], arrived.at[i])

    def start(i, carry):
        fetch(i).start()
        return carry

    batches = stations // batch
    fetch(0).start()

    masked[:, :lead] = jnp.zeros((rows, lead), jnp.float32)
    shifted[...] = jnp.zeros(shifted.shape, jnp.float32)
    total[...] = jnp.zeros(total.shape, total.dtype)
    bank[...] = jnp.zeros(bank.shape, bank.dtype)
    depth = batch * components * groups * GROUP
    if windows_a.shape[0] > depth:
        for windows in (windows_a, windows_b):
            rest = (windows.shape[0] - depth, length)
            windows[depth:, :] = jnp.zeros(rest, windows.dtype)
    offsets = lax.broadcasted_iota(jnp.int32, (stations, LANES), 1)
    which = lax.broadcasted_iota(jnp.int32, (stations, LANES), 0)
    mirror = LANES - 1 - lax.broadcasted_iota(jnp.int32, (up(stations, 8), LANES), 1)

    def mask_tile(i, carry):
        at = pl.multiple_of(i * LANES, LANES)
        to = pl.multiple_of(lead + length - LANES - at, LANES)
        block = at // block_len
        limit = jnp.zeros((stations, LANES), jnp.int32)
        for s in range(stations):
            limit = jnp.where(which == s, numbers_ref[components + block, s], limit)
        live = offsets + (at - block * block_len) < limit
        for j in range(components):
            values = records_ref[j, :, pl.ds(at, LANES)].astype(jnp.float32)
            values = jnp.where(live, values, 0.0)
            if stations % 8:
                rest = jnp.zeros((up(stations, 8) - stations, LANES), jnp.float32)
                values = jnp.concatenate([values, rest], axis=0)
            values = jnp.take_along_axis(values, mirror, axis=1)
            masked[j * stations:(j + 1) * stations, pl.ds(to, LANES)] = values[:stations]
        return carry

    lax.fori_loop(0, length // LANES, mask_tile, 0, unroll=length // LANES <= 8)
    burst = stations

    def shift_some(i, carry):
        shifts = []
        for u in range(burst):
            for j in range(components):
                c = j * stations + i * burst + u
                moveout = numbers_ref[j, i * burst + u]
                whole = moveout // LANES * LANES
                base = pl.multiple_of(lead - margin - LANES - whole, LANES)
                row = masked[pl.ds(c, 1), pl.ds(base, span + LANES)]
                shifts.append((c, pltpu.roll(row, moveout - whole, 1)))
        for c, row in shifts:
            shifted[pl.ds(c, 1), :] = row[:, LANES:]
        return carry

    lax.fori_loop(0, stations // burst, shift_some, 0)
    lax.fori_loop(1, batches, start, 0)
    chunk = rows

    def energy_some(i, carry):
        at = pl.ds(pl.multiple_of(i * chunk, 8), chunk)
        values = shifted[at, :]
        energy = window_sum(values * values, window)[:, margin:]
        factor[at, :] = lax.rsqrt(jnp.maximum(energy, 1.0))
        return carry

    lax.fori_loop(0, rows // chunk, energy_some, 0)
    width = min(2 * LANES, length)

    def multiply(n, windows, turned):
        total[:, n:n + width] += jnp.dot(
            turned[...], windows[:, n:n + width], preferred_element_type=jnp.float32)

    def build(i, windows, turned, pending):
        places = [(u, j) for u in range(batch) for j in range(components)]
        strips, scales = [], []
        for u, j in places:
            c = j * stations + i * batch + u
            half = jnp.broadcast_to(shifted[pl.ds(c, 1), :], (8, span))
            strips.append(jnp.concatenate(
                [pltpu.roll(half, b, 1, stride=1, stride_axis=0) for b in (0, 8)], axis=0
            ).astype(jnp.bfloat16))
            scale = jnp.broadcast_to(factor[pl.ds(c, 1), :], (GROUP, length))
            scales.append(scale.astype(jnp.bfloat16))
        for m, (u, j) in enumerate(places):
            values = loaded[i * batch + u, j].astype(jnp.float32)
            squares = jnp.sum(values * values, axis=0, keepdims=True)
            unit = (values * lax.rsqrt(squares + 1e-06)).astype(jnp.bfloat16)
            bank[m * groups * GROUP:m * groups * GROUP + window, :] = unit
        turned[...] = bank[...].T
        left = list(range(0, length, width)) if pending else []
        share = up(len(left), len(places)) // len(places)
        for m in range(len(places)):
            for a in range(min(groups, LANES // GROUP)):
                rolled = strips[m] if a == 0 else pltpu.roll(strips[m], a * GROUP, 1)
                for g in range(a, groups, LANES // GROUP):
                    begin = margin - (g - a) * GROUP
                    at = (m * groups + g) * GROUP
                    windows[at:at + GROUP, :] = rolled[:, begin:begin + length] * scales[m]
            for n in left[:share]:
                multiply(n, *pending)
            left = left[share:]

    a, b = (windows_a, bank_a), (windows_b, bank_b)
    fetch(0).wait()
    build(0, *a, None)

    def two_batches(i, carry):
        fetch(2 * i + 1).wait()
        build(2 * i + 1, *b, a)

        @pl.when(2 * i + 2 < batches)
        def _():
            fetch(2 * i + 2).wait()

        build(jnp.minimum(2 * i + 2, batches - 1), *a, b)
        return carry

    if batches > 1:
        lax.fori_loop(0, batches // 2, two_batches, 0)
    if batches % 2:
        for n in range(0, length, width):
            multiply(n, *a)

    core = place_ref[0] % 2
    hops, region = keep_ref.shape[0], keep_ref.shape[1]
    flip = LANES - 1 - lax.broadcasted_iota(jnp.int32, (LANES, LANES), 1)

    def ordered(begin, h):
        at = pl.multiple_of(length - LANES - begin, LANES)
        block = total[h:h + LANES, pl.ds(at, LANES)]
        return jnp.take_along_axis(block, flip, axis=1).T

    for x in range(hops):
        for r in range(0, region, LANES):
            for h in range(0, total.shape[0], LANES):
                own = (2 * x + core) * region + r
                other = (2 * x + 1 - core) * region + r
                keep_ref[x, r:r + LANES, h:h + LANES] = ordered(own, h)
                send_ref[x, r:r + LANES, h:h + LANES] = ordered(other, h).astype(send_ref.dtype)


def correlate(place, numbers, records, templates, hops):
    components, stations, length = records.shape
    window, bank_size = templates.shape[2:]
    margin = up(window, LANES)
    rows = up(stations * components, 8)
    region = length // (2 * hops)
    batch = 2 if stations % 2 == 0 else 1
    depth = up(batch * components * up(window, GROUP), LANES)
    scalars = pl.BlockSpec(memory_space=pltpu.SMEM)
    vectors = pl.BlockSpec(memory_space=pltpu.VMEM)
    return pl.pallas_call(
        functools.partial(correlate_kernel, window=window, batch=batch),
        in_specs=[scalars, scalars, vectors, pl.BlockSpec(memory_space=pl.ANY)],
        out_specs=[vectors] * 2,
        scratch_shapes=[
            pltpu.VMEM((rows, length + margin + LANES + up(MAXMO, LANES)), jnp.float32),
            pltpu.VMEM((rows, length + margin), jnp.float32),
            pltpu.VMEM((rows, length), jnp.float32),
            pltpu.VMEM(templates.shape, templates.dtype),
            pltpu.VMEM((depth, bank_size), jnp.bfloat16),
            pltpu.VMEM((depth, length), jnp.bfloat16),
            pltpu.VMEM((depth, length), jnp.bfloat16),
            pltpu.VMEM((bank_size, depth), jnp.bfloat16),
            pltpu.VMEM((bank_size, depth), jnp.bfloat16),
            pltpu.VMEM((bank_size, length), jnp.float32),
            pltpu.SemaphoreType.DMA((stations // batch,)),
        ],
        out_shape=[
            jax.ShapeDtypeStruct((hops, region, bank_size), kind)
            for kind in (jnp.bfloat16, jnp.float32)
        ],
        compiler_params=pltpu.CompilerParams(vmem_limit_bytes=52 * 2**20),
        name="correlate",
    )(place, numbers, records, templates)


def body(records, templates, moveouts, uptime):
    tm, chan = lax.axis_size("tm"), lax.axis_size("chan")
    hops = tm // 2
    t, z = lax.axis_index("tm"), lax.axis_index("chan")
    x = t // 2
    send, keep = correlate(
        t.reshape(1), jnp.concatenate([moveouts.T, uptime.T]), records.transpose(1, 0, 2), templates, hops
    )
    got = lax.ppermute(send, "tm", [(i, i ^ 1) for i in range(tm)])
    mine = keep + got.astype(jnp.float32)
    result = lax.dynamic_index_in_dim(mine, x, 0, keepdims=False)
    for step in range(1, hops):
        block = lax.dynamic_index_in_dim(mine, (x + step) % hops, 0, keepdims=False)
        perm = [(i, ((i // 2 + step) % hops) * 2 + i % 2) for i in range(tm)]
        result = result + lax.ppermute(block.astype(jnp.bfloat16), "tm", perm).astype(jnp.float32)
    mine = result.reshape(chan, result.shape[0] // chan, result.shape[1])
    result = lax.dynamic_index_in_dim(mine, z, 0, keepdims=False)
    paired = chan & (chan - 1) == 0

    def partner(place, step):
        return place ^ step if paired else (place + step) % chan

    for step in range(1, chan):
        block = lax.dynamic_index_in_dim(mine, partner(z, step), 0, keepdims=False)
        perm = [(i, partner(i, step)) for i in range(chan)]
        result = result + lax.ppermute(block.astype(jnp.bfloat16), "chan", perm).astype(jnp.float32)
    return result.T


def solution(mesh):
    placed = (
        P(("grp", "tm", "chan"), None, None),
        P(("tm", "chan"), None, None, None),
        P(("tm", "chan"), None),
        P(("grp", "tm", "chan"), None),
    )
    return jax.shard_map(
        body, mesh=mesh, in_specs=placed, out_specs=P(None, ("grp", "tm", "chan")), check_vma=False
    )
```

```python
import functools

import jax
import jax.numpy as jnp
from jax import lax
from jax.experimental import pallas as pl
from jax.experimental.pallas import tpu as pltpu
from jax.sharding import PartitionSpec as P

MAXMO = 1000
LANES = 128
GROUP = 16


def up(value, unit):
    return -(-value // unit) * unit


def window_sum(values, window):
    def behind(array, by):
        return array if by == 0 else pltpu.roll(array, by, 1)

    total, offset, size, run = None, 0, 1, values
    while size <= window:
        if window & size:
            piece = behind(run, offset)
            total = piece if total is None else total + piece
            offset += size
        size *= 2
        if size <= window:
            run = run + behind(run, size // 2)
    return total


def correlate_kernel(
    place_ref, numbers_ref, records_ref, templates_ref, send_ref, keep_ref,
    masked, shifted, factor, loaded, bank, windows_a, windows_b, bank_a, bank_b, total, arrived,
    *, window, batch,
):
    components, stations, length = records_ref.shape
    block_count = numbers_ref.shape[0] - components
    rows = masked.shape[0]
    groups = up(window, GROUP) // GROUP
    margin = up(window, LANES)
    block_len = length // block_count
    span = shifted.shape[1]
    lead = masked.shape[1] - length

    def fetch(i):
        at = pl.ds(i * batch, batch)
        return pltpu.make_async_copy(templates_ref.at[at], loaded.at[at], arrived.at[i])

    def start(i, carry):
        fetch(i).start()
        return carry

    batches = stations // batch
    fetch(0).start()

    masked[:, :lead] = jnp.zeros((rows, lead), jnp.float32)
    shifted[...] = jnp.zeros(shifted.shape, jnp.float32)
    total[...] = jnp.zeros(total.shape, total.dtype)
    bank[...] = jnp.zeros(bank.shape, bank.dtype)
    depth = batch * components * groups * GROUP
    if windows_a.shape[0] > depth:
        for windows in (windows_a, windows_b):
            rest = (windows.shape[0] - depth, length)
            windows[depth:, :] = jnp.zeros(rest, windows.dtype)
    offsets = lax.broadcasted_iota(jnp.int32, (stations, LANES), 1)
    which = lax.broadcasted_iota(jnp.int32, (stations, LANES), 0)
    mirror = LANES - 1 - lax.broadcasted_iota(jnp.int32, (up(stations, 8), LANES), 1)

    def mask_tile(i, carry):
        at = pl.multiple_of(i * LANES, LANES)
        to = pl.multiple_of(lead + length - LANES - at, LANES)
        block = at // block_len
        limit = jnp.zeros((stations, LANES), jnp.int32)
        for s in range(stations):
            limit = jnp.where(which == s, numbers_ref[components + block, s], limit)
        live = offsets + (at - block * block_len) < limit
        for j in range(components):
            values = records_ref[j, :, pl.ds(at, LANES)].astype(jnp.float32)
            values = jnp.where(live, values, 0.0)
            if stations % 8:
                rest = jnp.zeros((up(stations, 8) - stations, LANES), jnp.float32)
                values = jnp.concatenate([values, rest], axis=0)
            values = jnp.take_along_axis(values, mirror, axis=1)
            masked[j * stations:(j + 1) * stations, pl.ds(to, LANES)] = values[:stations]
        return carry

    lax.fori_loop(0, length // LANES, mask_tile, 0, unroll=length // LANES <= 8)
    burst = stations

    def shift_some(i, carry):
        shifts = []
        for u in range(burst):
            for j in range(components):
                c = j * stations + i * burst + u
                moveout = numbers_ref[j, i * burst + u]
                whole = moveout // LANES * LANES
                base = pl.multiple_of(lead - margin - LANES - whole, LANES)
                row = masked[pl.ds(c, 1), pl.ds(base, span + LANES)]
                shifts.append((c, pltpu.roll(row, moveout - whole, 1)))
        for c, row in shifts:
            shifted[pl.ds(c, 1), :] = row[:, LANES:]
        return carry

    lax.fori_loop(0, stations // burst, shift_some, 0)
    lax.fori_loop(1, batches, start, 0)
    chunk = rows

    def energy_some(i, carry):
        at = pl.ds(pl.multiple_of(i * chunk, 8), chunk)
        values = shifted[at, :]
        energy = window_sum(values * values, window)[:, margin:]
        factor[at, :] = lax.rsqrt(jnp.maximum(energy, 1.0))
        return carry

    lax.fori_loop(0, rows // chunk, energy_some, 0)
    width = min(4 * LANES, length)

    def multiply(n, windows, turned):
        total[:, n:n + width] += jnp.dot(
            turned[...], windows[:, n:n + width], preferred_element_type=jnp.float32)

    def build(i, windows, turned, pending):
        places = [(u, j) for u in range(batch) for j in range(components)]
        strips, scales = [], []
        for u, j in places:
            c = j * stations + i * batch + u
            half = jnp.broadcast_to(shifted[pl.ds(c, 1), :], (8, span))
            strips.append(jnp.concatenate(
                [pltpu.roll(half, b, 1, stride=1, stride_axis=0) for b in (0, 8)], axis=0
            ).astype(jnp.bfloat16))
            scale = jnp.broadcast_to(factor[pl.ds(c, 1), :], (GROUP, length))
            scales.append(scale.astype(jnp.bfloat16))
        for m, (u, j) in enumerate(places):
            values = loaded[i * batch + u, j].astype(jnp.float32)
            squares = jnp.sum(values * values, axis=0, keepdims=True)
            unit = (values * lax.rsqrt(squares + 1e-06)).astype(jnp.bfloat16)
            bank[m * groups * GROUP:m * groups * GROUP + window, :] = unit
        turned[...] = bank[...].T
        left = list(range(0, length, width)) if pending else []
        share = up(len(left), len(places)) // len(places)
        for m in range(len(places)):
            for a in range(min(groups, LANES // GROUP)):
                rolled = strips[m] if a == 0 else pltpu.roll(strips[m], a * GROUP, 1)
                for g in range(a, groups, LANES // GROUP):
                    begin = margin - (g - a) * GROUP
                    at = (m * groups + g) * GROUP
                    windows[at:at + GROUP, :] = rolled[:, begin:begin + length] * scales[m]
            for n in left[:share]:
                multiply(n, *pending)
            left = left[share:]

    a, b = (windows_a, bank_a), (windows_b, bank_b)
    fetch(0).wait()
    build(0, *a, None)

    def two_batches(i, carry):
        fetch(2 * i + 1).wait()
        build(2 * i + 1, *b, a)

        @pl.when(2 * i + 2 < batches)
        def _():
            fetch(2 * i + 2).wait()

        build(jnp.minimum(2 * i + 2, batches - 1), *a, b)
        return carry

    if batches > 1:
        lax.fori_loop(0, batches // 2, two_batches, 0)
    if batches % 2:
        for n in range(0, length, width):
            multiply(n, *a)

    core = place_ref[0] % 2
    hops, region = keep_ref.shape[0], keep_ref.shape[1]
    flip = LANES - 1 - lax.broadcasted_iota(jnp.int32, (LANES, LANES), 1)

    def ordered(begin, h):
        at = pl.multiple_of(length - LANES - begin, LANES)
        block = total[h:h + LANES, pl.ds(at, LANES)]
        return jnp.take_along_axis(block, flip, axis=1).T

    for x in range(hops):
        for r in range(0, region, LANES):
            for h in range(0, total.shape[0], LANES):
                own = (2 * x + core) * region + r
                other = (2 * x + 1 - core) * region + r
                keep_ref[x, r:r + LANES, h:h + LANES] = ordered(own, h)
                send_ref[x, r:r + LANES, h:h + LANES] = ordered(other, h).astype(send_ref.dtype)


def correlate(place, numbers, records, templates, hops):
    components, stations, length = records.shape
    window, bank_size = templates.shape[2:]
    margin = up(window, LANES)
    rows = up(stations * components, 8)
    region = length // (2 * hops)
    batch = 2 if stations % 2 == 0 else 1
    depth = up(batch * components * up(window, GROUP), LANES)
    scalars = pl.BlockSpec(memory_space=pltpu.SMEM)
    vectors = pl.BlockSpec(memory_space=pltpu.VMEM)
    return pl.pallas_call(
        functools.partial(correlate_kernel, window=window, batch=batch),
        in_specs=[scalars, scalars, vectors, pl.BlockSpec(memory_space=pl.ANY)],
        out_specs=[vectors] * 2,
        scratch_shapes=[
            pltpu.VMEM((rows, length + margin + LANES + up(MAXMO, LANES)), jnp.float32),
            pltpu.VMEM((rows, length + margin), jnp.float32),
            pltpu.VMEM((rows, length), jnp.float32),
            pltpu.VMEM(templates.shape, templates.dtype),
            pltpu.VMEM((depth, bank_size), jnp.bfloat16),
            pltpu.VMEM((depth, length), jnp.bfloat16),
            pltpu.VMEM((depth, length), jnp.bfloat16),
            pltpu.VMEM((bank_size, depth), jnp.bfloat16),
            pltpu.VMEM((bank_size, depth), jnp.bfloat16),
            pltpu.VMEM((bank_size, length), jnp.float32),
            pltpu.SemaphoreType.DMA((stations // batch,)),
        ],
        out_shape=[
            jax.ShapeDtypeStruct((hops, region, bank_size), kind)
            for kind in (jnp.bfloat16, jnp.float32)
        ],
        compiler_params=pltpu.CompilerParams(vmem_limit_bytes=52 * 2**20),
        name="correlate",
    )(place, numbers, records, templates)


def body(records, templates, moveouts, uptime):
    tm, chan = lax.axis_size("tm"), lax.axis_size("chan")
    hops = tm // 2
    t, z = lax.axis_index("tm"), lax.axis_index("chan")
    x = t // 2
    send, keep = correlate(
        t.reshape(1), jnp.concatenate([moveouts.T, uptime.T]), records.transpose(1, 0, 2), templates, hops
    )
    got = lax.ppermute(send, "tm", [(i, i ^ 1) for i in range(tm)])
    mine = keep + got.astype(jnp.float32)
    result = lax.dynamic_index_in_dim(mine, x, 0, keepdims=False)
    for step in range(1, hops):
        block = lax.dynamic_index_in_dim(mine, (x + step) % hops, 0, keepdims=False)
        perm = [(i, ((i // 2 + step) % hops) * 2 + i % 2) for i in range(tm)]
        result = result + lax.ppermute(block.astype(jnp.bfloat16), "tm", perm).astype(jnp.float32)
    mine = result.reshape(chan, result.shape[0] // chan, result.shape[1])
    result = lax.dynamic_index_in_dim(mine, z, 0, keepdims=False)
    paired = chan & (chan - 1) == 0

    def partner(place, step):
        return place ^ step if paired else (place + step) % chan

    for step in range(1, chan):
        block = lax.dynamic_index_in_dim(mine, partner(z, step), 0, keepdims=False)
        perm = [(i, partner(i, step)) for i in range(chan)]
        result = result + lax.ppermute(block.astype(jnp.bfloat16), "chan", perm).astype(jnp.float32)
    return result.T


def solution(mesh):
    placed = (
        P(("grp", "tm", "chan"), None, None),
        P(("tm", "chan"), None, None, None),
        P(("tm", "chan"), None),
        P(("grp", "tm", "chan"), None),
    )
    return jax.shard_map(
        body, mesh=mesh, in_specs=placed, out_specs=P(None, ("grp", "tm", "chan")), check_vma=False
    )
```

```python
import functools

import jax
import jax.numpy as jnp
from jax import lax
from jax.experimental import pallas as pl
from jax.experimental.pallas import tpu as pltpu
from jax.sharding import PartitionSpec as P

MAXMO = 1000
LANES = 128
GROUP = 16


def up(value, unit):
    return -(-value // unit) * unit


def window_sum(values, window):
    def behind(array, by):
        return array if by == 0 else pltpu.roll(array, by, 1)

    total, offset, size, run = None, 0, 1, values
    while size <= window:
        if window & size:
            piece = behind(run, offset)
            total = piece if total is None else total + piece
            offset += size
        size *= 2
        if size <= window:
            run = run + behind(run, size // 2)
    return total


def correlate_kernel(
    place_ref, numbers_ref, records_ref, templates_ref, send_ref, keep_ref,
    masked, shifted, factor, loaded, bank, windows_a, windows_b, bank_a, bank_b, total, arrived,
    *, window, batch,
):
    components, stations, length = records_ref.shape
    block_count = numbers_ref.shape[0] - components
    rows = masked.shape[0]
    groups = up(window, GROUP) // GROUP
    margin = up(window, LANES)
    block_len = length // block_count
    span = shifted.shape[1]
    lead = masked.shape[1] - length

    def fetch(i):
        at = pl.ds(i * batch, batch)
        return pltpu.make_async_copy(templates_ref.at[at], loaded.at[at], arrived.at[i])

    def start(i, carry):
        fetch(i).start()
        return carry

    batches = stations // batch
    fetch(0).start()

    masked[:, :lead] = jnp.zeros((rows, lead), jnp.float32)
    shifted[...] = jnp.zeros(shifted.shape, jnp.float32)
    total[...] = jnp.zeros(total.shape, total.dtype)
    bank[...] = jnp.zeros(bank.shape, bank.dtype)
    depth = batch * components * groups * GROUP
    if windows_a.shape[0] > depth:
        for windows in (windows_a, windows_b):
            rest = (windows.shape[0] - depth, length)
            windows[depth:, :] = jnp.zeros(rest, windows.dtype)
    offsets = lax.broadcasted_iota(jnp.int32, (stations, LANES), 1)
    which = lax.broadcasted_iota(jnp.int32, (stations, LANES), 0)
    mirror = LANES - 1 - lax.broadcasted_iota(jnp.int32, (up(stations, 8), LANES), 1)

    def mask_tile(i, carry):
        at = pl.multiple_of(i * LANES, LANES)
        to = pl.multiple_of(lead + length - LANES - at, LANES)
        block = at // block_len
        limit = jnp.zeros((stations, LANES), jnp.int32)
        for s in range(stations):
            limit = jnp.where(which == s, numbers_ref[components + block, s], limit)
        live = offsets + (at - block * block_len) < limit
        for j in range(components):
            values = records_ref[j, :, pl.ds(at, LANES)].astype(jnp.float32)
            values = jnp.where(live, values, 0.0)
            if stations % 8:
                rest = jnp.zeros((up(stations, 8) - stations, LANES), jnp.float32)
                values = jnp.concatenate([values, rest], axis=0)
            values = jnp.take_along_axis(values, mirror, axis=1)
            masked[j * stations:(j + 1) * stations, pl.ds(to, LANES)] = values[:stations]
        return carry

    lax.fori_loop(0, length // LANES, mask_tile, 0, unroll=length // LANES <= 8)
    burst = stations

    def shift_some(i, carry):
        shifts = []
        for u in range(burst):
            for j in range(components):
                c = j * stations + i * burst + u
                moveout = numbers_ref[j, i * burst + u]
                whole = moveout // LANES * LANES
                base = pl.multiple_of(lead - margin - LANES - whole, LANES)
                row = masked[pl.ds(c, 1), pl.ds(base, span + LANES)]
                shifts.append((c, pltpu.roll(row, moveout - whole, 1)))
        for c, row in shifts:
            shifted[pl.ds(c, 1), :] = row[:, LANES:]
        return carry

    lax.fori_loop(0, stations // burst, shift_some, 0)
    lax.fori_loop(1, batches, start, 0)
    for g in range(0, rows, 8):
        values = shifted[g:g + 8, :]
        energy = window_sum(values * values, window)[:, margin:]
        factor[g:g + 8, :] = lax.rsqrt(jnp.maximum(energy, 1.0))
    width = min(2 * LANES, length)

    def multiply(n, windows, turned):
        total[:, n:n + width] += jnp.dot(
            turned[...], windows[:, n:n + width], preferred_element_type=jnp.float32)

    def build(i, windows, turned, pending):
        places = [(u, j) for u in range(batch) for j in range(components)]
        strips, scales = [], []
        for u, j in places:
            c = j * stations + i * batch + u
            half = jnp.broadcast_to(shifted[pl.ds(c, 1), :], (8, span))
            strips.append(jnp.concatenate(
                [pltpu.roll(half, b, 1, stride=1, stride_axis=0) for b in (0, 8)], axis=0
            ).astype(jnp.bfloat16))
            scale = jnp.broadcast_to(factor[pl.ds(c, 1), :], (GROUP, length))
            scales.append(scale.astype(jnp.bfloat16))
        for m, (u, j) in enumerate(places):
            values = loaded[i * batch + u, j].astype(jnp.float32)
            squares = jnp.sum(values * values, axis=0, keepdims=True)
            unit = (values * lax.rsqrt(squares + 1e-06)).astype(jnp.bfloat16)
            bank[m * groups * GROUP:m * groups * GROUP + window, :] = unit
        turned[...] = bank[...].T
        left = list(range(0, length, width)) if pending else []
        share = up(len(left), len(places)) // len(places)
        for m in range(len(places)):
            for a in range(min(groups, LANES // GROUP)):
                rolled = strips[m] if a == 0 else pltpu.roll(strips[m], a * GROUP, 1)
                for g in range(a, groups, LANES // GROUP):
                    begin = margin - (g - a) * GROUP
                    at = (m * groups + g) * GROUP
                    windows[at:at + GROUP, :] = rolled[:, begin:begin + length] * scales[m]
            for n in left[:share]:
                multiply(n, *pending)
            left = left[share:]

    a, b = (windows_a, bank_a), (windows_b, bank_b)
    fetch(0).wait()
    build(0, *a, None)

    def two_batches(i, carry):
        fetch(2 * i + 1).wait()
        build(2 * i + 1, *b, a)

        @pl.when(2 * i + 2 < batches)
        def _():
            fetch(2 * i + 2).wait()

        build(jnp.minimum(2 * i + 2, batches - 1), *a, b)
        return carry

    if batches > 1:
        lax.fori_loop(0, batches // 2, two_batches, 0)
    if batches % 2:
        for n in range(0, length, width):
            multiply(n, *a)

    core = place_ref[0] % 2
    hops, region = keep_ref.shape[0], keep_ref.shape[1]
    flip = LANES - 1 - lax.broadcasted_iota(jnp.int32, (LANES, LANES), 1)

    def ordered(begin, h):
        at = pl.multiple_of(length - LANES - begin, LANES)
        block = total[h:h + LANES, pl.ds(at, LANES)]
        return jnp.take_along_axis(block, flip, axis=1).T

    for x in range(hops):
        for r in range(0, region, LANES):
            for h in range(0, total.shape[0], LANES):
                own = (2 * x + core) * region + r
                other = (2 * x + 1 - core) * region + r
                keep_ref[x, r:r + LANES, h:h + LANES] = ordered(own, h)
                send_ref[x, r:r + LANES, h:h + LANES] = ordered(other, h).astype(send_ref.dtype)


def correlate(place, numbers, records, templates, hops):
    components, stations, length = records.shape
    window, bank_size = templates.shape[2:]
    margin = up(window, LANES)
    rows = up(stations * components, 8)
    region = length // (2 * hops)
    batch = 2 if stations % 2 == 0 else 1
    depth = up(batch * components * up(window, GROUP), LANES)
    scalars = pl.BlockSpec(memory_space=pltpu.SMEM)
    vectors = pl.BlockSpec(memory_space=pltpu.VMEM)
    return pl.pallas_call(
        functools.partial(correlate_kernel, window=window, batch=batch),
        in_specs=[scalars, scalars, vectors, pl.BlockSpec(memory_space=pl.ANY)],
        out_specs=[vectors] * 2,
        scratch_shapes=[
            pltpu.VMEM((rows, length + margin + LANES + up(MAXMO, LANES)), jnp.float32),
            pltpu.VMEM((rows, length + margin), jnp.float32),
            pltpu.VMEM((rows, length), jnp.float32),
            pltpu.VMEM(templates.shape, templates.dtype),
            pltpu.VMEM((depth, bank_size), jnp.bfloat16),
            pltpu.VMEM((depth, length), jnp.bfloat16),
            pltpu.VMEM((depth, length), jnp.bfloat16),
            pltpu.VMEM((bank_size, depth), jnp.bfloat16),
            pltpu.VMEM((bank_size, depth), jnp.bfloat16),
            pltpu.VMEM((bank_size, length), jnp.float32),
            pltpu.SemaphoreType.DMA((stations // batch,)),
        ],
        out_shape=[
            jax.ShapeDtypeStruct((hops, region, bank_size), kind)
            for kind in (jnp.bfloat16, jnp.float32)
        ],
        compiler_params=pltpu.CompilerParams(vmem_limit_bytes=52 * 2**20),
        name="correlate",
    )(place, numbers, records, templates)


def body(records, templates, moveouts, uptime):
    tm, chan = lax.axis_size("tm"), lax.axis_size("chan")
    hops = tm // 2
    t, z = lax.axis_index("tm"), lax.axis_index("chan")
    x = t // 2
    send, keep = correlate(
        t.reshape(1), jnp.concatenate([moveouts.T, uptime.T]), records.transpose(1, 0, 2), templates, hops
    )
    got = lax.ppermute(send, "tm", [(i, i ^ 1) for i in range(tm)])
    mine = keep + got.astype(jnp.float32)
    result = lax.dynamic_index_in_dim(mine, x, 0, keepdims=False)
    for step in range(1, hops):
        block = lax.dynamic_index_in_dim(mine, (x + step) % hops, 0, keepdims=False)
        perm = [(i, ((i // 2 + step) % hops) * 2 + i % 2) for i in range(tm)]
        result = result + lax.ppermute(block.astype(jnp.bfloat16), "tm", perm).astype(jnp.float32)
    mine = result.reshape(chan, result.shape[0] // chan, result.shape[1])
    result = lax.dynamic_index_in_dim(mine, z, 0, keepdims=False)
    paired = chan & (chan - 1) == 0

    def partner(place, step):
        return place ^ step if paired else (place + step) % chan

    for step in range(1, chan):
        block = lax.dynamic_index_in_dim(mine, partner(z, step), 0, keepdims=False)
        perm = [(i, partner(i, step)) for i in range(chan)]
        result = result + lax.ppermute(block.astype(jnp.bfloat16), "chan", perm).astype(jnp.float32)
    return result.T


def solution(mesh):
    placed = (
        P(("grp", "tm", "chan"), None, None),
        P(("tm", "chan"), None, None, None),
        P(("tm", "chan"), None),
        P(("grp", "tm", "chan"), None),
    )
    return jax.shard_map(
        body, mesh=mesh, in_specs=placed, out_specs=P(None, ("grp", "tm", "chan")), check_vma=False
    )
```
